32 devices in a mesh: pair: 2 (over core), edge: 16 (over z, y, x).
Axes of the slice: x: 2, y: 2, z: 4, core: 2. Of those that a mesh axis runs over, the one named last changes fastest.
Arguments:
- edge_embed: float32 [32768, 512], P('edge', 'pair'), may hold values from -6 to 6
- atom_embed: float32 [1024, 256], P('edge', 'pair'), may hold values from -6 to 6
- edge_rbf: float32 [32768, 128], P('edge'), may hold values from 0 to 1
- edge_src: int32 [32768], P('edge'), may hold values from 0 to 191
- edge_dst: int32 [32768], P('edge'), may hold values from 0 to 63
- halo_send: int32 [2048], P('edge'), may hold values from 0 to 63
- trip_index: int32 [32768, 16], P('edge'), may hold values from 0 to 2047
- trip_cos: float32 [32768, 16], P('edge'), may hold values from -1 to 1
- trip_live: int32 [32768, 16], P('edge'), may hold values 0 or 1
- quad_index: int32 [8192, 8], P('edge'), may hold values from 0 to 2047
- quad_cos: float32 [8192, 8], P('edge'), may hold values from -1 to 1
- quad_dih: float32 [8192, 8], P('edge'), may hold values from -1 to 1
- quad_live: int32 [8192, 8], P('edge'), may hold values 0 or 1
- quad_target: int32 [8192], P('edge'), may hold values from 0 to 2047
- w_quad_rbf: float32 [128, 512], replicated, may hold values from -0.5 to 0.5
- w_quad_down: float32 [512, 32], replicated, may hold values from -0.25 to 0.25
- w_quad_bil: float32 [1024, 32], replicated, may hold values from -0.375 to 0.375
- w_quad_up: float32 [32, 512], replicated, may hold values from -1 to 1
- w_trip_rbf: float32 [128, 512], replicated, may hold values from -0.5 to 0.5
- w_trip_down: float32 [512, 64], replicated, may hold values from -0.25 to 0.25
- triplet_bilinear_weight: float32 [1024, 64], replicated, may hold values from -0.375 to 0.375
- w_trip_up: float32 [64, 512], replicated, may hold values from -0.75 to 0.75
- w_res_one: float32 [512, 512], replicated, may hold values from -0.25 to 0.25
- w_res_two: float32 [512, 512], replicated, may hold values from -0.5 to 0.5
- w_atom_edge: float32 [1024, 512], replicated, may hold values from -0.1875 to 0.1875
- w_edge_rbf: float32 [128, 512], replicated, may hold values from -0.5 to 0.5
- w_edge_atom: float32 [512, 256], replicated, may hold values from -0.5 to 0.5
- w_out: float32 [256, 256], replicated, may hold values from -0.375 to 0.375
- cot_edge: float32 [32768, 512], P('edge', 'pair'), may hold values from -6 to 6
- cot_atom: float32 [1024, 256], P('edge', 'pair'), may hold values from -6 to 6
- cot_feat: float32 [1024, 256], P('edge', 'pair'), may hold values from -6 to 6
Outputs:
- edge_out: float32 [32768, 512], P('edge', 'pair')
- atom_out: float32 [1024, 256], P('edge', 'pair')
- atom_feat: float32 [1024, 256], P('edge', 'pair')
- grad_edge: float32 [32768, 512], P('edge', 'pair')
- grad_atom: float32 [1024, 256], P('edge', 'pair')
- grad_quad_rbf: float32 [128, 512], replicated
- grad_quad_down: float32 [512, 32], replicated
- grad_quad_bil: float32 [1024, 32], replicated
- grad_quad_up: float32 [32, 512], replicated
- grad_trip_rbf: float32 [128, 512], replicated
- grad_trip_down: float32 [512, 64], replicated
- grad_trip_bil: float32 [1024, 64], replicated
- grad_trip_up: float32 [64, 512], replicated
- grad_res_one: float32 [512, 512], replicated
- grad_res_two: float32 [512, 512], replicated
- grad_atom_edge: float32 [1024, 512], replicated
- grad_edge_rbf: float32 [128, 512], replicated
- grad_edge_atom: float32 [512, 256], replicated
- grad_out: float32 [256, 256], replicated
The draws below stay inside these ranges and needn't reach their ends.
Inputs may be any that keep to these rules, and one draw needn't show every extreme that they name: `edge_src`: A value below 64 is an atom row of the edge's own partition; a value v at or above it is received row v - 64 of step pool. `halo_send`: entry d * 8 + c of a partition's block is the atom row it sends to partition d as its c-th row. `trip_index`: rows within the edge's own partition. `quad_index`: rows within the quadruplet row's own partition; quadruplet rows d * 32 to d * 32 + 31 of a partition go to partition d. `quad_target`: entry s * 32 + c of a partition's block names the edge of that partition that row c sent by partition s adds to.
All inputs are finite; a program needn't handle non-finite values. No bound on the sum of `trip_live` or of `quad_live` on one device may be relied on, other than what follows from the above.
Results may differ from the reference program's by a relative error of at most 0.0003.
Values sent between devices are 32-bit elements; how exact they have to be, the bound alone decides.
No kernel may reach another device: no remote copies, remote signals or barrier semaphores. Data moves between devices by JAX's collectives and lax.ppermute only.
A program may use at most 256 MiB of HBM per device.

```python
import jax
import jax.numpy as jnp
from jax import lax

DE = 512
DA = 256
TRIPLET_WIDTH = 64
DQ = 32
RBF = 128
CIRCULAR_ORDERS = 16
SBF = 32
E_DEV = 2048
A_DEV = 64
QO_DEV = 512
HALO_DEV = 128
KT = 16
KQ = 8
CAP = 32
HCAP = 8
EDGES = 32768
ATOMS = 1024
QOUT = 8192
HALO_ALL = 2048
N_EDGE = 16


def plant(result, rng, smallest, high):
    index_at = [jax.random.randint(jax.random.fold_in(rng, axis), (), 0, length) for axis, length in enumerate(result.shape)]
    longest = result.shape.index(max(result.shape))
    neighbour = index_at[:longest] + [(index_at[longest] + 1) % result.shape[longest]] + index_at[longest + 1:]
    return result.at[tuple(index_at)].set(smallest).at[tuple(neighbour)].set(high)


def levels(stream_key, shape, split, least, top_value):
    gain, own = 1.0, jax.random.fold_in(stream_key, 6)
    for axis_at, parts in split:
        heights = jnp.exp(jax.random.uniform(jax.random.fold_in(own, axis_at), (parts,), jnp.float32, least / len(split), top_value / len(split)))
        gain = gain * jnp.repeat(heights, shape[axis_at] // parts).reshape([-1 if axis == axis_at else 1 for axis in range(len(shape))])
    return gain


def noise(stream_key, shape, deviation, most, cuts=(), held_as=jnp.bfloat16):
    gain = levels(stream_key, shape, cuts, -0.22, 0.18) if cuts else 1.0
    entries = jax.random.normal(stream_key, shape, jnp.float32) * deviation * gain
    return jnp.minimum(jnp.maximum(entries, -most), most).astype(held_as)


def setup_inputs(seed: int = 0) -> dict:
    arg_keys = jax.random.split(jax.random.key(seed), 32)
    return {
        "edge_embed": noise(arg_keys[0], (EDGES, DE), 1.0, 6.0, ((0, 16), (1, 2)), jnp.float32),
        "atom_embed": noise(arg_keys[1], (ATOMS, DA), 1.0, 6.0, ((0, 16), (1, 2)), jnp.float32),
        "edge_rbf": jnp.clip(1.0 * jax.random.uniform(arg_keys[2], (EDGES, RBF), jnp.float32) ** levels(arg_keys[2], (EDGES, RBF), ((0, 16),), -0.2, 0.2), 0.0, 1.0),
        "edge_src": plant(jax.random.randint(arg_keys[3], (EDGES,), 0, A_DEV + HALO_DEV), jax.random.fold_in(arg_keys[3], 1), 0, (A_DEV + HALO_DEV) - 1).astype(jnp.int32),
        "edge_dst": plant(jax.random.randint(arg_keys[4], (EDGES,), 0, A_DEV), jax.random.fold_in(arg_keys[4], 1), 0, A_DEV - 1).astype(jnp.int32),
        "halo_send": plant(jax.random.randint(arg_keys[5], (HALO_ALL,), 0, A_DEV), jax.random.fold_in(arg_keys[5], 1), 0, A_DEV - 1).astype(jnp.int32),
        "trip_index": plant(jax.random.randint(arg_keys[6], (EDGES, KT), 0, E_DEV), jax.random.fold_in(arg_keys[6], 1), 0, E_DEV - 1).astype(jnp.int32),
        "trip_cos": jnp.clip(jax.random.uniform(arg_keys[7], (EDGES, KT), jnp.float32, -1.0, 1.0) * levels(arg_keys[7], (EDGES, KT), ((0, 16),), -0.4, 0.0), -1.0, 1.0),
        "trip_live": plant((jax.random.randint(arg_keys[8], (EDGES, KT), 0, 4) < 3).astype(jnp.int32), jax.random.fold_in(arg_keys[8], 1), 0, 1),
        "quad_index": plant(jax.random.randint(arg_keys[9], (QOUT, KQ), 0, E_DEV), jax.random.fold_in(arg_keys[9], 1), 0, E_DEV - 1).astype(jnp.int32),
        "quad_cos": jnp.clip(jax.random.uniform(arg_keys[10], (QOUT, KQ), jnp.float32, -1.0, 1.0) * levels(arg_keys[10], (QOUT, KQ), ((0, 16),), -0.4, 0.0), -1.0, 1.0),
        "quad_dih": jnp.clip(jax.random.uniform(arg_keys[11], (QOUT, KQ), jnp.float32, -1.0, 1.0) * levels(arg_keys[11], (QOUT, KQ), ((0, 16),), -0.4, 0.0), -1.0, 1.0),
        "quad_live": plant((jax.random.randint(arg_keys[12], (QOUT, KQ), 0, 4) < 3).astype(jnp.int32), jax.random.fold_in(arg_keys[12], 1), 0, 1),
        "quad_target": plant(jax.random.randint(arg_keys[13], (QOUT,), 0, E_DEV), jax.random.fold_in(arg_keys[13], 1), 0, E_DEV - 1).astype(jnp.int32),
        "w_quad_rbf": noise(arg_keys[14], (RBF, DE), RBF ** -0.5, 0.5, (), jnp.float32),
        "w_quad_down": noise(arg_keys[15], (DE, DQ), DE ** -0.5, 0.25, (), jnp.float32),
        "w_quad_bil": noise(arg_keys[16], (SBF * DQ, DQ), (SBF * DQ // 4) ** -0.5, 0.375, (), jnp.float32),
        "w_quad_up": noise(arg_keys[17], (DQ, DE), DQ ** -0.5, 1.0, (), jnp.float32),
        "w_trip_rbf": noise(arg_keys[18], (RBF, DE), RBF ** -0.5, 0.5, (), jnp.float32),
        "w_trip_down": noise(arg_keys[19], (DE, TRIPLET_WIDTH), DE ** -0.5, 0.25, (), jnp.float32),
        "triplet_bilinear_weight": noise(arg_keys[20], (CIRCULAR_ORDERS * TRIPLET_WIDTH, TRIPLET_WIDTH), (CIRCULAR_ORDERS * TRIPLET_WIDTH // 4) ** -0.5, 0.375, (), jnp.float32),
        "w_trip_up": noise(arg_keys[21], (TRIPLET_WIDTH, DE), TRIPLET_WIDTH ** -0.5, 0.75, (), jnp.float32),
        "w_res_one": noise(arg_keys[22], (DE, DE), DE ** -0.5, 0.25, (), jnp.float32),
        "w_res_two": noise(arg_keys[23], (DE, DE), (DE // 4) ** -0.5, 0.5, (), jnp.float32),
        "w_atom_edge": noise(arg_keys[24], (2 * DA + DE, DE), (2 * DA + DE) ** -0.5, 0.1875, (), jnp.float32),
        "w_edge_rbf": noise(arg_keys[25], (RBF, DE), RBF ** -0.5, 0.5, (), jnp.float32),
        "w_edge_atom": noise(arg_keys[26], (DE, DA), (DE // 4) ** -0.5, 0.5, (), jnp.float32),
        "w_out": noise(arg_keys[27], (DA, DA), DA ** -0.5, 0.375, (), jnp.float32),
        "cot_edge": noise(arg_keys[28], (EDGES, DE), 1.0, 6.0, ((0, 16), (1, 2)), jnp.float32),
        "cot_atom": noise(arg_keys[29], (ATOMS, DA), 1.0, 6.0, ((0, 16), (1, 2)), jnp.float32),
        "cot_feat": noise(arg_keys[30], (ATOMS, DA), 1.0, 6.0, ((0, 16), (1, 2)), jnp.float32),
    }


@jax.custom_vjp
def low(v):
    return lax.optimization_barrier(v.astype(jnp.bfloat16)).astype(jnp.float32)

@jax.custom_vjp
def low_back(v):
    return v

def low_keep(v):
    return (low(v), None)

def low_pass(kept, grad):
    return (grad,)

def back_keep(v):
    return (v, None)

def back_low(kept, grad):
    return (low(grad),)
low.defvjp(low_keep, low_pass)
low_back.defvjp(back_keep, back_low)
root_third = 0.5773502691896258
root_half = 0.7071067811865476

def matmul(left, right):
    return jnp.dot(left, right, precision=lax.Precision.HIGHEST, preferred_element_type=jnp.float32)

def legendre(cosine, orders):
    series = [jnp.ones_like(cosine), cosine]
    for order in range(1, orders - 1):
        series.append(((2 * order + 1) * cosine * series[-1] - order * series[-2]) / (order + 1))
    return jnp.stack(series[:orders], axis=-1)

def triplet_expansion(cosine, live_slots, orders):
    return legendre(cosine, orders) * live_slots.astype(jnp.float32)[..., None]

def quadruplet_expansion(cosine, dihedral, live_slots, orders):
    angular = triplet_expansion(cosine, live_slots, orders)
    return jnp.concatenate([angular, angular * dihedral[..., None]], axis=-1)

def local_quad(embedding, radial, indices, basis_values, quad_weights):
    w_radial, w_down, w_bilinear = quad_weights
    mixed = jax.nn.silu(matmul(embedding * matmul(radial, w_radial), w_down))
    selected_rows = mixed[indices]
    basis_product = jnp.einsum('pcd,pce->pde', basis_values, selected_rows, precision=lax.Precision.HIGHEST)
    return matmul(basis_product.reshape(basis_product.shape[0], -1), w_bilinear)

def local_interaction(embedding, atom_rows, halo_rows, quad_sum, radial, sources, targets, indices, basis_values, inter_weights):
    w_radial, w_down, w_bilinear, w_lift, w_res_one, w_res_two, w_atom_edge, w_edge_rbf, w_edge_atom, w_out = inter_weights
    mixed = jax.nn.silu(matmul(embedding * matmul(radial, w_radial), w_down))
    selected_rows = mixed[indices]
    basis_product = jnp.einsum('eks,eki->esi', basis_values, selected_rows, precision=lax.Precision.HIGHEST)
    triplet = matmul(matmul(basis_product.reshape(basis_product.shape[0], -1), w_bilinear), w_lift)
    joined = (embedding + triplet + quad_sum) * root_third
    hidden = jax.nn.silu(matmul(joined, w_res_one))
    residual = (joined + jax.nn.silu(matmul(hidden, w_res_two))) * root_half
    atom_pool = jnp.concatenate([atom_rows, halo_rows], axis=0)
    stacked = jnp.concatenate([atom_pool[sources], atom_rows[targets], residual], axis=1)
    edge_new = (residual + jax.nn.silu(matmul(stacked, w_atom_edge))) * root_half
    weighted = edge_new * matmul(radial, w_edge_rbf)
    member = (targets[None, :] == jnp.arange(atom_rows.shape[0], dtype=jnp.int32)[:, None]).astype(jnp.float32)
    collected = matmul(member, weighted) * (atom_rows.shape[0] / embedding.shape[0]) ** 0.5
    atom_new = (atom_rows + jax.nn.silu(matmul(collected, w_edge_atom))) * root_half
    feature = jax.nn.silu(matmul(atom_new, w_out))
    return (edge_new, atom_new, feature)

def reference(edge_embed, atom_embed, edge_rbf, edge_src, edge_dst, halo_send, trip_index, trip_cos, trip_live, quad_index, quad_cos, quad_dih, quad_live, quad_target, w_quad_rbf, w_quad_down, w_quad_bil, w_quad_up, w_trip_rbf, w_trip_down, triplet_bilinear_weight, w_trip_up, w_res_one, w_res_two, w_atom_edge, w_edge_rbf, w_edge_atom, w_out, cot_edge, cot_atom, cot_feat):
    groups = N_EDGE
    rbf_blocks = edge_rbf.reshape(groups, E_DEV, RBF)
    source_blocks = edge_src.reshape(groups, E_DEV)
    target_blocks = edge_dst.reshape(groups, E_DEV)
    send_blocks = halo_send.reshape(groups, HALO_DEV)
    trip_blocks = trip_index.reshape(groups, E_DEV, KT)
    trip_cos_blocks = trip_cos.reshape(groups, E_DEV, KT)
    trip_live_blocks = trip_live.reshape(groups, E_DEV, KT)
    quad_blocks = quad_index.reshape(groups, QO_DEV, KQ)
    quad_cos_blocks = quad_cos.reshape(groups, QO_DEV, KQ)
    quad_dih_blocks = quad_dih.reshape(groups, QO_DEV, KQ)
    quad_live_blocks = quad_live.reshape(groups, QO_DEV, KQ)
    quad_target_blocks = quad_target.reshape(groups, QO_DEV)
    weights = (w_quad_rbf, w_quad_down, w_quad_bil, w_quad_up, w_trip_rbf, w_trip_down, triplet_bilinear_weight, w_trip_up, w_res_one, w_res_two, w_atom_edge, w_edge_rbf, w_edge_atom, w_out)

    def forward(embedding, atom_rows, weight_set):
        quad_weights = weight_set[:3]
        lift = weight_set[3]
        inter_weights = weight_set[4:]
        embed_blocks = embedding.reshape(groups, E_DEV, DE)
        atom_blocks = atom_rows.reshape(groups, A_DEV, DA)

        def quad_part(pieces):
            part_embed, part_rbf, part_index, partition_cosine, partition_dihedral, partition_active = pieces
            basis_values = quadruplet_expansion(partition_cosine, partition_dihedral, partition_active, CIRCULAR_ORDERS)
            return local_quad(part_embed, part_rbf, part_index, basis_values, quad_weights)
        quad_rows = lax.map(jax.checkpoint(quad_part), (embed_blocks, rbf_blocks, quad_blocks, quad_cos_blocks, quad_dih_blocks, quad_live_blocks))
        lifted = matmul(quad_rows.reshape(groups * QO_DEV, DQ), lift)
        routed = lifted.reshape(groups, groups, CAP, DE).transpose(1, 0, 2, 3).reshape(groups, QO_DEV, DE)
        quad_sum = jax.vmap(lambda targets, values: jnp.zeros((E_DEV, DE), jnp.float32).at[targets].add(values))(quad_target_blocks, routed)
        sent = jax.vmap(lambda rows, picks: rows[picks])(atom_blocks, send_blocks)
        halo_rows = sent.reshape(groups, groups, HCAP, DA).transpose(1, 0, 2, 3).reshape(groups, HALO_DEV, DA)

        def inter_part(pieces):
            part_embed, part_atoms, part_halo, part_quad, part_rbf, part_src, part_dst, part_index, partition_cosine, partition_active = pieces
            basis_values = triplet_expansion(partition_cosine, partition_active, CIRCULAR_ORDERS)
            return local_interaction(part_embed, part_atoms, part_halo, part_quad, part_rbf, part_src, part_dst, part_index, basis_values, inter_weights)
        edge_new, atom_new, feature = lax.map(jax.checkpoint(inter_part), (embed_blocks, atom_blocks, halo_rows, quad_sum, rbf_blocks, source_blocks, target_blocks, trip_blocks, trip_cos_blocks, trip_live_blocks))
        return (edge_new.reshape(EDGES, DE), atom_new.reshape(ATOMS, DA), feature.reshape(ATOMS, DA))
    outputs, pullback = jax.vjp(forward, edge_embed, atom_embed, weights)
    grad_embed, grad_atoms, grad_weights = pullback((cot_edge, cot_atom, cot_feat))
    return (outputs[0], outputs[1], outputs[2], grad_embed, grad_atoms, grad_weights[0], grad_weights[1], grad_weights[2], grad_weights[3], grad_weights[4], grad_weights[5], grad_weights[6], grad_weights[7], grad_weights[8], grad_weights[9], grad_weights[10], grad_weights[11], grad_weights[12], grad_weights[13])
```

```python
import functools

import jax
import jax.numpy as jnp
from jax import lax
from jax.experimental import pallas as pl
from jax.experimental.pallas import tpu as pltpu
from jax.sharding import PartitionSpec as P

f32, bf16, i32 = jnp.float32, jnp.bfloat16, jnp.int32
root_third = 0.5773502691896258
root_half = 0.7071067811865476
LANES = 128
CLASSES = 4
VMEM_LIMIT = 56 * 2**20


def split(x):
    high = x.astype(bf16)
    return high, (x - high.astype(f32)).astype(bf16)


def dot(left, right, dims):
    return lax.dot_general(left, right, (dims, ((), ())), preferred_element_type=f32)


NN = ((1,), (0,))
NT = ((1,), (1,))
TN = ((0,), (0,))


def dot3(left, right, dims=NN):
    lh, ll = left if isinstance(left, tuple) else split(left)
    rh, rl = right if isinstance(right, tuple) else split(right)
    return dot(lh, rh, dims) + dot(lh, rl, dims) + dot(ll, rh, dims)


def pick(onehot, right, dims=NN):
    rh, rl = right if isinstance(right, tuple) else split(right)
    return dot(onehot, rh, dims) + dot(onehot, rl, dims)


def sigmoid(v):
    return 0.5 * jnp.tanh(0.5 * v) + 0.5


def silu(v):
    return v * sigmoid(v)


def silu_grad(v):
    s = sigmoid(v)
    return s * (1.0 + v * (1.0 - s))


def as_bf16(mask):
    return mask.astype(f32).astype(bf16)


def legendre_steps(cosine, orders):
    before, now = jnp.ones_like(cosine), cosine
    yield before
    yield now
    for order in range(1, orders - 1):
        before, now = now, ((2 * order + 1) / (order + 1)) * cosine * now - (order / (order + 1)) * before
        yield now


def class_table(own, other, classes):
    per = classes // 2
    step = own.shape[1] // per
    parts = []
    for block in (own, other):
        high, low = split(block)
        for q in range(per):
            parts += [high[:, q * step : (q + 1) * step], low[:, q * step : (q + 1) * step]]
    return jnp.concatenate(parts, axis=0)


def gather_classes(table, index, classes, width):
    step = table.shape[1]
    shift = step.bit_length() - 1
    slots = index.shape[1]
    onehot = as_bf16(lax.broadcasted_iota(i32, (step, slots), 0) == (index & (step - 1)))
    found = dot(table, onehot, NN)
    kind = index >> shift
    out = found[0:width] + found[width : 2 * width]
    for q in range(1, classes):
        base = q * 2 * width
        out = jnp.where(kind >= q, found[base : base + width] + found[base + width : base + 2 * width], out)
    return out


def scatter_classes(values, indices, classes, step):
    shift = step.bit_length() - 1
    lefts, rights = [], []
    for value, index in zip(values, indices):
        width, slots = value.shape
        high, low = split(value)
        both = jnp.concatenate([high, low], axis=0)
        kind = jnp.broadcast_to(index >> shift, (2 * width, slots))
        lefts.append(jnp.concatenate([jnp.where(kind == q, both, jnp.zeros((), bf16)) for q in range(classes)], axis=0))
        rights.append(as_bf16(lax.broadcasted_iota(i32, (step, slots), 0) == (index & (step - 1))))
    return dot(jnp.concatenate(lefts, axis=1), jnp.concatenate(rights, axis=1), NT)


def unfold_classes(sums, classes, width):
    parts = []
    for q in range(classes):
        base = q * 2 * width
        parts.append(sums[base : base + width] + sums[base + width : base + 2 * width])
    return jnp.concatenate(parts, axis=1)


def down_kernel(role, own, recv, rbf, w_rad, w_down, emb_out, pre_out, table_out, rad_h, rad_l, down_h, down_l):
    @pl.when(pl.program_id(0) == 0)
    def _():
        rad_h[...], rad_l[...] = split(w_rad[...])
        down_h[...], down_l[...] = split(w_down[...])

    zero = role[0] == 0
    mine, theirs = own[...], recv[...]
    emb = jnp.concatenate([jnp.where(zero, mine, theirs), jnp.where(zero, theirs, mine)], axis=1)
    emb_out[...] = emb
    radial = dot3(rbf[...], (rad_h[...], rad_l[...]))
    mixed = jnp.concatenate([emb, emb], axis=1) * radial
    pre = dot3(mixed, (down_h[...], down_l[...]))
    pre_out[...] = pre
    table_out[...] = silu(pre).T


def quad_forward_kernel(own, other, index, cosine, dihedral, live, w_bil, z_out, rows_out, sel, sel2, basis, *, orders, base):
    slots_k, rows = index.shape
    width = w_bil.shape[1]
    table = class_table(own[base : base + width, :], other[base : base + width, :], 2 * CLASSES)
    alive = live[...].astype(f32)
    for order, series in enumerate(legendre_steps(cosine[...], orders)):
        basis[order] = series * alive
    for k in range(slots_k):
        picked = gather_classes(table, index[k : k + 1, :], 2 * CLASSES, width)
        sel[k] = picked
        sel2[k] = picked * dihedral[k : k + 1, :]
    groups = width // 8
    for t in range(rows // LANES):
        at = slice(t * LANES, (t + 1) * LANES)
        for part, source in enumerate((sel, sel2)):
            for order_at in range(0, orders, 8):
                sums = {}
                for k in range(slots_k):
                    chosen = [source[k, g * 8 : g * 8 + 8, at] for g in range(groups)]
                    for order in range(8):
                        weight = jnp.broadcast_to(basis[order_at + order, k : k + 1, at], (8, LANES))
                        for g in range(groups):
                            term = weight * chosen[g]
                            sums[order, g] = term if k == 0 else sums[order, g] + term
                for (order, g), total in sums.items():
                    row = (part * orders + order_at + order) * width + g * 8
                    z_out[row : row + 8, at] = total
    rows_out[...] = dot3(w_bil[...], z_out[...], TN).T


def triplet_forward_kernel(own, other, index, cosine, live, w_bil, z_out, mid_out, table, sel, basis, bil_h, bil_l, *, orders):
    slots_k, tile = index.shape
    width = w_bil.shape[1]

    @pl.when(pl.program_id(0) == 0)
    def _():
        table[...] = class_table(own[0:width, :], other[0:width, :], CLASSES)
        bil_h[...], bil_l[...] = split(w_bil[...])

    alive = live[...].astype(f32)
    for order, series in enumerate(legendre_steps(cosine[...], orders)):
        basis[order] = series * alive

    def gather_step(k, carry):
        sel[k] = gather_classes(table[...], index[pl.ds(k, 1), :], CLASSES, width)
        return carry

    lax.fori_loop(0, slots_k, gather_step, 0)
    for t in range(tile // LANES):
        at = slice(t * LANES, (t + 1) * LANES)
        for first in range(0, width // 8, 2):
            sums = {}
            for k in range(slots_k):
                chosen = [sel[k, g * 8 : g * 8 + 8, at] for g in (first, first + 1)]
                for order in range(orders):
                    weight = jnp.broadcast_to(basis[order, k : k + 1, at], (8, LANES))
                    for g in range(2):
                        term = weight * chosen[g]
                        sums[order, g] = term if k == 0 else sums[order, g] + term
            for (order, g), total in sums.items():
                row = order * width + (first + g) * 8
                z_out[row : row + 8, at] = total
    mid = dot3((bil_h[...], bil_l[...]), z_out[...], TN)
    mid_out[...] = jnp.concatenate([mid, jnp.zeros_like(mid)], axis=0).T


def rows_by_role(zero, mine, theirs):
    return jnp.concatenate([jnp.where(zero, mine, theirs), jnp.where(zero, theirs, mine)], axis=1)


def pool_of(zero, atom_own, atom_recv, halo_own, halo_recv):
    atoms = rows_by_role(zero, atom_own, atom_recv)
    halo = rows_by_role(zero, halo_own, halo_recv)
    return atoms, jnp.concatenate([atoms, halo], axis=0)


def main_forward_kernel(
    role, emb, mid_trip, rbf, ends, target, quad_rows, atom_own, atom_recv, halo_own, halo_recv,
    w_up, w_one, w_two, w_edge, w_rbf,
    mid_out, joined_out, one_out, two_out, six_out, new_own, new_send, collected,
    up, one, two, three, rad, pool_w, quad_hl,
):
    step = pl.program_id(0)
    tile = emb.shape[0]
    atoms = atom_own.shape[0]
    pool_rows = atoms + halo_own.shape[0]
    atom_width = 2 * atom_own.shape[1]
    zero = role[0] == 0

    @pl.when(step == 0)
    def _():
        up[0], up[1] = split(w_up[...])
        one[0], one[1] = split(w_one[...])
        two[0], two[1] = split(w_two[...])
        three[0], three[1] = split(w_edge[2 * atom_width :, :])
        rad[0], rad[1] = split(w_rbf[...])
        atom_rows, pool = pool_of(zero, atom_own[...], atom_recv[...], halo_own[...], halo_recv[...])
        projected = jnp.concatenate(
            [dot3(pool, w_edge[0:atom_width, :]), dot3(atom_rows, w_edge[atom_width : 2 * atom_width, :])], axis=0
        )
        pool_w[0], pool_w[1] = split(projected)
        high, low = split(quad_rows[...])
        quad_hl[...] = jnp.concatenate([high, low], axis=1)

    own_row = lax.broadcasted_iota(i32, (tile, target.shape[1]), 0) + step * tile
    found = dot(as_bf16(own_row == target[...]), quad_hl[...], NN)
    width = found.shape[1] // 2
    mid = mid_trip[...] + found[:, :width] + found[:, width:]
    mid_out[...] = mid
    joined = (emb[...] + dot3(mid, (up[0], up[1]))) * root_third
    joined_out[...] = joined
    pre_one = dot3(joined, (one[0], one[1]))
    one_out[...] = pre_one
    pre_two = dot3(silu(pre_one), (two[0], two[1]))
    two_out[...] = pre_two
    residual = (joined + silu(pre_two)) * root_half
    row = lax.broadcasted_iota(i32, (pool_rows + atoms, tile), 0)
    member = as_bf16(row == jnp.where(row < pool_rows, ends[0:1, :], ends[1:2, :] + pool_rows))
    pre_six = pick(member, (pool_w[0], pool_w[1]), TN) + dot3(residual, (three[0], three[1]))
    six_out[...] = pre_six
    edge_new = (residual + silu(pre_six)) * root_half
    half = edge_new.shape[1] // 2
    new_own[...] = jnp.where(zero, edge_new[:, :half], edge_new[:, half:])
    new_send[...] = jnp.where(zero, edge_new[:, half:], edge_new[:, :half])
    weighted = edge_new * dot3(rbf[...], (rad[0], rad[1]))
    part = pick(member[pool_rows:, :], weighted)

    @pl.when(step == 0)
    def _():
        collected[...] = part

    @pl.when(step > 0)
    def _():
        collected[...] += part


def main_backward_kernel(
    role, joined, pre_one_ref, pre_two_ref, pre_six_ref, mid_ref, rbf, ends, target, cot_own, cot_recv,
    coll_own, coll_recv, small_own, small_recv, halo_own, halo_recv,
    w_up, w_one, w_two, w_edge, w_rbf, w_edge_atom, w_out,
    sum_grad_out, mid_grad_out, grads, quad_back, pool_grad_own, pool_grad_send, atom_out, feat_out, up_grad,
    up, one, two, three, rad, coll_grad, pool_sum, direct,
    *, scale,
):
    step = pl.program_id(0)
    last = pl.num_programs(0) - 1
    tile = joined.shape[0]
    edge_width = joined.shape[1]
    atoms = small_own.shape[0]
    half = small_own.shape[1] // 3
    atom_width = 2 * half
    pool_rows = atoms + halo_own.shape[0]
    zero = role[0] == 0
    at_edge = 0
    at_two = at_edge + w_edge.shape[0]
    at_one = at_two + edge_width
    at_rbf = at_one + edge_width
    at_atom = at_rbf + w_rbf.shape[0]
    at_last = at_atom + edge_width * atom_width // edge_width

    @pl.when(step == 0)
    def _():
        up[0], up[1] = split(w_up[...])
        one[0], one[1] = split(w_one[...])
        two[0], two[1] = split(w_two[...])
        three[0], three[1] = split(w_edge[2 * atom_width :, :])
        rad[0], rad[1] = split(w_rbf[...])
        mine, theirs = small_own[...], small_recv[...]
        atom_rows = rows_by_role(zero, mine[:, :half], theirs[:, :half])
        cot_atom = rows_by_role(zero, mine[:, half : 2 * half], theirs[:, half : 2 * half])
        cot_feat = rows_by_role(zero, mine[:, 2 * half :], theirs[:, 2 * half :])
        total = (coll_own[...] + coll_recv[...]) * scale
        w_a, w_f = split(w_edge_atom[...]), split(w_out[...])
        pre_atom = dot3(total, w_a)
        atom_new = (atom_rows + silu(pre_atom)) * root_half
        pre_feat = dot3(atom_new, w_f)
        feature = silu(pre_feat)
        atom_out[...] = jnp.where(zero, atom_new[:, :half], atom_new[:, half:])
        feat_out[...] = jnp.where(zero, feature[:, :half], feature[:, half:])
        feat_grad = cot_feat * silu_grad(pre_feat)
        out_grad = 0.5 * dot3(atom_new, feat_grad, TN)
        rows = out_grad.shape[0] // 2
        grads[at_last : at_last + rows, :] = jnp.concatenate([out_grad[:rows], out_grad[rows:]], axis=1)
        atom_grad = (cot_atom + dot3(feat_grad, w_f, NT)) * root_half
        direct[...] = 0.5 * atom_grad
        pre_grad = atom_grad * silu_grad(pre_atom)
        ea_grad = 0.5 * dot3(total, pre_grad, TN)
        rows = ea_grad.shape[0] // 2
        grads[at_atom : at_atom + rows, :] = jnp.concatenate([ea_grad[:rows], ea_grad[rows:]], axis=1)
        coll_grad[0], coll_grad[1] = split(dot3(pre_grad, w_a, NT) * scale)
        grads[0:at_atom, :] = jnp.zeros((at_atom, grads.shape[1]), f32)
        quad_back[...] = jnp.zeros_like(quad_back)
        pool_sum[...] = jnp.zeros_like(pool_sum)
        up_grad[...] = jnp.zeros_like(up_grad)

    row = lax.broadcasted_iota(i32, (pool_rows + atoms, tile), 0)
    member = as_bf16(row == jnp.where(row < pool_rows, ends[0:1, :], ends[1:2, :] + pool_rows))
    joined_now = joined[...]
    pre_two = pre_two_ref[...]
    pre_six = pre_six_ref[...]
    s_two = sigmoid(pre_two)
    s_six = sigmoid(pre_six)
    residual = (joined_now + pre_two * s_two) * root_half
    edge_new = (residual + pre_six * s_six) * root_half
    radial = rbf[...]
    radial_split = split(radial)
    weighted_grad = pick(member[pool_rows:, :], (coll_grad[0], coll_grad[1]), TN)
    grads[at_rbf : at_rbf + rbf.shape[1], :] += dot3(radial_split, weighted_grad * edge_new, TN)
    new_grad = rows_by_role(zero, cot_own[...], cot_recv[...])
    new_grad = (new_grad + weighted_grad * dot3(radial_split, (rad[0], rad[1]))) * root_half
    six_grad = new_grad * (s_six * (1.0 + pre_six * (1.0 - s_six)))
    six_split = split(six_grad)
    pool_sum[...] += pick(member, six_split)
    grads[at_edge + 2 * atom_width : at_two, :] += dot3(residual, six_split, TN)
    res_grad = (new_grad + dot3(six_split, (three[0], three[1]), NT)) * root_half
    two_grad = res_grad * (s_two * (1.0 + pre_two * (1.0 - s_two)))
    two_split = split(two_grad)
    pre_one = pre_one_ref[...]
    s_one = sigmoid(pre_one)
    grads[at_two : at_two + edge_width, :] += dot3(pre_one * s_one, two_split, TN)
    one_grad = dot3(two_split, (two[0], two[1]), NT) * (s_one * (1.0 + pre_one * (1.0 - s_one)))
    one_split = split(one_grad)
    grads[at_one : at_one + edge_width, :] += dot3(joined_now, one_split, TN)
    sum_grad = (res_grad + dot3(one_split, (one[0], one[1]), NT)) * root_third
    sum_grad_out[...] = sum_grad
    sum_split = split(sum_grad)
    up_grad[...] += dot3(mid_ref[...], sum_split, TN)
    mid_grad = dot3(sum_split, (up[0], up[1]), NT)
    mid_grad_out[...] = mid_grad
    own_row = lax.broadcasted_iota(i32, (tile, target.shape[1]), 0) + step * tile
    high, low = split(mid_grad)
    back = dot(as_bf16(own_row == target[...]), jnp.concatenate([high, low], axis=1), TN)
    width = mid_grad.shape[1]
    quad_back[...] += back[:, :width] + back[:, width:]

    @pl.when(step == last)
    def _():
        atom_rows, pool = pool_of(zero, small_own[:, :half], small_recv[:, :half], halo_own[...], halo_recv[...])
        w_src, w_dst = split(w_edge[0:atom_width, :]), split(w_edge[atom_width : 2 * atom_width, :])
        src_split, dst_split = split(pool_sum[0:pool_rows, :]), split(pool_sum[pool_rows:, :])
        grads[at_edge : at_edge + atom_width, :] = dot3(pool, src_split, TN)
        grads[at_edge + atom_width : at_edge + 2 * atom_width, :] = dot3(atom_rows, dst_split, TN)
        from_src = dot3(src_split, w_src, NT)
        from_atoms = from_src[0:atoms] + dot3(dst_split, w_dst, NT) + direct[...]
        result = jnp.concatenate([from_atoms, from_src[atoms:]], axis=0)
        pool_grad_own[...] = jnp.where(zero, result[:, :half], result[:, half:])
        pool_grad_send[...] = jnp.where(zero, result[:, half:], result[:, :half])


def triplet_backward_kernel(mid_grad, z, index, cosine, live, w_bil, bil_grad, table_grad, zg, sg, basis, sums, bil_h, bil_l, *, orders):
    step = pl.program_id(0)
    slots_k, tile = index.shape
    width = w_bil.shape[1]
    classes_step = sums.shape[1]

    @pl.when(step == 0)
    def _():
        bil_h[...], bil_l[...] = split(w_bil[...])
        bil_grad[...] = jnp.zeros_like(bil_grad)
        sums[...] = jnp.zeros_like(sums)

    alive = live[...].astype(f32)
    for order, series in enumerate(legendre_steps(cosine[...], orders)):
        basis[order] = series * alive
    grad = mid_grad[...]
    lane = lax.broadcasted_iota(i32, grad.shape, 1)
    grad = jnp.where(lane < width, grad, 0.0)
    bil_grad[...] += dot3(z[...], grad)
    zg[...] = dot3((bil_h[...], bil_l[...]), grad.T[0:width, :])
    for t in range(tile // LANES):
        at = slice(t * LANES, (t + 1) * LANES)
        for first in range(0, width // 8, 2):
            totals = {}
            for order in range(orders):
                row = order * width + first * 8
                got = [zg[row + g * 8 : row + g * 8 + 8, at] for g in range(2)]
                for k in range(slots_k):
                    weight = jnp.broadcast_to(basis[order, k : k + 1, at], (8, LANES))
                    for g in range(2):
                        term = weight * got[g]
                        totals[k, g] = term if order == 0 else totals[k, g] + term
            for (k, g), total in totals.items():
                sg[k, (first + g) * 8 : (first + g) * 8 + 8, at] = total

    def scatter_step(at, carry):
        first = at * 4
        sums[...] += scatter_classes(
            [sg[first + q] for q in range(4)], [index[pl.ds(first + q, 1), :] for q in range(4)], CLASSES, classes_step
        )
        return carry

    lax.fori_loop(0, slots_k // 4, scatter_step, 0)

    @pl.when(step == pl.num_programs(0) - 1)
    def _():
        table_grad[...] = unfold_classes(sums[...], CLASSES, width)


def quad_backward_kernel(rows_grad, z, index, cosine, dihedral, live, w_bil, bil_grad_in, grads, table_grad, zg, sg, basis, *, orders, base):
    slots_k, rows = index.shape
    width = w_bil.shape[1]
    alive = live[...].astype(f32)
    for order, series in enumerate(legendre_steps(cosine[...], orders)):
        basis[order] = series * alive
    grad = rows_grad[...]
    lane = lax.broadcasted_iota(i32, grad.shape, 1)
    grad = jnp.where((lane >= base) & (lane < base + width), grad, 0.0)
    both = bil_grad_in[...] + dot3(z[...], grad)
    count = both.shape[0] // 4
    grads[...] = jnp.concatenate([both[q * count : (q + 1) * count] for q in range(4)], axis=1)
    zg[...] = dot3(w_bil[...], grad.T[base : base + width, :])
    groups = width // 8
    for t in range(rows // LANES):
        at = slice(t * LANES, (t + 1) * LANES)
        for g in range(groups):
            plain, turned = {}, {}
            for order in range(orders):
                one = zg[order * width + g * 8 : order * width + g * 8 + 8, at]
                two = zg[(orders + order) * width + g * 8 : (orders + order) * width + g * 8 + 8, at]
                for k in range(slots_k):
                    weight = jnp.broadcast_to(basis[order, k : k + 1, at], (8, LANES))
                    plain[k] = weight * one if order == 0 else plain[k] + weight * one
                    turned[k] = weight * two if order == 0 else turned[k] + weight * two
            for k in range(slots_k):
                sg[k, g * 8 : g * 8 + 8, at] = plain[k] + turned[k] * jnp.broadcast_to(dihedral[k : k + 1, at], (8, LANES))
    step = table_grad.shape[1] // (2 * CLASSES)
    sums = scatter_classes([sg[k] for k in range(slots_k)], [index[k : k + 1, :] for k in range(slots_k)], 2 * CLASSES, step)
    table_grad[...] = unfold_classes(sums, 2 * CLASSES, width)


def final_kernel(
    role, emb_ref, rbf, pre_ref, trip_own, trip_recv, quad_own, quad_recv, sum_grad, w_rad, w_down,
    grad_own, grad_send, rad_grad, down_grad,
    rad, down, total,
):
    step = pl.program_id(0)
    zero = role[0] == 0

    @pl.when(step == 0)
    def _():
        rad[0], rad[1] = split(w_rad[...])
        down[0], down[1] = split(w_down[...])
        rad_grad[...] = jnp.zeros_like(rad_grad)
        total[...] = jnp.zeros_like(total)

    emb = emb_ref[...]
    width = emb.shape[1]
    radial_split = split(rbf[...])
    radial = dot3(radial_split, (rad[0], rad[1]))
    doubled = jnp.concatenate([emb, emb], axis=1)
    trip = trip_own[...] + trip_recv[...]
    quad = quad_own[...] + quad_recv[...]
    rest = LANES - trip.shape[0] - quad.shape[0]
    table = jnp.concatenate([trip, quad, jnp.zeros((rest, trip.shape[1]), f32)], axis=0).T
    pre_split = split(table * silu_grad(pre_ref[...]))
    total[...] += dot3(doubled * radial, pre_split, TN)
    mixed_grad = dot3(pre_split, (down[0], down[1]), NT)
    spread = mixed_grad * radial
    grad = sum_grad[...] + spread[:, :width] + spread[:, width:]
    half = width // 2
    grad_own[...] = jnp.where(zero, grad[:, :half], grad[:, half:])
    grad_send[...] = jnp.where(zero, grad[:, half:], grad[:, :half])
    update = dot3(radial_split, mixed_grad * doubled, TN)
    rows = update.shape[0]
    rad_grad[0:rows, :] += update[:, :width]
    rad_grad[rows:, :] += update[:, width:]

    @pl.when(step == pl.num_programs(0) - 1)
    def _():
        lane = lax.broadcasted_iota(i32, (width, LANES), 1)
        both = jnp.where(lane < trip.shape[0], total[0:width, :], total[width:, :])
        count = width // 4
        down_grad[...] = jnp.concatenate([both[q * count : (q + 1) * count] for q in range(4)], axis=1)


def whole(shape):
    return pl.BlockSpec(shape, lambda *_: (0,) * len(shape))


def rows_of(tile, width):
    return pl.BlockSpec((tile, width), lambda i, *_: (i, 0))


def columns_of(rows, tile):
    return pl.BlockSpec((rows, tile), lambda i, *_: (0, i))


def out(*shape):
    return jax.ShapeDtypeStruct(shape, f32)


def call(body, name, grid, in_specs, out_specs, out_shape, scratch, args, scalars=0, flops=0):
    size = sum(a.size * 4 for a in args) + sum(o.size * 4 for o in out_shape)
    return pl.pallas_call(
        body,
        name=name,
        grid_spec=pltpu.PrefetchScalarGridSpec(
            num_scalar_prefetch=scalars, grid=grid, in_specs=in_specs, out_specs=out_specs, scratch_shapes=scratch
        ),
        out_shape=out_shape,
        compiler_params=pltpu.CompilerParams(vmem_limit_bytes=VMEM_LIMIT, dimension_semantics=("arbitrary",) * len(grid)),
        cost_estimate=pl.CostEstimate(flops=flops, bytes_accessed=size, transcendentals=0),
    )(*args)


def swap(x):
    return lax.ppermute(x, "pair", [(0, 1), (1, 0)])


def reduce_everywhere(buffer):
    return lax.psum(buffer, ("pair", "edge"))


def local(
    edge_embed, atom_embed, edge_rbf, edge_src, edge_dst, halo_send, trip_index, trip_cos, trip_live,
    quad_index, quad_cos, quad_dih, quad_live, quad_target,
    w_quad_rbf, w_quad_down, w_quad_bil, w_quad_up, w_trip_rbf, w_trip_down, w_trip_bil, w_trip_up,
    w_res_one, w_res_two, w_atom_edge, w_edge_rbf, w_edge_atom, w_out,
    cot_edge, cot_atom, cot_feat,
):
    peers = lax.axis_size("edge")
    role = lax.axis_index("pair")
    role_arg = role.astype(i32).reshape(1)
    edges, half_width = edge_embed.shape
    half = edges // 2
    width = 2 * half_width
    atoms, half_atom = atom_embed.shape
    radial_width = edge_rbf.shape[1]
    slots = trip_index.shape[1]
    quad_slots = quad_index.shape[1]
    quad_count = quad_index.shape[0]
    half_quad = quad_count // 2
    halo_count = halo_send.shape[0]
    trip_width = w_trip_down.shape[1]
    quad_width = w_quad_down.shape[1]
    orders = w_trip_bil.shape[0] // trip_width
    tile = half // 4
    grid = (half // tile,)
    pad = LANES - trip_width - quad_width

    def own_rows(x, which=role, count=half):
        return lax.dynamic_slice_in_dim(x, which * count, count, axis=0)

    def local_rows(index):
        return jnp.where(role == 0, index, jnp.where(index < half, index + half, index - half))

    emb_recv = swap(own_rows(edge_embed, 1 - role))
    cot_recv = swap(own_rows(cot_edge, 1 - role))
    small_own = jnp.concatenate([atom_embed, cot_atom, cot_feat], axis=1)
    small_recv = swap(small_own)

    w_rad = jnp.concatenate([w_trip_rbf, w_quad_rbf], axis=1)
    w_down = jnp.concatenate(
        [jnp.pad(w_trip_down, ((0, 0), (0, LANES - trip_width))), jnp.pad(w_quad_down, ((0, 0), (trip_width, pad)))], axis=0
    )
    w_up = jnp.concatenate([w_trip_up, w_quad_up, jnp.zeros((pad, width), f32)], axis=0)
    t_index = local_rows(own_rows(trip_index)).T
    t_cos = own_rows(trip_cos).T
    t_live = own_rows(trip_live).T

    def own_quad(x, which=role):
        parts = x.reshape(peers, 2, quad_count // peers // 2, *x.shape[1:])
        return lax.dynamic_index_in_dim(parts, which, axis=1, keepdims=False).reshape(half_quad, *x.shape[1:])

    q_index = local_rows(own_quad(quad_index)).T
    q_cos, q_dih, q_live = (own_quad(x).T for x in (quad_cos, quad_dih, quad_live))
    target = local_rows(jnp.concatenate([own_quad(quad_target), own_quad(quad_target, 1 - role)])).reshape(1, quad_count)
    ends = jnp.stack([own_rows(edge_src), own_rows(edge_dst)])
    halo_out = atom_embed[halo_send].reshape(peers, -1)

    mine = pl.BlockSpec((tile, half_width), lambda i, r: (r[0] * grid[0] + i, 0))
    mine_rbf = pl.BlockSpec((tile, radial_width), lambda i, r: (r[0] * grid[0] + i, 0))
    emb, pre, table = call(
        down_kernel, "down", grid,
        [mine, rows_of(tile, half_width), mine_rbf, whole(w_rad.shape), whole(w_down.shape)],
        [rows_of(tile, width), rows_of(tile, LANES), columns_of(LANES, tile)],
        [out(half, width), out(half, LANES), out(LANES, half)],
        [pltpu.VMEM(w_rad.shape, bf16)] * 2 + [pltpu.VMEM(w_down.shape, bf16)] * 2,
        (role_arg, edge_embed, emb_recv, edge_rbf, w_rad, w_down), scalars=1, flops=6 * half * 2 * width * (radial_width + LANES),
    )
    table_recv = swap(table)

    bil_rows = w_quad_bil.shape[0]
    z_quad, quad_rows = call(
        functools.partial(quad_forward_kernel, orders=orders, base=trip_width), "quad_forward", (1,),
        [whole(table.shape)] * 2 + [whole(q_index.shape)] * 4 + [whole(w_quad_bil.shape)],
        [whole((bil_rows, half_quad)), whole((half_quad, quad_width))],
        [out(bil_rows, half_quad), out(half_quad, quad_width)],
        [pltpu.VMEM((quad_slots, quad_width, half_quad), f32)] * 2 + [pltpu.VMEM((orders, quad_slots, half_quad), f32)],
        (table, table_recv, q_index, q_cos, q_dih, q_live, w_quad_bil), flops=2 * 10**9,
    )
    sent = jnp.concatenate([quad_rows.reshape(peers, -1), halo_out], axis=1)
    cut = quad_rows.size // peers
    routed = lax.all_to_all(sent, "edge", split_axis=0, concat_axis=0, tiled=True)
    routed_recv = swap(routed)

    bil_rows = w_trip_bil.shape[0]
    z_trip, mid_trip = call(
        functools.partial(triplet_forward_kernel, orders=orders), "triplet_forward", grid,
        [whole(table.shape)] * 2 + [columns_of(slots, tile)] * 3 + [whole(w_trip_bil.shape)],
        [columns_of(bil_rows, tile), rows_of(tile, LANES)],
        [out(bil_rows, half), out(half, LANES)],
        [
            pltpu.VMEM((2 * CLASSES * trip_width, edges // CLASSES), bf16),
            pltpu.VMEM((slots, trip_width, tile), f32),
            pltpu.VMEM((orders, slots, tile), f32),
            pltpu.VMEM(w_trip_bil.shape, bf16),
            pltpu.VMEM(w_trip_bil.shape, bf16),
        ],
        (table, table_recv, t_index, t_cos, t_live, w_trip_bil), flops=10 * 10**9,
    )

    quad_all = jnp.concatenate([routed[:, :cut].reshape(half_quad, quad_width), routed_recv[:, :cut].reshape(half_quad, quad_width)], axis=0)
    quad_all = jnp.pad(quad_all, ((0, 0), (trip_width, pad)))
    halo_own = routed[:, cut:].reshape(halo_count, half_atom)
    halo_recv = routed_recv[:, cut:].reshape(halo_count, half_atom)
    atom_recv = small_recv[:, :half_atom]

    pool_rows = atoms + halo_count
    weights_scratch = [
        pltpu.VMEM((2, *w_up.shape), bf16), pltpu.VMEM((2, width, width), bf16), pltpu.VMEM((2, width, width), bf16),
        pltpu.VMEM((2, width, width), bf16), pltpu.VMEM((2, radial_width, width), bf16),
    ]
    mid, joined, pre_one, pre_two, pre_six, new_own, new_send, coll_own = call(
        main_forward_kernel, "main_forward", grid,
        [rows_of(tile, width), rows_of(tile, LANES), mine_rbf, columns_of(2, tile), whole(target.shape), whole(quad_all.shape),
         whole(atom_embed.shape), whole(atom_recv.shape), whole(halo_own.shape), whole(halo_recv.shape),
         whole(w_up.shape), whole(w_res_one.shape), whole(w_res_two.shape), whole(w_atom_edge.shape), whole(w_edge_rbf.shape)],
        [rows_of(tile, LANES)] + [rows_of(tile, width)] * 4 + [rows_of(tile, half_width)] * 2 + [whole((atoms, width))],
        [out(half, LANES)] + [out(half, width)] * 4 + [out(half, half_width)] * 2 + [out(atoms, width)],
        weights_scratch + [pltpu.VMEM((2, pool_rows + atoms, width), bf16), pltpu.VMEM((quad_count, 2 * LANES), bf16)],
        (role_arg, emb, mid_trip, edge_rbf, ends, target, quad_all, atom_embed, atom_recv, halo_own, halo_recv,
         w_up, w_res_one, w_res_two, w_atom_edge, w_edge_rbf), scalars=1, flops=10 * 10**9,
    )
    coll_recv = swap(coll_own)
    new_recv = swap(new_send)

    early_rows = w_atom_edge.shape[0] + 2 * width + radial_width + w_edge_atom.size // width + w_out.size // width
    (sum_grad, mid_grad, early, quad_back, pool_grad_own, pool_grad_send, atom_out, feat_out, up_grad) = call(
        functools.partial(main_backward_kernel, scale=(atoms / edges) ** 0.5), "main_backward", grid,
        [rows_of(tile, width)] * 4 + [rows_of(tile, LANES), mine_rbf, columns_of(2, tile), whole(target.shape), mine, rows_of(tile, half_width),
         whole(coll_own.shape), whole(coll_own.shape), whole(small_own.shape), whole(small_own.shape), whole(halo_own.shape), whole(halo_own.shape),
         whole(w_up.shape), whole(w_res_one.shape), whole(w_res_two.shape), whole(w_atom_edge.shape), whole(w_edge_rbf.shape),
         whole(w_edge_atom.shape), whole(w_out.shape)],
        [rows_of(tile, width), rows_of(tile, LANES), whole((early_rows, width)), whole((quad_count, LANES)),
         whole((pool_rows, half_atom)), whole((pool_rows, half_atom)), whole((atoms, half_atom)), whole((atoms, half_atom)), whole(w_up.shape)],
        [out(half, width), out(half, LANES), out(early_rows, width), out(quad_count, LANES),
         out(pool_rows, half_atom), out(pool_rows, half_atom), out(atoms, half_atom), out(atoms, half_atom), out(*w_up.shape)],
        weights_scratch + [pltpu.VMEM((2, atoms, width), bf16), pltpu.VMEM((pool_rows + atoms, width), f32), pltpu.VMEM((atoms, 2 * half_atom), f32)],
        (role_arg, joined, pre_one, pre_two, pre_six, mid, edge_rbf, ends, target, cot_edge, cot_recv,
         coll_own, coll_recv, small_own, small_recv, halo_own, halo_recv,
         w_up, w_res_one, w_res_two, w_atom_edge, w_edge_rbf, w_edge_atom, w_out), scalars=1, flops=20 * 10**9,
    )
    back_send = jnp.concatenate([quad_back[half_quad:], pool_grad_send], axis=0)
    back_recv = swap(back_send)
    quad_sum = (quad_back[:half_quad] + back_recv[:half_quad])[:, trip_width : trip_width + quad_width]
    pool_grad = pool_grad_own + back_recv[half_quad:]
    returned = jnp.concatenate([quad_sum.reshape(peers, -1), pool_grad[atoms:].reshape(peers, -1)], axis=1)
    returned = lax.all_to_all(returned, "edge", split_axis=0, concat_axis=0, tiled=True)
    early_sum = reduce_everywhere(early)

    bil_grad, trip_table = call(
        functools.partial(triplet_backward_kernel, orders=orders), "triplet_backward", grid,
        [rows_of(tile, LANES), columns_of(bil_rows, tile)] + [columns_of(slots, tile)] * 3 + [whole(w_trip_bil.shape)],
        [whole((bil_rows, LANES)), whole((trip_width, edges))],
        [out(bil_rows, LANES), out(trip_width, edges)],
        [
            pltpu.VMEM((bil_rows, tile), f32),
            pltpu.VMEM((slots, trip_width, tile), f32),
            pltpu.VMEM((orders, slots, tile), f32),
            pltpu.VMEM((2 * CLASSES * trip_width, edges // CLASSES), f32),
            pltpu.VMEM(w_trip_bil.shape, bf16),
            pltpu.VMEM(w_trip_bil.shape, bf16),
        ],
        (mid_grad, z_trip, t_index, t_cos, t_live, w_trip_bil), flops=10 * 10**9,
    )
    rows_grad = jnp.pad(returned[:, :cut].reshape(half_quad, quad_width), ((0, 0), (trip_width, pad)))
    halo_back = returned[:, cut:].reshape(halo_count, half_atom)
    bil_rows = w_quad_bil.shape[0]
    bil_packed, quad_table = call(
        functools.partial(quad_backward_kernel, orders=orders, base=trip_width), "quad_backward", (1,),
        [whole(rows_grad.shape), whole(z_quad.shape)] + [whole(q_index.shape)] * 4 + [whole(w_quad_bil.shape), whole(bil_grad.shape)],
        [whole((bil_rows // 4, 4 * LANES)), whole((quad_width, edges))],
        [out(bil_rows // 4, 4 * LANES), out(quad_width, edges)],
        [pltpu.VMEM((bil_rows, half_quad), f32), pltpu.VMEM((quad_slots, quad_width, half_quad), f32), pltpu.VMEM((orders, quad_slots, half_quad), f32)],
        (rows_grad, z_quad, q_index, q_cos, q_dih, q_live, w_quad_bil, bil_grad), flops=2 * 10**9,
    )
    tables_recv = swap(jnp.concatenate([trip_table[:, half:], quad_table[:, half:]], axis=0))
    trip_recv, quad_recv = tables_recv[:trip_width], tables_recv[trip_width:]

    grad_own, grad_send, rad_grad, down_grad = call(
        final_kernel, "final", grid,
        [rows_of(tile, width), mine_rbf, rows_of(tile, LANES), columns_of(trip_width, tile), columns_of(trip_width, tile),
         columns_of(quad_width, tile), columns_of(quad_width, tile), rows_of(tile, width), whole(w_rad.shape), whole(w_down.shape)],
        [rows_of(tile, half_width)] * 2 + [whole((2 * radial_width, width)), whole((width // 4, 4 * LANES))],
        [out(half, half_width)] * 2 + [out(2 * radial_width, width), out(width // 4, 4 * LANES)],
        [pltpu.VMEM((2, *w_rad.shape), bf16), pltpu.VMEM((2, *w_down.shape), bf16), pltpu.VMEM((2 * width, LANES), f32)],
        (role_arg, emb, edge_rbf, pre, trip_table, trip_recv, quad_table, quad_recv, sum_grad, w_rad, w_down), scalars=1,
        flops=6 * half * 2 * width * (2 * radial_width + 2 * LANES),
    )
    grad_recv = swap(grad_send)
    late = jnp.concatenate([rad_grad, down_grad, bil_packed, up_grad], axis=0)
    late_sum = reduce_everywhere(late)

    def both_halves(own, recv):
        return jnp.where(role == 0, jnp.concatenate([own, recv], axis=0), jnp.concatenate([recv, own], axis=0))

    grad_atom = pool_grad[:atoms] + jnp.zeros((atoms, half_atom), f32).at[halo_send].add(halo_back)

    at = 0
    pieces = []
    for rows in (w_atom_edge.shape[0], width, width, radial_width, w_edge_atom.size // width, w_out.size // width):
        pieces.append(early_sum[at : at + rows])
        at += rows
    g_atom_edge, g_two, g_one, g_edge_rbf, g_ea, g_out = pieces
    atom_width = 2 * half_atom

    def unpack(x, columns):
        return jnp.concatenate([x[:, q * columns : (q + 1) * columns] for q in range(x.shape[1] // columns)], axis=0)

    g_ea, g_out = unpack(g_ea, atom_width), unpack(g_out, atom_width)
    at = 2 * radial_width
    g_trip_rbf, g_quad_rbf = late_sum[:radial_width], late_sum[radial_width:at]
    g_down = unpack(late_sum[at : at + width // 4], LANES)
    at += width // 4
    g_bil = unpack(late_sum[at : at + bil_rows // 4], LANES)
    at += bil_rows // 4
    g_up = late_sum[at:]
    narrow = slice(trip_width, trip_width + quad_width)
    return (
        both_halves(new_own, new_recv), atom_out, feat_out, both_halves(grad_own, grad_recv), grad_atom,
        g_quad_rbf, g_down[:, narrow], g_bil[:, narrow], g_up[narrow],
        g_trip_rbf, g_down[:, :trip_width], g_bil[:, :trip_width], g_up[:trip_width],
        g_one, g_two, g_atom_edge, g_edge_rbf, g_ea, g_out,
    )


def solution(mesh):
    whole_spec, rows_spec, both_spec = P(), P("edge"), P("edge", "pair")
    in_specs = (both_spec, both_spec) + (rows_spec,) * 12 + (whole_spec,) * 14 + (both_spec,) * 3
    out_specs = (both_spec,) * 5 + (whole_spec,) * 14
    return jax.shard_map(local, mesh=mesh, in_specs=in_specs, out_specs=out_specs, check_vma=False)
```

```python
import functools

import jax
import jax.numpy as jnp
from jax import lax
from jax.experimental import pallas as pl
from jax.experimental.pallas import tpu as pltpu
from jax.sharding import PartitionSpec as P

f32, bf16, i32 = jnp.float32, jnp.bfloat16, jnp.int32
root_third = 0.5773502691896258
root_half = 0.7071067811865476
LANES = 128
CLASSES = 4
VMEM_LIMIT = 56 * 2**20


def split(x):
    high = x.astype(bf16)
    return high, (x - high.astype(f32)).astype(bf16)


def dot(left, right, dims):
    return lax.dot_general(left, right, (dims, ((), ())), preferred_element_type=f32)


NN = ((1,), (0,))
NT = ((1,), (1,))
TN = ((0,), (0,))


def dot3(left, right, dims=NN):
    lh, ll = left if isinstance(left, tuple) else split(left)
    rh, rl = right if isinstance(right, tuple) else split(right)
    return dot(lh, rh, dims) + dot(lh, rl, dims) + dot(ll, rh, dims)


def pick(onehot, right, dims=NN):
    rh, rl = right if isinstance(right, tuple) else split(right)
    return dot(onehot, rh, dims) + dot(onehot, rl, dims)


def sigmoid(v):
    return 0.5 * jnp.tanh(0.5 * v) + 0.5


def silu(v):
    return v * sigmoid(v)


def silu_grad(v):
    s = sigmoid(v)
    return s * (1.0 + v * (1.0 - s))


def as_bf16(mask):
    return mask.astype(f32).astype(bf16)


def legendre_steps(cosine, orders):
    before, now = jnp.ones_like(cosine), cosine
    yield before
    yield now
    for order in range(1, orders - 1):
        before, now = now, ((2 * order + 1) / (order + 1)) * cosine * now - (order / (order + 1)) * before
        yield now


def class_table(own, other, classes):
    per = classes // 2
    step = own.shape[1] // per
    parts = []
    for block in (own, other):
        high, low = split(block)
        for q in range(per):
            parts += [high[:, q * step : (q + 1) * step], low[:, q * step : (q + 1) * step]]
    return jnp.concatenate(parts, axis=0)


def gather_classes(table, index, classes, width):
    step = table.shape[1]
    shift = step.bit_length() - 1
    slots = index.shape[1]
    onehot = as_bf16(lax.broadcasted_iota(i32, (step, slots), 0) == (index & (step - 1)))
    found = dot(table, onehot, NN)
    kind = index >> shift
    out = found[0:width] + found[width : 2 * width]
    for q in range(1, classes):
        base = q * 2 * width
        out = jnp.where(kind >= q, found[base : base + width] + found[base + width : base + 2 * width], out)
    return out


def scatter_classes(values, indices, classes, step):
    shift = step.bit_length() - 1
    lefts, rights = [], []
    for value, index in zip(values, indices):
        width, slots = value.shape
        high, low = split(value)
        both = jnp.concatenate([high, low], axis=0)
        kind = jnp.broadcast_to(index >> shift, (2 * width, slots))
        lefts.append(jnp.concatenate([jnp.where(kind == q, both, jnp.zeros((), bf16)) for q in range(classes)], axis=0))
        rights.append(as_bf16(lax.broadcasted_iota(i32, (step, slots), 0) == (index & (step - 1))))
    return dot(jnp.concatenate(lefts, axis=1), jnp.concatenate(rights, axis=1), NT)


def unfold_classes(sums, classes, width):
    parts = []
    for q in range(classes):
        base = q * 2 * width
        parts.append(sums[base : base + width] + sums[base + width : base + 2 * width])
    return jnp.concatenate(parts, axis=1)


def joined_halves(zero, mine, theirs, axis=1):
    return jnp.concatenate([jnp.where(zero, mine, theirs), jnp.where(zero, theirs, mine)], axis=axis)


def down_kernel(role, own, recv, rbf, w_trip_rad, w_quad_rad, w_trip, w_quad, emb_out, pre_out, table_out, rad, down_t, down_q):
    width = w_trip_rad.shape[1]

    @pl.when(pl.program_id(0) == 0)
    def _():
        rad[0, :, :width], rad[1, :, :width] = split(w_trip_rad[...])
        rad[0, :, width:], rad[1, :, width:] = split(w_quad_rad[...])
        down_t[0], down_t[1] = split(w_trip[...])
        down_q[0], down_q[1] = split(w_quad[...])

    emb = joined_halves(role[0] == 0, own[...], recv[...])
    emb_out[...] = emb
    radial = dot3(rbf[...], (rad[0], rad[1]))
    pre = jnp.concatenate(
        [
            dot3((down_t[0], down_t[1]), emb * radial[:, :width], NT),
            dot3((down_q[0], down_q[1]), emb * radial[:, width:], NT),
        ],
        axis=0,
    )
    pre_out[...] = pre
    table_out[...] = silu(pre)


def quad_forward_kernel(role, own, other, index, cosine, dihedral, live, w_bil, z_out, rows_out, sel, sel2, basis, *, orders, base):
    slots_k, rows = index.shape
    width = w_bil.shape[0]
    zero = role[0] == 0
    mine, theirs = own[base : base + width, :], other[base : base + width, :]
    table = class_table(jnp.where(zero, mine, theirs), jnp.where(zero, theirs, mine), 2 * CLASSES)
    alive = live[...].astype(f32)
    for order, series in enumerate(legendre_steps(cosine[...], orders)):
        basis[order] = series * alive
    for k in range(slots_k):
        picked = gather_classes(table, index[k : k + 1, :], 2 * CLASSES, width)
        sel[k] = picked
        sel2[k] = picked * dihedral[k : k + 1, :]
    groups = width // 8
    for t in range(rows // LANES):
        at = slice(t * LANES, (t + 1) * LANES)
        for part, source in enumerate((sel, sel2)):
            for order_at in range(0, orders, 8):
                sums = {}
                for k in range(slots_k):
                    chosen = [source[k, g * 8 : g * 8 + 8, at] for g in range(groups)]
                    for order in range(8):
                        weight = jnp.broadcast_to(basis[order_at + order, k : k + 1, at], (8, LANES))
                        for g in range(groups):
                            term = weight * chosen[g]
                            sums[order, g] = term if k == 0 else sums[order, g] + term
                for (order, g), total in sums.items():
                    row = (part * orders + order_at + order) * width + g * 8
                    z_out[row : row + 8, at] = total
    rows_out[...] = dot3(w_bil[...], z_out[...])


def triplet_forward_kernel(role, own, other, index, cosine, live, w_bil, z_out, mid_out, table, sel, basis, bil, *, orders):
    slots_k, tile = index.shape
    width = w_bil.shape[0]

    @pl.when(pl.program_id(0) == 0)
    def _():
        zero = role[0] == 0
        mine, theirs = own[0:width, :], other[0:width, :]
        table[...] = class_table(jnp.where(zero, mine, theirs), jnp.where(zero, theirs, mine), CLASSES)
        bil[0], bil[1] = split(w_bil[...])

    alive = live[...].astype(f32)
    for order, series in enumerate(legendre_steps(cosine[...], orders)):
        basis[order] = series * alive

    def gather(at, k, into):
        where_to = jnp.concatenate([index[k : k + 1, at], index[k + 1 : k + 2, at]], axis=1)
        found = gather_classes(table[...], where_to, CLASSES, width)
        sel[into, k] = found[:, :LANES]
        sel[into, k + 1] = found[:, LANES:]

    def combine(at, first, source):
        sums = {}
        for k in range(slots_k):
            chosen = [sel[source, k, g * 8 : g * 8 + 8, :] for g in (first, first + 1)]
            for order in range(orders):
                weight = jnp.broadcast_to(basis[order, k : k + 1, at], (8, LANES))
                for g in range(2):
                    term = weight * chosen[g]
                    sums[order, g] = term if k == 0 else sums[order, g] + term
        for (order, g), total in sums.items():
            row = order * width + (first + g) * 8
            z_out[row : row + 8, at] = total

    firsts = range(0, width // 8, 2)
    turns = slots_k // 2 // len(firsts)
    columns = lambda c: pl.ds(pl.multiple_of(c * LANES, LANES), LANES)
    for k in range(0, slots_k, 2):
        gather(columns(0), k, 0)

    def step_columns(c, carry):
        for n, first in enumerate(firsts):
            for k in range(n * turns, (n + 1) * turns):
                gather(columns(c), 2 * k, c & 1)
            combine(columns(c - 1), first, 1 - (c & 1))
        return carry

    lax.fori_loop(1, tile // LANES, step_columns, 0)
    for first in firsts:
        combine(columns(tile // LANES - 1), first, (tile // LANES - 1) & 1)
    mid_out[...] = dot3((bil[0], bil[1]), z_out[...])


def edge_members(ends, pool_rows, atoms, tile):
    row = lax.broadcasted_iota(i32, (pool_rows + atoms, tile), 0)
    return as_bf16(row == jnp.where(row < pool_rows, ends[0:1, :], ends[1:2, :] + pool_rows))


def entry_members(role, target, step, tile, half):
    row = lax.broadcasted_iota(i32, (tile, target.shape[1]), 0) + (step * tile + role[0] * half)
    return as_bf16(row == target[...])


def main_forward_kernel(
    role, emb, mid_one, mid_two, rbf, ends, target, quad_own, quad_recv, atom_own, atom_recv, halo_own, halo_recv,
    w_trip_up, w_quad_up, w_one, w_two, w_edge, w_rbf,
    mid_out, joined_out, one_out, two_out, six_out, new_own, new_send, collected,
    up, one, two, three, rad, pool_w, quad_hl,
):
    step = pl.program_id(0)
    tile = emb.shape[0]
    half_rows = tile * pl.num_programs(0)
    atoms = atom_own.shape[0]
    pool_rows = atoms + halo_own.shape[0]
    atom_width = 2 * atom_own.shape[1]
    trip_width = w_trip_up.shape[0]
    zero = role[0] == 0

    @pl.when(step == 0)
    def _():
        up[0, :trip_width], up[1, :trip_width] = split(w_trip_up[...])
        up[0, trip_width:], up[1, trip_width:] = split(w_quad_up[...])
        one[0], one[1] = split(w_one[...])
        two[0], two[1] = split(w_two[...])
        three[0], three[1] = split(w_edge[2 * atom_width :, :])
        rad[0], rad[1] = split(w_rbf[...])
        atom_rows = joined_halves(zero, atom_own[...], atom_recv[...])
        pool = jnp.concatenate([atom_rows, joined_halves(zero, halo_own[...], halo_recv[...])], axis=0)
        projected = jnp.concatenate(
            [dot3(pool, w_edge[0:atom_width, :]), dot3(atom_rows, w_edge[atom_width : 2 * atom_width, :])], axis=0
        )
        pool_w[0], pool_w[1] = split(projected)
        high, low = split(quad_own[...] + quad_recv[...])
        quad_hl[...] = jnp.concatenate([high, low], axis=0)

    found = dot(quad_hl[...], entry_members(role, target, step, tile, half_rows), NT)
    width = found.shape[0] // 2
    mid_trip = jnp.where(step < pl.num_programs(0) // 2, mid_one[...], mid_two[...])
    mid = jnp.concatenate([mid_trip, found[:width] + found[width:]], axis=0)
    mid_out[...] = mid
    joined = (emb[...] + dot3(mid, (up[0], up[1]), TN)) * root_third
    joined_out[...] = joined
    pre_one = dot3(joined, (one[0], one[1]))
    one_out[...] = pre_one
    pre_two = dot3(silu(pre_one), (two[0], two[1]))
    two_out[...] = pre_two
    residual = (joined + silu(pre_two)) * root_half
    member = edge_members(ends, pool_rows, atoms, tile)
    pre_six = pick(member, (pool_w[0], pool_w[1]), TN) + dot3(residual, (three[0], three[1]))
    six_out[...] = pre_six
    edge_new = (residual + silu(pre_six)) * root_half
    half = edge_new.shape[1] // 2
    new_own[...] = jnp.where(zero, edge_new[:, :half], edge_new[:, half:])
    new_send[...] = jnp.where(zero, edge_new[:, half:], edge_new[:, :half])
    weighted = edge_new * dot3(rbf[...], (rad[0], rad[1]))
    part = pick(member[pool_rows:, :], weighted)

    @pl.when(step == 0)
    def _():
        collected[...] = part

    @pl.when(step > 0)
    def _():
        collected[...] += part


def give_halves(place_at, total, keep, send, codes):
    half = keep.shape[0]
    rows = half // len(codes)
    for side, target in ((place_at[0], keep), (1 - place_at[0], send)):
        for n, code in enumerate(codes):
            at = pl.multiple_of(side * half + (place_at[1] ^ code) * rows, 8)
            target[n * rows : (n + 1) * rows, :] = total[pl.ds(at, rows), :]


def side_by_side(x, width):
    parts = width // x.shape[1]
    rows = x.shape[0] // parts
    return jnp.concatenate([x[q * rows : (q + 1) * rows] for q in range(parts)], axis=1)


def edge_backward_kernel(
    role, joined, pre_two_ref, pre_six_ref, rbf, ends, cot_own, cot_recv,
    coll_own, coll_recv, small_own, small_recv, halo_own, halo_recv,
    w_edge, w_rbf, w_edge_atom, w_out,
    res_grad_out, keep, send, pool_grad_own, pool_grad_send, atom_out, feat_out,
    three, rad, coll_grad, pool_sum, direct, grads,
    *, scale, codes,
):
    step = pl.program_id(0)
    last = pl.num_programs(0) - 1
    tile, edge_width = joined.shape
    half = small_own.shape[1]
    atoms = small_own.shape[0] // 3
    atom_width = 2 * half
    pool_rows = atoms + halo_own.shape[0]
    zero = role[0] == 0
    at_rbf = w_edge.shape[0]
    at_atom = at_rbf + w_rbf.shape[0]
    at_last = at_atom + w_edge_atom.shape[0] * atom_width // edge_width
    at_end = at_last + atom_width * atom_width // edge_width

    @pl.when(step == 0)
    def _():
        three[0], three[1] = split(w_edge[2 * atom_width :, :])
        rad[0], rad[1] = split(w_rbf[...])
        mine, theirs = small_own[...], small_recv[...]
        atom_rows = joined_halves(zero, mine[:atoms], theirs[:atoms])
        cot_atom = joined_halves(zero, mine[atoms : 2 * atoms], theirs[atoms : 2 * atoms])
        cot_feat = joined_halves(zero, mine[2 * atoms :], theirs[2 * atoms :])
        total = (coll_own[...] + coll_recv[...]) * scale
        w_a, w_f = split(w_edge_atom[...]), split(w_out[...])
        pre_atom = dot3(total, w_a)
        atom_new = (atom_rows + silu(pre_atom)) * root_half
        pre_feat = dot3(atom_new, w_f)
        feature = silu(pre_feat)
        atom_out[...] = jnp.where(zero, atom_new[:, :half], atom_new[:, half:])
        feat_out[...] = jnp.where(zero, feature[:, :half], feature[:, half:])
        feat_grad = cot_feat * silu_grad(pre_feat)
        grads[at_last:at_end, :] = side_by_side(0.5 * dot3(atom_new, feat_grad, TN), edge_width)
        atom_grad = (cot_atom + dot3(feat_grad, w_f, NT)) * root_half
        direct[...] = 0.5 * atom_grad
        pre_grad = atom_grad * silu_grad(pre_atom)
        grads[at_atom:at_last, :] = side_by_side(0.5 * dot3(total, pre_grad, TN), edge_width)
        coll_grad[0], coll_grad[1] = split(dot3(pre_grad, w_a, NT) * scale)
        grads[0:at_atom, :] = jnp.zeros((at_atom, grads.shape[1]), f32)
        if grads.shape[0] > at_end:
            grads[at_end:, :] = jnp.zeros((grads.shape[0] - at_end, grads.shape[1]), f32)
        pool_sum[...] = jnp.zeros_like(pool_sum)

    member = edge_members(ends, pool_rows, atoms, tile)
    pre_two, pre_six = pre_two_ref[...], pre_six_ref[...]
    s_six = sigmoid(pre_six)
    residual = (joined[...] + silu(pre_two)) * root_half
    edge_new = (residual + pre_six * s_six) * root_half
    radial_split = split(rbf[...])
    weighted_grad = pick(member[pool_rows:, :], (coll_grad[0], coll_grad[1]), TN)
    grads[at_rbf:at_atom, :] += dot3(radial_split, weighted_grad * edge_new, TN)
    new_grad = joined_halves(zero, cot_own[...], cot_recv[...])
    new_grad = (new_grad + weighted_grad * dot3(radial_split, (rad[0], rad[1]))) * root_half
    six_split = split(new_grad * (s_six * (1.0 + pre_six * (1.0 - s_six))))
    pool_sum[...] += pick(member, six_split)
    grads[2 * atom_width : at_rbf, :] += dot3(residual, six_split, TN)
    res_grad_out[...] = (new_grad + dot3(six_split, (three[0], three[1]), NT)) * root_half

    @pl.when(step == last)
    def _():
        atom_rows = joined_halves(zero, small_own[:atoms, :], small_recv[:atoms, :])
        pool = jnp.concatenate([atom_rows, joined_halves(zero, halo_own[...], halo_recv[...])], axis=0)
        w_src, w_dst = split(w_edge[0:atom_width, :]), split(w_edge[atom_width : 2 * atom_width, :])
        src_split, dst_split = split(pool_sum[0:pool_rows, :]), split(pool_sum[pool_rows:, :])
        grads[0:atom_width, :] = dot3(pool, src_split, TN)
        grads[atom_width : 2 * atom_width, :] = dot3(atom_rows, dst_split, TN)
        from_src = dot3(src_split, w_src, NT)
        from_atoms = from_src[0:atoms] + dot3(dst_split, w_dst, NT) + direct[...]
        result = jnp.concatenate([from_atoms, from_src[atoms:]], axis=0)
        pool_grad_own[...] = jnp.where(zero, result[:, :half], result[:, half:])
        pool_grad_send[...] = jnp.where(zero, result[:, half:], result[:, :half])
        give_halves(role, grads, keep, send, codes)


def residual_backward_kernel(
    role, joined, pre_one_ref, pre_two_ref, mid_ref, z_one, z_two, target, res_grad_ref,
    w_trip_up, w_quad_up, w_one, w_two,
    sum_grad_out, mid_grad_out, keep, send, back,
    up, one, two, grads, bil_grad,
    *, codes,
):
    step = pl.program_id(0)
    tile, width = joined.shape
    half_rows = tile * pl.num_programs(0)
    trip_width = w_trip_up.shape[0]
    narrow = up.shape[1]
    at_bil = 2 * width + narrow

    @pl.when(step == 0)
    def _():
        up[0, :trip_width], up[1, :trip_width] = split(w_trip_up[...])
        up[0, trip_width:], up[1, trip_width:] = split(w_quad_up[...])
        one[0], one[1] = split(w_one[...])
        two[0], two[1] = split(w_two[...])
        grads[...] = jnp.zeros_like(grads)
        bil_grad[...] = jnp.zeros_like(bil_grad)
        back[...] = jnp.zeros_like(back)

    blocks = [slice(n * tile // 2, (n + 1) * tile // 2) for n in range(2)]

    def laid(pairs):
        return tuple(jnp.concatenate([p[n] for p in pairs], axis=0) for n in range(2))

    res_grad = [res_grad_ref[at, :] for at in blocks]
    two_split = [split(grad * silu_grad(pre_two_ref[at, :])) for grad, at in zip(res_grad, blocks)]
    pre_one = [pre_one_ref[at, :] for at in blocks]
    s_one = [sigmoid(pre) for pre in pre_one]
    hidden = [split(pre * s) for pre, s in zip(pre_one, s_one)]
    one_split = [
        split(dot3(grad, (two[0], two[1]), NT) * (s * (1.0 + pre * (1.0 - s)))) for grad, pre, s in zip(two_split, pre_one, s_one)
    ]
    grads[0:width, :] += dot3(laid(hidden), laid(two_split), TN)
    sum_grad = [(grad + dot3(inner, (one[0], one[1]), NT)) * root_third for grad, inner in zip(res_grad, one_split)]
    grads[width : 2 * width, :] += dot3(joined[...], laid(one_split), TN)
    for at, grad in zip(blocks, sum_grad):
        sum_grad_out[at, :] = grad
    sum_split = laid([split(grad) for grad in sum_grad])
    grads[2 * width : at_bil, :] += dot3(mid_ref[...], sum_split, NN)
    mid_grad = dot3((up[0], up[1]), sum_split, NT)
    mid_grad_out[...] = mid_grad
    mid_high, mid_low = split(mid_grad)
    z = jnp.where(step < pl.num_programs(0) // 2, z_one[...], z_two[...])
    bil_grad[...] += dot3((mid_high[:trip_width], mid_low[:trip_width]), z, NT)
    found = dot(jnp.concatenate([mid_high[trip_width:], mid_low[trip_width:]], axis=0), entry_members(role, target, step, tile, half_rows), NN)
    rows = narrow - trip_width
    back[...] += found[:rows] + found[rows:]

    @pl.when(step == pl.num_programs(0) - 1)
    def _():
        for q in range(bil_grad.shape[1] // width):
            grads[at_bil + q * trip_width : at_bil + (q + 1) * trip_width, :] = bil_grad[:, q * width : (q + 1) * width]
        give_halves(role, grads, keep, send, codes)


def triplet_backward_kernel(role, mid_grad, index, cosine, live, w_bil, *refs, orders):
    held, (sums, zg, sg, basis, bil) = refs[:-5], refs[-5:]
    step = pl.program_id(0)
    slots_k, tile = index.shape
    width = w_bil.shape[0]
    classes_step = sums.shape[1]

    @pl.when(step == 0)
    def _():
        bil[0], bil[1] = split(w_bil[...])
        sums[...] = held[0][...] if held else jnp.zeros_like(sums)

    alive = live[...].astype(f32)
    for order, series in enumerate(legendre_steps(cosine[...], orders)):
        basis[order] = series * alive
    grad_split = split(mid_grad[0:width, :])
    zg[...] = dot3((bil[0], bil[1]), grad_split, TN)

    def combine(at, first, into):
        totals = {}
        for order in range(orders):
            row = order * width + first * 8
            got = [zg[row + g * 8 : row + g * 8 + 8, at] for g in range(2)]
            for k in range(slots_k):
                weight = jnp.broadcast_to(basis[order, k : k + 1, at], (8, LANES))
                for g in range(2):
                    term = weight * got[g]
                    totals[k, g] = term if order == 0 else totals[k, g] + term
        for (k, g), total in totals.items():
            sg[into, k, (first + g) * 8 : (first + g) * 8 + 8, :] = total

    def scatter(at, first, source):
        slots_at = range(first, first + slots_k // 2)
        sums[...] += scatter_classes(
            [sg[source, k] for k in slots_at], [index[k : k + 1, at] for k in slots_at], CLASSES, classes_step
        )

    firsts = range(0, width // 8, 2)
    columns = lambda c: pl.ds(pl.multiple_of(c * LANES, LANES), LANES)
    for first in firsts:
        combine(columns(0), first, 0)

    def step_columns(c, carry):
        for n, first in enumerate(firsts):
            if n % 2 == 0:
                scatter(columns(c - 1), n // 2 * (slots_k // 2), 1 - (c & 1))
            combine(columns(c), first, c & 1)
        return carry

    lax.fori_loop(1, tile // LANES, step_columns, 0)
    for n in range(2):
        scatter(columns(tile // LANES - 1), n * (slots_k // 2), (tile // LANES - 1) & 1)


def quad_backward_kernel(role, own, z, index, cosine, dihedral, live, w_bil, trip_sums, bil_grad, keep, send, zg, sg, basis, *, orders):
    slots_k, rows = index.shape
    width = w_bil.shape[0]
    edges = trip_sums.shape[1] * CLASSES
    trip_width = trip_sums.shape[0] // (2 * CLASSES)
    zero = role[0] == 0
    alive = live[...].astype(f32)
    for order, series in enumerate(legendre_steps(cosine[...], orders)):
        basis[order] = series * alive
    grad_split = split(own[...])
    bil_grad[...] = dot3(grad_split, z[...], NT)
    zg[...] = dot3(w_bil[...], grad_split, TN)
    groups = width // 8
    for t in range(rows // LANES):
        at = slice(t * LANES, (t + 1) * LANES)
        for g in range(groups):
            plain, turned = {}, {}
            for order in range(orders):
                one = zg[order * width + g * 8 : order * width + g * 8 + 8, at]
                two = zg[(orders + order) * width + g * 8 : (orders + order) * width + g * 8 + 8, at]
                for k in range(slots_k):
                    weight = jnp.broadcast_to(basis[order, k : k + 1, at], (8, LANES))
                    plain[k] = weight * one if order == 0 else plain[k] + weight * one
                    turned[k] = weight * two if order == 0 else turned[k] + weight * two
            for k in range(slots_k):
                sg[k, g * 8 : g * 8 + 8, at] = plain[k] + turned[k] * jnp.broadcast_to(dihedral[k : k + 1, at], (8, LANES))
    step = edges // (2 * CLASSES)
    sums = scatter_classes([sg[k] for k in range(slots_k)], [index[k : k + 1, :] for k in range(slots_k)], 2 * CLASSES, step)
    total = jnp.concatenate([unfold_classes(trip_sums[...], CLASSES, trip_width), unfold_classes(sums, 2 * CLASSES, width)], axis=0)
    half = edges // 2
    keep[...] = jnp.where(zero, total[:, :half], total[:, half:])
    send[...] = jnp.where(zero, total[:, half:], total[:, :half])


def final_kernel(
    role, emb_ref, rbf, pre_ref, table_own, table_recv, sum_grad, quad_bil, w_trip_rad, w_quad_rad, w_trip, w_quad,
    grad_own, grad_send, keep, send,
    rad, down_t, down_q, total,
    *, codes,
):
    step = pl.program_id(0)
    zero = role[0] == 0
    radial_rows, width = w_trip_rad.shape
    trip_width, quad_width = w_trip.shape[0], w_quad.shape[0]
    at_quad_rad = radial_rows
    at_trip = 2 * radial_rows
    at_quad = at_trip + trip_width
    at_quad_bil = at_quad + quad_width
    at_end = at_quad_bil + quad_width * quad_bil.shape[1] // width

    @pl.when(step == 0)
    def _():
        rad[0, :, :width], rad[1, :, :width] = split(w_trip_rad[...])
        rad[0, :, width:], rad[1, :, width:] = split(w_quad_rad[...])
        down_t[0], down_t[1] = split(w_trip[...])
        down_q[0], down_q[1] = split(w_quad[...])
        total[...] = jnp.zeros_like(total)
        rows = quad_bil.shape[0]
        for q in range(quad_bil.shape[1] // width):
            total[at_quad_bil + q * rows : at_quad_bil + (q + 1) * rows, :] = quad_bil[:, q * width : (q + 1) * width]

    emb = emb_ref[...]
    radial_split = split(rbf[...])
    radial = dot3(radial_split, (rad[0], rad[1]))
    pre_grad = (table_own[...] + table_recv[...]) * silu_grad(pre_ref[...])
    trip_split, quad_split = split(pre_grad[:trip_width]), split(pre_grad[trip_width:])
    trip_radial, quad_radial = radial[:, :width], radial[:, width:]
    total[at_trip:at_quad, :] += dot3(trip_split, emb * trip_radial)
    total[at_quad:at_quad_bil, :] += dot3(quad_split, emb * quad_radial)
    trip_mixed = dot3(trip_split, (down_t[0], down_t[1]), TN)
    quad_mixed = dot3(quad_split, (down_q[0], down_q[1]), TN)
    grad = sum_grad[...] + trip_mixed * trip_radial + quad_mixed * quad_radial
    half = width // 2
    grad_own[...] = jnp.where(zero, grad[:, :half], grad[:, half:])
    grad_send[...] = jnp.where(zero, grad[:, half:], grad[:, :half])
    total[0:at_quad_rad, :] += dot3(radial_split, trip_mixed * emb, TN)
    total[at_quad_rad:at_trip, :] += dot3(radial_split, quad_mixed * emb, TN)

    @pl.when(step == pl.num_programs(0) - 1)
    def _():
        give_halves(role, total, keep, send, codes)


def fold_kernel(source, target):
    target[...] = jnp.sum(source[...], axis=0)


def fold(blocks, name, after=()):
    return call(fold_kernel, name, (1,), [whole(blocks.shape)], [whole(blocks.shape[1:])], [out(*blocks.shape[1:])], [], (blocks,), after=after)[0]


def exchange(blocks):
    return lax.all_to_all(blocks, "edge", split_axis=0, concat_axis=0, tiled=True)


def scatter_blocks(rows):
    return exchange(rows.reshape(lax.axis_size("edge"), -1, rows.shape[1]))


def partners(bits, axis="edge"):
    return [(i, i ^ bits) for i in range(lax.axis_size(axis))]


def edge_stages():
    size, shift, stages = lax.axis_size("edge"), 0, []
    while size > 1:
        radix = 8 if size == 8 else 4 if size % 4 == 0 else 2
        stages.append((shift, radix))
        shift += radix.bit_length() - 1
        size //= radix
    return stages


def padded_rows(rows):
    unit = 2 * 8 * lax.axis_size("edge")
    return -(-rows // unit) * unit


def spread(piece, codes, stage):
    shift, radix = stage
    pieces = [piece] + [lax.ppermute(piece, "edge", partners(j << shift)) for j in range(1, radix)]
    return pieces, [[c ^ (j << shift) for c in codes] for j in range(radix)]


def stage_codes(stages):
    codes = [0]
    for shift, radix in reversed(stages):
        codes = [c ^ (j << shift) for j in range(radix) for c in codes]
    return codes


def phase_kernel(*refs, jobs):
    ins, outs = list(refs[: sum(count for _, count, _ in jobs)]), list(refs[sum(count for _, count, _ in jobs) :])
    for kind, count, blocks in jobs:
        parts, ins = ins[:count], ins[count:]
        targets, outs = outs[:blocks], outs[blocks:]
        if kind == "join":
            rows = parts[0].shape[0]
            for n, part in enumerate(parts):
                targets[0][n * rows : (n + 1) * rows, :] = part[...]
        else:
            rows = parts[0].shape[0] // blocks
            for n, target in enumerate(targets):
                total = parts[0][n * rows : (n + 1) * rows, :]
                for part in parts[1:]:
                    total = total + part[n * rows : (n + 1) * rows, :]
                target[...] = total


def phase(jobs, name, after=()):
    ins, shapes = [], []
    for kind, parts, blocks in jobs:
        rows, width = parts[0].shape
        ins += parts
        shapes += [(len(parts) * rows, width)] if kind == "join" else [(rows // blocks, width)] * blocks
    got = call(
        functools.partial(phase_kernel, jobs=[(kind, len(parts), blocks) for kind, parts, blocks in jobs]), name, (1,),
        [whole(x.shape) for x in ins], [whole(x) for x in shapes], [out(*x) for x in shapes], [], tuple(ins), after=after,
    )
    results = []
    for _, _, blocks in jobs:
        results.append(got[:blocks])
        got = got[blocks:]
    return results


def send_blocks(blocks, stage):
    shift, radix = stage
    return [blocks[0]] + [lax.ppermute(blocks[j], "edge", partners(j << shift)) for j in range(1, radix)]


def middle_stages(parts, stages, name):
    for at, stage in enumerate(stages):
        parts = send_blocks(phase([("add", parts, stage[1])], f"{name}{at}")[0], stage)
    return parts


def middle_gathers(piece, stages, name):
    codes = [0]
    for at, stage in enumerate(reversed(stages)):
        pieces, lists = spread(piece, codes, stage)
        piece, codes = phase([("join", pieces, 1)], f"{name}{at}")[0][0], sum(lists, [])
    return piece, codes


def unpack_kernel(place_at, *refs, count, codes, layout):
    ins, outs, total = refs[:count], refs[count:-1], refs[-1]
    half = total.shape[0] // 2
    for n, source in enumerate(ins):
        side, listed = codes[n]
        first = jnp.where(place_at[0] == 0, side, 1 - side) * half
        rows = source.shape[0] // len(listed)
        for at, code in enumerate(listed):
            block = place_at[1] ^ code
            total[pl.ds(pl.multiple_of(first + block * rows, 8), rows), :] = source[at * rows : (at + 1) * rows, :]
    at = 0
    for target, kind in zip(outs, layout):
        height, breadth = target.shape
        width = total.shape[1]
        if kind == "plain":
            target[...] = total[at : at + height, :]
            at += height
        elif kind == "rows":
            parts = width // breadth
            rows = height // parts
            for q in range(parts):
                target[q * rows : (q + 1) * rows, :] = total[at : at + rows, q * breadth : (q + 1) * breadth]
            at += rows
        else:
            for q in range(breadth // width):
                target[:, q * width : (q + 1) * width] = total[at : at + height, :]
                at += height


def unpack(pieces, codes, place_at, shapes, layout, name, after=()):
    count = 2 * len(pieces)
    pieces = pieces + [swap(p) for p in pieces]
    codes = [(0, c) for c in codes] + [(1, c) for c in codes]
    rows = sum(p.shape[0] for p in pieces)
    return call(
        functools.partial(unpack_kernel, count=count, codes=codes, layout=layout), name, (1,), [whole(p.shape) for p in pieces],
        [whole(s) for s in shapes], [out(*s) for s in shapes], [pltpu.VMEM((rows, pieces[0].shape[1]), f32)], (place_at, *pieces), scalars=1, after=after,
    )


def whole(shape):
    return pl.BlockSpec(shape, lambda *_: (0,) * len(shape))


def rows_of(tile, width):
    return pl.BlockSpec((tile, width), lambda i, *_: (i, 0))


def columns_of(rows, tile):
    return pl.BlockSpec((rows, tile), lambda i, *_: (0, i))


def out(*shape):
    return jax.ShapeDtypeStruct(shape, f32)


def call(body, name, grid, in_specs, out_specs, out_shape, scratch, args, scalars=0, flops=0, after=(), aliases={}):
    first, count = len(args), len(after)

    def run(*refs):
        body(*refs[:first], *refs[first + count :])

    args = (*args, *after)
    in_specs = in_specs + [pl.BlockSpec(memory_space=pl.ANY)] * count
    return pl.pallas_call(
        run,
        name=name,
        grid_spec=pltpu.PrefetchScalarGridSpec(
            num_scalar_prefetch=scalars, grid=grid, in_specs=in_specs, out_specs=out_specs, scratch_shapes=scratch
        ),
        out_shape=out_shape,
        compiler_params=pltpu.CompilerParams(vmem_limit_bytes=VMEM_LIMIT, dimension_semantics=("arbitrary",) * len(grid)),
        cost_estimate=pl.CostEstimate(flops=max(flops, 1000), bytes_accessed=1000, transcendentals=0),
        input_output_aliases=aliases,
    )(*args)


def swap(x):
    return lax.ppermute(x, "pair", [(0, 1), (1, 0)])


def local(
    edge_embed, atom_embed, edge_rbf, edge_src, edge_dst, halo_send, trip_index, trip_cos, trip_live,
    quad_index, quad_cos, quad_dih, quad_live, quad_target,
    w_quad_rbf, w_quad_down, w_quad_bil, w_quad_up, w_trip_rbf, w_trip_down, w_trip_bil, w_trip_up,
    w_res_one, w_res_two, w_atom_edge, w_edge_rbf, w_edge_atom, w_out,
    cot_edge, cot_atom, cot_feat,
):
    peers = lax.axis_size("edge")
    role = lax.axis_index("pair")
    role_arg = role.astype(i32).reshape(1)
    place_at = jnp.stack([role, lax.axis_index("edge")]).astype(i32)
    stages = edge_stages()
    plane, line = stages[0], stages[1:]
    codes = stage_codes(stages)
    edges, half_width = edge_embed.shape
    half = edges // 2
    width = 2 * half_width
    atoms, half_atom = atom_embed.shape
    radial_width = edge_rbf.shape[1]
    slots = trip_index.shape[1]
    quad_count, quad_slots = quad_index.shape
    half_quad = quad_count // 2
    halo_count = halo_send.shape[0]
    trip_width = w_trip_down.shape[1]
    quad_width = w_quad_down.shape[1]
    narrow = trip_width + quad_width
    orders = w_trip_bil.shape[0] // trip_width
    atom_width = 2 * half_atom
    tile = half // 2
    grid = (half // tile,)

    def other_rows(x):
        return lax.dynamic_slice_in_dim(x, (1 - role) * half, half, axis=0)

    emb_recv = swap(other_rows(edge_embed))
    cot_recv = swap(other_rows(cot_edge))
    small_own = jnp.concatenate([atom_embed, cot_atom, cot_feat], axis=0)
    small_recv = swap(small_own)
    target = quad_target.reshape(1, quad_count)
    ends = jnp.stack([edge_src, edge_dst])
    halo_out = atom_embed[halo_send].reshape(peers, -1)
    t_index, t_cos, t_live = trip_index.T, trip_cos.T, trip_live.T
    q_index, q_cos, q_dih, q_live = quad_index.T, quad_cos.T, quad_dih.T, quad_live.T
    w_down_t, w_down_q, w_bil_t, w_bil_q = w_trip_down.T, w_quad_down.T, w_trip_bil.T, w_quad_bil.T

    mine = pl.BlockSpec((tile, half_width), lambda i, r: (r[0] * grid[0] + i, 0))
    mine_rbf = pl.BlockSpec((tile, radial_width), lambda i, r: (r[0] * grid[0] + i, 0))
    mine_ends = pl.BlockSpec((2, tile), lambda i, r: (0, r[0] * grid[0] + i))
    mine_slots = pl.BlockSpec((slots, tile), lambda i, r: (0, r[0] * grid[0] + i))
    mine_quad = pl.BlockSpec((quad_slots, half_quad), lambda i, r: (0, r[0]))
    down_scratch = [
        pltpu.VMEM((2, radial_width, 2 * width), bf16), pltpu.VMEM((2, trip_width, width), bf16), pltpu.VMEM((2, quad_width, width), bf16),
    ]
    down_weights = (w_trip_rbf, w_quad_rbf, w_down_t, w_down_q)
    emb, pre, table = call(
        down_kernel, "down", grid,
        [mine, rows_of(tile, half_width), mine_rbf] + [whole(w.shape) for w in down_weights],
        [rows_of(tile, width), columns_of(narrow, tile), columns_of(narrow, tile)],
        [out(half, width), out(narrow, half), out(narrow, half)], down_scratch,
        (role_arg, edge_embed, emb_recv, edge_rbf, *down_weights), scalars=1, flops=4 * 10**9,
    )
    table_recv = swap(table)

    bil_rows = w_bil_q.shape[1]
    z_quad, quad_rows = call(
        functools.partial(quad_forward_kernel, orders=orders, base=trip_width), "quad_forward", (1,),
        [whole(table.shape)] * 2 + [mine_quad] * 4 + [whole(w_bil_q.shape)],
        [whole((bil_rows, half_quad)), whole((quad_width, half_quad))],
        [out(bil_rows, half_quad), out(quad_width, half_quad)],
        [pltpu.VMEM((quad_slots, quad_width, half_quad), f32)] * 2 + [pltpu.VMEM((orders, quad_slots, half_quad), f32)],
        (role_arg, table, table_recv, q_index, q_cos, q_dih, q_live, w_bil_q), scalars=1, flops=2 * 10**9,
    )
    cap = quad_count // peers
    cut = quad_width * cap

    def by_peer(x):
        return x.reshape(quad_width, -1, cap).transpose(1, 0, 2).reshape(-1, cut)

    def by_entry(x):
        return x.reshape(-1, quad_width, cap).transpose(1, 0, 2).reshape(quad_width, -1)

    quad_sent = lax.dynamic_update_slice_in_dim(jnp.zeros((peers, cut), f32), by_peer(quad_rows), role * (peers // 2), axis=0)
    routed = exchange(jnp.concatenate([quad_sent, halo_out], axis=1))
    quad_own = by_entry(routed[:, :cut])
    halo_own = routed[:, cut:].reshape(halo_count, half_atom)
    quad_recv = swap(quad_own)
    halo_recv = swap(halo_own)

    bil_rows = w_bil_t.shape[1]
    steps = grid[0] // 2
    table_shape = (2 * CLASSES * trip_width, edges // CLASSES)

    def halves_of(rows):
        return [
            pl.BlockSpec((rows, tile), lambda i, *_: (0, jnp.minimum(i, steps - 1))),
            pl.BlockSpec((rows, tile), lambda i, *_: (0, jnp.maximum(i - steps, 0))),
        ]

    def slots_at(first):
        return [pl.BlockSpec((slots, tile), lambda i, r: (0, r[0] * grid[0] + first + i))] * 3

    def triplet_forward(first, after):
        return call(
            functools.partial(triplet_forward_kernel, orders=orders), f"triplet_forward{first}", (steps,),
            [whole(table.shape)] * 2 + slots_at(first) + [whole(w_bil_t.shape)],
            [columns_of(bil_rows, tile), columns_of(trip_width, tile)],
            [out(bil_rows, half // 2), out(trip_width, half // 2)],
            [
                pltpu.VMEM(table_shape, bf16),
                pltpu.VMEM((2, slots, trip_width, LANES), f32),
                pltpu.VMEM((orders, slots, tile), f32),
                pltpu.VMEM((2, *w_bil_t.shape), bf16),
            ],
            (role_arg, table, table_recv, t_index, t_cos, t_live, w_bil_t), scalars=1, flops=5 * 10**9, after=after,
        )

    z_one, mid_one = triplet_forward(0, [])
    z_two, mid_two = triplet_forward(steps, [quad_own, halo_own, mid_one])

    atom_recv = small_recv[:atoms]
    pool_rows = atoms + halo_count
    square = pltpu.VMEM((2, width, width), bf16)
    up_scratch = pltpu.VMEM((2, narrow, width), bf16)
    rad_scratch = pltpu.VMEM((2, radial_width, width), bf16)
    main_weights = (w_trip_up, w_quad_up, w_res_one, w_res_two, w_atom_edge, w_edge_rbf)
    main_small = (target, quad_own, quad_recv, atom_embed, atom_recv, halo_own, halo_recv)
    mid, joined, pre_one, pre_two, pre_six, new_own, new_send, coll_own = call(
        main_forward_kernel, "main_forward", grid,
        [rows_of(tile, width), *halves_of(trip_width), mine_rbf, mine_ends]
        + [whole(x.shape) for x in main_small + main_weights],
        [columns_of(narrow, tile)] + [rows_of(tile, width)] * 4 + [mine, rows_of(tile, half_width), whole((atoms, width))],
        [out(narrow, half)] + [out(half, width)] * 4 + [out(edges, half_width), out(half, half_width), out(atoms, width)],
        [up_scratch, square, square, square, rad_scratch, pltpu.VMEM((2, pool_rows + atoms, width), bf16), pltpu.VMEM((2 * quad_width, quad_count), bf16)],
        (role_arg, emb, mid_one, mid_two, edge_rbf, ends, *main_small, *main_weights), scalars=1, flops=8 * 10**9,
    )
    coll_recv = swap(coll_own)
    new_recv = swap(new_send)

    edge_rows = padded_rows(w_atom_edge.shape[0] + radial_width + w_edge_atom.size // width + w_out.size // width)
    atom_args = (coll_own, coll_recv, small_own, small_recv, halo_own, halo_recv, w_atom_edge, w_edge_rbf, w_edge_atom, w_out)
    res_grad, edge_keep, edge_send, pool_grad_own, pool_grad_send, atom_out, feat_out = call(
        functools.partial(edge_backward_kernel, scale=(atoms / edges) ** 0.5, codes=codes), "edge_backward", grid,
        [rows_of(tile, width)] * 3 + [mine_rbf, mine_ends, mine, rows_of(tile, half_width)] + [whole(x.shape) for x in atom_args],
        [rows_of(tile, width), whole((edge_rows // 2, width)), whole((edge_rows // 2, width)),
         whole((pool_rows, half_atom)), whole((pool_rows, half_atom)), whole((atoms, half_atom)), whole((atoms, half_atom))],
        [out(half, width), out(edge_rows // 2, width), out(edge_rows // 2, width),
         out(pool_rows, half_atom), out(pool_rows, half_atom), out(atoms, half_atom), out(atoms, half_atom)],
        [square, rad_scratch, pltpu.VMEM((2, atoms, width), bf16), pltpu.VMEM((pool_rows + atoms, width), f32), pltpu.VMEM((atoms, atom_width), f32),
         pltpu.VMEM((edge_rows, width), f32)],
        (place_at, joined, pre_two, pre_six, edge_rbf, ends, cot_edge, cot_recv, *atom_args), scalars=1, flops=8 * 10**9,
    )
    edge_blocks = phase([("add", [edge_keep, swap(edge_send)], plane[1])], "phase_one")[0]
    edge_parts = middle_stages(send_blocks(edge_blocks, plane), line[:-1], "edge_middle")

    res_rows = padded_rows(2 * width + narrow + w_bil_t.size // width)
    res_weights = (w_trip_up, w_quad_up, w_res_one, w_res_two)
    sum_grad, mid_grad, res_keep, res_send, back_part = call(
        functools.partial(residual_backward_kernel, codes=codes), "residual_backward", grid,
        [rows_of(tile, width)] * 3 + [columns_of(narrow, tile), *halves_of(bil_rows), whole(target.shape), rows_of(tile, width)]
        + [whole(w.shape) for w in res_weights],
        [rows_of(tile, width), columns_of(narrow, tile), whole((res_rows // 2, width)), whole((res_rows // 2, width)), whole((quad_width, quad_count))],
        [out(half, width), out(narrow, half), out(res_rows // 2, width), out(res_rows // 2, width), out(quad_width, quad_count)],
        [up_scratch, square, square, pltpu.VMEM((res_rows, width), f32), pltpu.VMEM(w_bil_t.shape, f32)],
        (place_at, joined, pre_one, pre_two, mid, z_one, z_two, target, res_grad, *res_weights), scalars=1, flops=8 * 10**9, after=edge_blocks,
    )
    sums_shape = (2 * CLASSES * trip_width, edges // CLASSES)

    def triplet_backward(first, held, after):
        return call(
            functools.partial(triplet_backward_kernel, orders=orders), f"triplet_backward{first}", (steps,),
            [pl.BlockSpec((narrow, tile), lambda i, r: (0, first + i))] + slots_at(first) + [whole(w_bil_t.shape)] + [whole(h.shape) for h in held],
            [whole(sums_shape)],
            [out(*sums_shape)],
            [
                pltpu.VMEM((bil_rows, tile), f32),
                pltpu.VMEM((2, slots, trip_width, LANES), f32),
                pltpu.VMEM((orders, slots, tile), f32),
                pltpu.VMEM((2, *w_bil_t.shape), bf16),
            ],
            (role_arg, mid_grad, t_index, t_cos, t_live, w_bil_t, *held), scalars=1, flops=6 * 10**9, after=after,
        )

    edge_blocks, (res_send,), (back_part,), (pool_grad_send,) = phase(
        [("add", edge_parts, line[-1][1]), ("join", [res_send], 1), ("join", [back_part], 1), ("join", [pool_grad_send], 1)], "phase_two", [sum_grad]
    )
    edge_parts = send_blocks(edge_blocks, line[-1])
    res_recv = swap(res_send)
    held = triplet_backward(0, [], edge_blocks)
    (edge_piece,), res_blocks, (pool_grad,), (back_sum,) = phase(
        [
            ("add", edge_parts, 1),
            ("add", [res_keep, res_recv], plane[1]),
            ("add", [pool_grad_own, swap(pool_grad_send)], 1),
            ("add", [back_part, swap(back_part)], 1),
        ],
        "phase_three", held,
    )
    returned_sent = jnp.concatenate([by_peer(back_sum), pool_grad[atoms:].reshape(peers, -1)], axis=1)
    edge_piece, edge_codes = middle_gathers(edge_piece, line[1:], "edge_middle_gather")
    edge_pieces, edge_lists = spread(edge_piece, edge_codes, line[0])
    res_parts = middle_stages(send_blocks(res_blocks, plane), line[:-1], "res_middle")
    returned = exchange(returned_sent)
    (trip_sums,) = triplet_backward(steps, held, [edge_piece, *res_blocks, returned_sent])
    (edge_piece,), res_blocks = phase([("join", edge_pieces, 1), ("add", res_parts, line[-1][1])], "phase_four", [trip_sums])
    edge_pieces, edge_codes = spread(edge_piece, sum(edge_lists, []), plane)
    res_parts = send_blocks(res_blocks, line[-1])
    back_rows = lax.dynamic_slice_in_dim(returned[:, :cut], role * (peers // 2), peers // 2, axis=0)
    back_own = by_entry(back_rows)
    halo_back = returned[:, cut:].reshape(halo_count, half_atom)
    bil_rows = w_bil_q.shape[1]
    quad_bil, table_keep, table_send = call(
        functools.partial(quad_backward_kernel, orders=orders), "quad_backward", (1,),
        [whole(back_own.shape), whole(z_quad.shape)] + [mine_quad] * 4 + [whole(w_bil_q.shape), whole(trip_sums.shape)],
        [whole(w_bil_q.shape), whole((narrow, half)), whole((narrow, half))],
        [out(*w_bil_q.shape), out(narrow, half), out(narrow, half)],
        [pltpu.VMEM((bil_rows, half_quad), f32), pltpu.VMEM((quad_slots, quad_width, half_quad), f32), pltpu.VMEM((orders, quad_slots, half_quad), f32)],
        (role_arg, back_own, z_quad, q_index, q_cos, q_dih, q_live, w_bil_q, trip_sums), scalars=1, flops=2 * 10**9,
        after=[edge_piece, *res_blocks],
    )
    table_recv = swap(table_send)
    ((res_piece,),) = phase([("add", res_parts, 1)], "phase_quad", [table_keep])
    res_piece, res_codes = middle_gathers(res_piece, line[1:], "res_middle_gather")
    res_pieces, res_lists = spread(res_piece, res_codes, line[0])

    late_rows = padded_rows(2 * radial_width + narrow + w_bil_q.size // width)
    grad_own, grad_send, late_keep, late_send = call(
        functools.partial(final_kernel, codes=[0]), "final", grid,
        [rows_of(tile, width), mine_rbf] + [columns_of(narrow, tile)] * 3 + [rows_of(tile, width)]
        + [whole(x.shape) for x in (quad_bil,) + down_weights],
        [mine, rows_of(tile, half_width)] + [whole((late_rows // 2, width))] * 2,
        [out(edges, half_width), out(half, half_width)] + [out(late_rows // 2, width)] * 2,
        down_scratch + [pltpu.VMEM((late_rows, width), f32)],
        (place_at * jnp.array([1, 0], i32), emb, edge_rbf, pre, table_keep, table_recv, sum_grad, quad_bil, *down_weights), scalars=1, flops=6 * 10**9,
        after=[res_piece],
    )
    grad_recv = swap(grad_send)
    (res_piece,), (late_send,) = phase([("join", res_pieces, 1), ("join", [late_send], 1)], "phase_five", edge_pieces[1:])
    ((late_half,),) = phase([("add", [late_keep, swap(late_send)], 1)], "phase_late")
    late_blocks = scatter_blocks(late_half)
    res_pieces, res_codes = spread(res_piece, sum(res_lists, []), plane)
    edge_full = lax.dynamic_update_slice_in_dim(new_own, new_recv, (1 - role) * half, axis=0)
    g_atom_edge, g_edge_rbf, g_edge_atom, g_out = unpack(
        edge_pieces, edge_codes, place_at, [w_atom_edge.shape, w_edge_rbf.shape, w_edge_atom.shape, w_out.shape],
        ["plain", "plain", "rows", "rows"], "edge_unpack", [late_half],
    )
    late_piece = fold(late_blocks, "late_fold", [g_out, *res_pieces])
    late_all = exchange(jnp.broadcast_to(late_piece[None], late_blocks.shape)).reshape(late_half.shape)
    grad_full = lax.dynamic_update_slice_in_dim(grad_own, grad_recv, (1 - role) * half, axis=0)
    g_two, g_one, g_trip_up, g_quad_up, g_bil_t = unpack(
        res_pieces, res_codes, place_at, [w_res_two.shape, w_res_one.shape, w_trip_up.shape, w_quad_up.shape, w_bil_t.shape],
        ["plain"] * 4 + ["columns"], "res_unpack", [late_piece],
    )
    grad_atom = pool_grad[:atoms] + jnp.zeros((atoms, half_atom), f32).at[halo_send].add(halo_back)
    late_all = phase([("join", [late_all], 1)], "phase_six", [g_one, edge_full, grad_full, grad_atom])[0][0]
    g_trip_rbf, g_quad_rbf, g_down_t, g_down_q, g_bil_q = unpack(
        [late_all], [[0]], place_at * jnp.array([1, 0], i32), [w_trip_rbf.shape, w_quad_rbf.shape, w_down_t.shape, w_down_q.shape, w_bil_q.shape],
        ["plain"] * 4 + ["columns"], "late_unpack",
    )
    return (
        edge_full, atom_out, feat_out, grad_full, grad_atom,
        g_quad_rbf, g_down_q.T, g_bil_q.T, g_quad_up, g_trip_rbf, g_down_t.T, g_bil_t.T, g_trip_up,
        g_one, g_two, g_atom_edge, g_edge_rbf, g_edge_atom, g_out,
    )


def solution(mesh):
    whole_spec, rows_spec, both_spec = P(), P("edge"), P("edge", "pair")
    in_specs = (both_spec, both_spec) + (rows_spec,) * 12 + (whole_spec,) * 14 + (both_spec,) * 3
    out_specs = (both_spec,) * 5 + (whole_spec,) * 14
    return jax.shard_map(local, mesh=mesh, in_specs=in_specs, out_specs=out_specs, check_vma=False)
```

```python
import functools

import jax
import jax.numpy as jnp
from jax import lax
from jax.experimental import pallas as pl
from jax.experimental.pallas import tpu as pltpu
from jax.sharding import PartitionSpec as P

f32, bf16, i32 = jnp.float32, jnp.bfloat16, jnp.int32
root_third = 0.5773502691896258
root_half = 0.7071067811865476
LANES = 128
CLASSES = 4
VMEM_LIMIT = 30 * 2**20
SMALL_LIMIT = 24 * 2**20


def split(x):
    high = x.astype(bf16)
    return high, (x - high.astype(f32)).astype(bf16)


def dot(left, right, dims):
    return lax.dot_general(left, right, (dims, ((), ())), preferred_element_type=f32)


NN = ((1,), (0,))
NT = ((1,), (1,))
TN = ((0,), (0,))


def dot3(left, right, dims=NN):
    lh, ll = left if isinstance(left, tuple) else split(left)
    rh, rl = right if isinstance(right, tuple) else split(right)
    at, to = dims[0][0], dims[1][0]
    depth, rows = lh.shape[at], lh.shape[1 - at]
    if (at == 0 or depth % LANES == 0) and (to == 0 or depth % LANES == 0):
        if 3 * depth <= 2 * LANES:
            return dot(jnp.concatenate([lh, lh, ll], axis=at), jnp.concatenate([rh, rl, rh], axis=to), dims)
        if 2 * depth <= 2 * LANES:
            return dot(jnp.concatenate([lh, ll], axis=at), jnp.concatenate([rh, rh], axis=to), dims) + dot(lh, rl, dims)
    if at == 1 and rows <= LANES:
        both = dot(jnp.concatenate([lh, ll], axis=0), rh, dims)
        return both[:rows] + both[rows:] + dot(lh, rl, dims)
    return dot(lh, rh, dims) + dot(lh, rl, dims) + dot(ll, rh, dims)


def pick(onehot, right, dims=NN):
    rh, rl = right if isinstance(right, tuple) else split(right)
    return dot(onehot, rh, dims) + dot(onehot, rl, dims)


def sigmoid(v):
    return 0.5 * jnp.tanh(0.5 * v) + 0.5


def silu(v):
    return v * sigmoid(v)


def silu_grad(v):
    s = sigmoid(v)
    return s * (1.0 + v * (1.0 - s))


def as_bf16(mask):
    return mask.astype(f32).astype(bf16)


def legendre_steps(cosine, orders):
    before, now = jnp.ones_like(cosine), cosine
    yield before
    yield now
    for order in range(1, orders - 1):
        before, now = now, ((2 * order + 1) / (order + 1)) * cosine * now - (order / (order + 1)) * before
        yield now


def class_table(own, other, classes):
    per = classes // 2
    step = own.shape[1] // per
    parts = []
    for block in (own, other):
        high, low = split(block)
        for q in range(per):
            parts += [high[:, q * step : (q + 1) * step], low[:, q * step : (q + 1) * step]]
    return jnp.concatenate(parts, axis=0)


def gather_classes(table, index, classes, width):
    step = table.shape[1]
    shift = step.bit_length() - 1
    slots = index.shape[1]
    onehot = as_bf16(lax.broadcasted_iota(i32, (step, slots), 0) == (index & (step - 1)))
    found = dot(table, onehot, NN)
    kind = index >> shift
    out = found[0:width] + found[width : 2 * width]
    for q in range(1, classes):
        base = q * 2 * width
        out = jnp.where(kind >= q, found[base : base + width] + found[base + width : base + 2 * width], out)
    return out


def scatter_classes(values, indices, classes, step):
    shift = step.bit_length() - 1
    lefts, rights = [], []
    for value, index in zip(values, indices):
        width, slots = value.shape
        high, low = split(value)
        both = jnp.concatenate([high, low], axis=0)
        kind = jnp.broadcast_to(index >> shift, (2 * width, slots))
        lefts.append(jnp.concatenate([jnp.where(kind == q, both, jnp.zeros((), bf16)) for q in range(classes)], axis=0))
        rights.append(as_bf16(lax.broadcasted_iota(i32, (step, slots), 0) == (index & (step - 1))))
    return dot(jnp.concatenate(lefts, axis=1), jnp.concatenate(rights, axis=1), NT)


def unfold_classes(sums, classes, width):
    parts = []
    for q in range(classes):
        base = q * 2 * width
        parts.append(sums[base : base + width] + sums[base + width : base + 2 * width])
    return jnp.concatenate(parts, axis=1)


def joined_halves(zero, mine, theirs, axis=1):
    return jnp.concatenate([jnp.where(zero, mine, theirs), jnp.where(zero, theirs, mine)], axis=axis)


def down_kernel(role, own, recv, rbf, w_trip_rad, w_quad_rad, w_trip, w_quad, emb_out, pre_out, table_out, rad, down_t, down_q):
    width = w_trip_rad.shape[1]

    @pl.when(pl.program_id(0) == 0)
    def _():
        rad[0, :, :width], rad[1, :, :width] = split(w_trip_rad[...])
        rad[0, :, width:], rad[1, :, width:] = split(w_quad_rad[...])
        down_t[0], down_t[1] = split(w_trip[...])
        down_q[0], down_q[1] = split(w_quad[...])

    emb = joined_halves(role[0] == 0, own[...], recv[...])
    emb_out[...] = emb
    radial = dot3(rbf[...], (rad[0], rad[1]))
    pre = jnp.concatenate(
        [
            dot3((down_t[0], down_t[1]), emb * radial[:, :width], NT),
            dot3((down_q[0], down_q[1]), emb * radial[:, width:], NT),
        ],
        axis=0,
    )
    pre_out[...] = pre
    table_out[...] = silu(pre)


def quad_forward_kernel(role, own, other, index, cosine, dihedral, live, w_bil, z_out, rows_out, sel, sel2, basis, *, orders, base):
    slots_k, rows = index.shape
    width = w_bil.shape[0]
    zero = role[0] == 0
    mine, theirs = own[base : base + width, :], other[base : base + width, :]
    table = class_table(jnp.where(zero, mine, theirs), jnp.where(zero, theirs, mine), 2 * CLASSES)
    alive = live[...].astype(f32)
    for order, series in enumerate(legendre_steps(cosine[...], orders)):
        basis[order] = series * alive
    for k in range(slots_k):
        picked = gather_classes(table, index[k : k + 1, :], 2 * CLASSES, width)
        sel[k] = picked
        sel2[k] = picked * dihedral[k : k + 1, :]
    groups = width // 8
    for t in range(rows // LANES):
        at = slice(t * LANES, (t + 1) * LANES)
        for part, source in enumerate((sel, sel2)):
            for order_at in range(0, orders, 8):
                sums = {}
                for k in range(slots_k):
                    chosen = [source[k, g * 8 : g * 8 + 8, at] for g in range(groups)]
                    for order in range(8):
                        weight = jnp.broadcast_to(basis[order_at + order, k : k + 1, at], (8, LANES))
                        for g in range(groups):
                            term = weight * chosen[g]
                            sums[order, g] = term if k == 0 else sums[order, g] + term
                for (order, g), total in sums.items():
                    row = (part * orders + order_at + order) * width + g * 8
                    z_out[row : row + 8, at] = total
    rows_out[...] = dot3(w_bil[...], z_out[...])


def triplet_forward_kernel(role, own, other, index, cosine, live, w_bil, z_out, mid_out, table, sel, basis, bil, *, orders):
    slots_k, tile = index.shape
    width = w_bil.shape[0]

    @pl.when(pl.program_id(0) == 0)
    def _():
        zero = role[0] == 0
        mine, theirs = own[0:width, :], other[0:width, :]
        table[...] = class_table(jnp.where(zero, mine, theirs), jnp.where(zero, theirs, mine), CLASSES)
        bil[0], bil[1] = split(w_bil[...])

    alive = live[...].astype(f32)
    for order, series in enumerate(legendre_steps(cosine[...], orders)):
        basis[order] = series * alive

    def gather(at, k, into):
        where_to = jnp.concatenate([index[k : k + 1, at], index[k + 1 : k + 2, at]], axis=1)
        found = gather_classes(table[...], where_to, CLASSES, width)
        sel[into, k] = found[:, :LANES]
        sel[into, k + 1] = found[:, LANES:]

    def combine(at, first, source):
        sums = {}
        for k in range(slots_k):
            chosen = [sel[source, k, g * 8 : g * 8 + 8, :] for g in (first, first + 1)]
            for order in range(orders):
                weight = jnp.broadcast_to(basis[order, k : k + 1, at], (8, LANES))
                for g in range(2):
                    term = weight * chosen[g]
                    sums[order, g] = term if k == 0 else sums[order, g] + term
        for (order, g), total in sums.items():
            row = order * width + (first + g) * 8
            z_out[row : row + 8, at] = total

    firsts = range(0, width // 8, 2)
    turns = slots_k // 2 // len(firsts)
    columns = lambda c: pl.ds(pl.multiple_of(c * LANES, LANES), LANES)
    for k in range(0, slots_k, 2):
        gather(columns(0), k, 0)

    def step_columns(c, carry):
        for n, first in enumerate(firsts):
            for k in range(n * turns, (n + 1) * turns):
                gather(columns(c), 2 * k, c & 1)
            combine(columns(c - 1), first, 1 - (c & 1))
        return carry

    lax.fori_loop(1, tile // LANES, step_columns, 0)
    for first in firsts:
        combine(columns(tile // LANES - 1), first, (tile // LANES - 1) & 1)
    mid_out[...] = dot3((bil[0], bil[1]), z_out[...])


def laid(pairs):
    return tuple(jnp.concatenate([p[n] for p in pairs], axis=0) for n in range(2))


def row_blocks(tile):
    return [slice(n * tile // 2, (n + 1) * tile // 2) for n in range(2)]


def edge_members(ends, pool_rows, atoms, tile):
    row = lax.broadcasted_iota(i32, (pool_rows + atoms, tile), 0)
    return as_bf16(row == jnp.where(row < pool_rows, ends[0:1, :], ends[1:2, :] + pool_rows))


def entry_members(role, target, step, tile, half):
    row = lax.broadcasted_iota(i32, (tile, target.shape[1]), 0) + (step * tile + role[0] * half)
    return as_bf16(row == target[...])


def main_forward_kernel(
    role, emb, mid_one, mid_two, rbf, ends, target, quad_own, quad_recv, atom_own, atom_recv, halo_own, halo_recv,
    w_trip_up, w_quad_up, w_one, w_two, w_edge, w_rbf,
    mid_out, joined_out, one_out, two_out, six_out, new_own, new_send, collected,
    up, one, two, three, rad, pool_w, quad_hl,
):
    step = pl.program_id(0)
    tile = emb.shape[0]
    half_rows = tile * pl.num_programs(0)
    atoms = atom_own.shape[0]
    pool_rows = atoms + halo_own.shape[0]
    atom_width = 2 * atom_own.shape[1]
    trip_width = w_trip_up.shape[0]
    zero = role[0] == 0

    @pl.when(step == 0)
    def _():
        up[0, :trip_width], up[1, :trip_width] = split(w_trip_up[...])
        up[0, trip_width:], up[1, trip_width:] = split(w_quad_up[...])
        one[0], one[1] = split(w_one[...])
        two[0], two[1] = split(w_two[...])
        three[0], three[1] = split(w_edge[2 * atom_width :, :])
        rad[0], rad[1] = split(w_rbf[...])
        atom_rows = joined_halves(zero, atom_own[...], atom_recv[...])
        pool = jnp.concatenate([atom_rows, joined_halves(zero, halo_own[...], halo_recv[...])], axis=0)
        projected = jnp.concatenate(
            [dot3(pool, w_edge[0:atom_width, :]), dot3(atom_rows, w_edge[atom_width : 2 * atom_width, :])], axis=0
        )
        pool_w[0], pool_w[1] = split(projected)
        high, low = split(quad_own[...] + quad_recv[...])
        quad_hl[...] = jnp.concatenate([high, low], axis=0)

    found = dot(quad_hl[...], entry_members(role, target, step, tile, half_rows), NT)
    width = found.shape[0] // 2
    mid_trip = jnp.where(step < pl.num_programs(0) // 2, mid_one[...], mid_two[...])
    mid = jnp.concatenate([mid_trip, found[:width] + found[width:]], axis=0)
    mid_out[...] = mid
    member = edge_members(ends, pool_rows, atoms, tile)
    blocks = row_blocks(tile)
    joined = [(emb[at, :] + dot3(mid[:, at], (up[0], up[1]), TN)) * root_third for at in blocks]
    pre_one = [dot3(x, (one[0], one[1])) for x in joined]
    pre_two = [dot3(silu(x), (two[0], two[1])) for x in pre_one]
    residual = [(x + silu(y)) * root_half for x, y in zip(joined, pre_two)]
    pre_six = [pick(member[:, at], (pool_w[0], pool_w[1]), TN) + dot3(x, (three[0], three[1])) for at, x in zip(blocks, residual)]
    edge_new = [(x + silu(y)) * root_half for x, y in zip(residual, pre_six)]
    half = emb.shape[1] // 2
    part = 0.0
    for n, at in enumerate(blocks):
        joined_out[at, :] = joined[n]
        one_out[at, :] = pre_one[n]
        two_out[at, :] = pre_two[n]
        six_out[at, :] = pre_six[n]
        new_own[at, :] = jnp.where(zero, edge_new[n][:, :half], edge_new[n][:, half:])
        new_send[at, :] = jnp.where(zero, edge_new[n][:, half:], edge_new[n][:, :half])
        part = part + pick(member[pool_rows:, at], edge_new[n] * dot3(rbf[at, :], (rad[0], rad[1])))

    @pl.when(step == 0)
    def _():
        collected[...] = part

    @pl.when(step > 0)
    def _():
        collected[...] += part


def give_halves(place_at, total, keep, send, codes):
    half = keep.shape[0]
    rows = half // len(codes)
    for side, target in ((place_at[0], keep), (1 - place_at[0], send)):
        for n, code in enumerate(codes):
            at = pl.multiple_of(side * half + (place_at[1] ^ code) * rows, 8)
            target[n * rows : (n + 1) * rows, :] = total[pl.ds(at, rows), :]


def side_by_side(x, width):
    parts = width // x.shape[1]
    rows = x.shape[0] // parts
    return jnp.concatenate([x[q * rows : (q + 1) * rows] for q in range(parts)], axis=1)


def edge_backward_kernel(
    role, joined, pre_two_ref, pre_six_ref, rbf, ends, cot_own, cot_recv,
    coll_own, coll_recv, small_own, small_recv, halo_own, halo_recv,
    w_edge, w_rbf, w_edge_atom, w_out,
    res_grad_out, keep, send, pool_grad_own, pool_grad_send, atom_out, feat_out,
    three, rad, coll_grad, pool_sum, direct, grads,
    *, scale, codes,
):
    step = pl.program_id(0)
    last = pl.num_programs(0) - 1
    tile, edge_width = joined.shape
    half = small_own.shape[1]
    atoms = small_own.shape[0] // 3
    atom_width = 2 * half
    pool_rows = atoms + halo_own.shape[0]
    zero = role[0] == 0
    at_rbf = w_edge.shape[0]
    at_atom = at_rbf + w_rbf.shape[0]
    at_last = at_atom + w_edge_atom.shape[0] * atom_width // edge_width
    at_end = at_last + atom_width * atom_width // edge_width

    @pl.when(step == 0)
    def _():
        three[0], three[1] = split(w_edge[2 * atom_width :, :])
        rad[0], rad[1] = split(w_rbf[...])
        mine, theirs = small_own[...], small_recv[...]
        atom_rows = joined_halves(zero, mine[:atoms], theirs[:atoms])
        cot_atom = joined_halves(zero, mine[atoms : 2 * atoms], theirs[atoms : 2 * atoms])
        cot_feat = joined_halves(zero, mine[2 * atoms :], theirs[2 * atoms :])
        total = (coll_own[...] + coll_recv[...]) * scale
        w_a, w_f = split(w_edge_atom[...]), split(w_out[...])
        pre_atom = dot3(total, w_a)
        atom_new = (atom_rows + silu(pre_atom)) * root_half
        pre_feat = dot3(atom_new, w_f)
        feature = silu(pre_feat)
        atom_out[...] = jnp.where(zero, atom_new[:, :half], atom_new[:, half:])
        feat_out[...] = jnp.where(zero, feature[:, :half], feature[:, half:])
        feat_grad = cot_feat * silu_grad(pre_feat)
        grads[at_last:at_end, :] = side_by_side(0.5 * dot3(atom_new, feat_grad, TN), edge_width)
        atom_grad = (cot_atom + dot3(feat_grad, w_f, NT)) * root_half
        direct[...] = 0.5 * atom_grad
        pre_grad = atom_grad * silu_grad(pre_atom)
        grads[at_atom:at_last, :] = side_by_side(0.5 * dot3(total, pre_grad, TN), edge_width)
        coll_grad[0], coll_grad[1] = split(dot3(pre_grad, w_a, NT) * scale)
        grads[0:at_atom, :] = jnp.zeros((at_atom, grads.shape[1]), f32)
        if grads.shape[0] > at_end:
            grads[at_end:, :] = jnp.zeros((grads.shape[0] - at_end, grads.shape[1]), f32)
        pool_sum[...] = jnp.zeros_like(pool_sum)

    member = edge_members(ends, pool_rows, atoms, tile)
    blocks = row_blocks(tile)
    six = [pre_six_ref[at, :] for at in blocks]
    s_six = [sigmoid(x) for x in six]
    residual = [(joined[at, :] + silu(pre_two_ref[at, :])) * root_half for at in blocks]
    edge_new = [(x + y * s) * root_half for x, y, s in zip(residual, six, s_six)]
    radial = split(rbf[...])
    weighted_grad = [pick(member[pool_rows:, at], (coll_grad[0], coll_grad[1]), TN) for at in blocks]
    new_grad = [
        (joined_halves(zero, cot_own[at, :], cot_recv[at, :]) + w * dot3((radial[0][at], radial[1][at]), (rad[0], rad[1]))) * root_half
        for at, w in zip(blocks, weighted_grad)
    ]
    six_split = [split(g * (s * (1.0 + y * (1.0 - s)))) for g, y, s in zip(new_grad, six, s_six)]
    for at, g, pair in zip(blocks, new_grad, six_split):
        res_grad_out[at, :] = (g + dot3(pair, (three[0], three[1]), NT)) * root_half
    grads[at_rbf:at_atom, :] += dot3(radial, laid([split(w * x) for w, x in zip(weighted_grad, edge_new)]), TN)
    six_all = laid(six_split)
    pool_sum[...] += pick(member, six_all)
    grads[2 * atom_width : at_rbf, :] += dot3(laid([split(x) for x in residual]), six_all, TN)

    @pl.when(step == last)
    def _():
        atom_rows = joined_halves(zero, small_own[:atoms, :], small_recv[:atoms, :])
        pool = jnp.concatenate([atom_rows, joined_halves(zero, halo_own[...], halo_recv[...])], axis=0)
        w_src, w_dst = split(w_edge[0:atom_width, :]), split(w_edge[atom_width : 2 * atom_width, :])
        src_split, dst_split = split(pool_sum[0:pool_rows, :]), split(pool_sum[pool_rows:, :])
        grads[0:atom_width, :] = dot3(pool, src_split, TN)
        grads[atom_width : 2 * atom_width, :] = dot3(atom_rows, dst_split, TN)
        from_src = dot3(src_split, w_src, NT)
        from_atoms = from_src[0:atoms] + dot3(dst_split, w_dst, NT) + direct[...]
        result = jnp.concatenate([from_atoms, from_src[atoms:]], axis=0)
        pool_grad_own[...] = jnp.where(zero, result[:, :half], result[:, half:])
        pool_grad_send[...] = jnp.where(zero, result[:, half:], result[:, :half])
        give_halves(role, grads, keep, send, codes)


def residual_backward_kernel(
    role, joined, pre_one_ref, pre_two_ref, mid_ref, z_one, z_two, target, res_grad_ref,
    w_trip_up, w_quad_up, w_one, w_two,
    sum_grad_out, mid_grad_out, keep, send, back,
    up, one, two, grads, bil_grad,
    *, codes,
):
    step = pl.program_id(0)
    tile, width = joined.shape
    half_rows = tile * pl.num_programs(0)
    trip_width = w_trip_up.shape[0]
    narrow = up.shape[1]
    at_bil = 2 * width + narrow

    @pl.when(step == 0)
    def _():
        up[0, :trip_width], up[1, :trip_width] = split(w_trip_up[...])
        up[0, trip_width:], up[1, trip_width:] = split(w_quad_up[...])
        one[0], one[1] = split(w_one[...])
        two[0], two[1] = split(w_two[...])
        grads[...] = jnp.zeros_like(grads)
        bil_grad[...] = jnp.zeros_like(bil_grad)
        back[...] = jnp.zeros_like(back)

    blocks = row_blocks(tile)

    res_grad = [res_grad_ref[at, :] for at in blocks]
    two_split = [split(grad * silu_grad(pre_two_ref[at, :])) for grad, at in zip(res_grad, blocks)]
    pre_one = [pre_one_ref[at, :] for at in blocks]
    s_one = [sigmoid(pre) for pre in pre_one]
    hidden = [split(pre * s) for pre, s in zip(pre_one, s_one)]
    one_split = [
        split(dot3(grad, (two[0], two[1]), NT) * (s * (1.0 + pre * (1.0 - s)))) for grad, pre, s in zip(two_split, pre_one, s_one)
    ]
    grads[0:width, :] += dot3(laid(hidden), laid(two_split), TN)
    sum_grad = [(grad + dot3(inner, (one[0], one[1]), NT)) * root_third for grad, inner in zip(res_grad, one_split)]
    grads[width : 2 * width, :] += dot3(joined[...], laid(one_split), TN)
    for at, grad in zip(blocks, sum_grad):
        sum_grad_out[at, :] = grad
    sum_split = laid([split(grad) for grad in sum_grad])
    grads[2 * width : at_bil, :] += dot3(mid_ref[...], sum_split, NN)
    mid_grad = dot3((up[0], up[1]), sum_split, NT)
    mid_grad_out[...] = mid_grad
    mid_high, mid_low = split(mid_grad)
    z = jnp.where(step < pl.num_programs(0) // 2, z_one[...], z_two[...])
    bil_grad[...] += dot3((mid_high[:trip_width], mid_low[:trip_width]), z, NT)
    found = dot(jnp.concatenate([mid_high[trip_width:], mid_low[trip_width:]], axis=0), entry_members(role, target, step, tile, half_rows), NN)
    rows = narrow - trip_width
    back[...] += found[:rows] + found[rows:]

    @pl.when(step == pl.num_programs(0) - 1)
    def _():
        for q in range(bil_grad.shape[1] // width):
            grads[at_bil + q * trip_width : at_bil + (q + 1) * trip_width, :] = bil_grad[:, q * width : (q + 1) * width]
        give_halves(role, grads, keep, send, codes)


def triplet_backward_kernel(role, mid_grad, index, cosine, live, w_bil, *refs, orders):
    held, (sums, zg, sg, basis, bil) = refs[:-5], refs[-5:]
    step = pl.program_id(0)
    slots_k, tile = index.shape
    width = w_bil.shape[0]
    classes_step = sums.shape[1]

    @pl.when(step == 0)
    def _():
        bil[0], bil[1] = split(w_bil[...])
        sums[...] = held[0][...] if held else jnp.zeros_like(sums)

    alive = live[...].astype(f32)
    for order, series in enumerate(legendre_steps(cosine[...], orders)):
        basis[order] = series * alive
    grad_split = split(mid_grad[0:width, :])
    zg[...] = dot3((bil[0], bil[1]), grad_split, TN)

    def combine(at, first, into):
        totals = {}
        for order in range(orders):
            row = order * width + first * 8
            got = [zg[row + g * 8 : row + g * 8 + 8, at] for g in range(2)]
            for k in range(slots_k):
                weight = jnp.broadcast_to(basis[order, k : k + 1, at], (8, LANES))
                for g in range(2):
                    term = weight * got[g]
                    totals[k, g] = term if order == 0 else totals[k, g] + term
        for (k, g), total in totals.items():
            sg[into, k, (first + g) * 8 : (first + g) * 8 + 8, :] = total

    def scatter(at, first, source):
        slots_at = range(first, first + slots_k // 2)
        sums[...] += scatter_classes(
            [sg[source, k] for k in slots_at], [index[k : k + 1, at] for k in slots_at], CLASSES, classes_step
        )

    firsts = range(0, width // 8, 2)
    columns = lambda c: pl.ds(pl.multiple_of(c * LANES, LANES), LANES)
    for first in firsts:
        combine(columns(0), first, 0)

    def step_columns(c, carry):
        for n, first in enumerate(firsts):
            if n % 2 == 0:
                scatter(columns(c - 1), n // 2 * (slots_k // 2), 1 - (c & 1))
            combine(columns(c), first, c & 1)
        return carry

    lax.fori_loop(1, tile // LANES, step_columns, 0)
    for n in range(2):
        scatter(columns(tile // LANES - 1), n * (slots_k // 2), (tile // LANES - 1) & 1)


def quad_backward_kernel(role, own, z, index, cosine, dihedral, live, w_bil, trip_sums, bil_grad, keep, send, zg, sg, basis, *, orders):
    slots_k, rows = index.shape
    width = w_bil.shape[0]
    edges = trip_sums.shape[1] * CLASSES
    trip_width = trip_sums.shape[0] // (2 * CLASSES)
    zero = role[0] == 0
    alive = live[...].astype(f32)
    for order, series in enumerate(legendre_steps(cosine[...], orders)):
        basis[order] = series * alive
    grad_split = split(own[...])
    bil_grad[...] = dot3(grad_split, z[...], NT)
    zg[...] = dot3(w_bil[...], grad_split, TN)
    groups = width // 8
    for t in range(rows // LANES):
        at = slice(t * LANES, (t + 1) * LANES)
        for g in range(groups):
            plain, turned = {}, {}
            for order in range(orders):
                one = zg[order * width + g * 8 : order * width + g * 8 + 8, at]
                two = zg[(orders + order) * width + g * 8 : (orders + order) * width + g * 8 + 8, at]
                for k in range(slots_k):
                    weight = jnp.broadcast_to(basis[order, k : k + 1, at], (8, LANES))
                    plain[k] = weight * one if order == 0 else plain[k] + weight * one
                    turned[k] = weight * two if order == 0 else turned[k] + weight * two
            for k in range(slots_k):
                sg[k, g * 8 : g * 8 + 8, at] = plain[k] + turned[k] * jnp.broadcast_to(dihedral[k : k + 1, at], (8, LANES))
    step = edges // (2 * CLASSES)
    sums = scatter_classes([sg[k] for k in range(slots_k)], [index[k : k + 1, :] for k in range(slots_k)], 2 * CLASSES, step)
    total = jnp.concatenate([unfold_classes(trip_sums[...], CLASSES, trip_width), unfold_classes(sums, 2 * CLASSES, width)], axis=0)
    half = edges // 2
    keep[...] = jnp.where(zero, total[:, :half], total[:, half:])
    send[...] = jnp.where(zero, total[:, half:], total[:, :half])


def final_kernel(
    role, emb_ref, rbf, pre_ref, table_own, table_recv, sum_grad, quad_bil, w_trip_rad, w_quad_rad, w_trip, w_quad,
    grad_own, grad_send, keep, send,
    rad, down_t, down_q, total,
    *, codes,
):
    step = pl.program_id(0)
    zero = role[0] == 0
    radial_rows, width = w_trip_rad.shape
    trip_width, quad_width = w_trip.shape[0], w_quad.shape[0]
    at_quad_rad = radial_rows
    at_trip = 2 * radial_rows
    at_quad = at_trip + trip_width
    at_quad_bil = at_quad + quad_width
    at_end = at_quad_bil + quad_width * quad_bil.shape[1] // width

    @pl.when(step == 0)
    def _():
        rad[0, :, :width], rad[1, :, :width] = split(w_trip_rad[...])
        rad[0, :, width:], rad[1, :, width:] = split(w_quad_rad[...])
        down_t[0], down_t[1] = split(w_trip[...])
        down_q[0], down_q[1] = split(w_quad[...])
        total[...] = jnp.zeros_like(total)
        rows = quad_bil.shape[0]
        for q in range(quad_bil.shape[1] // width):
            total[at_quad_bil + q * rows : at_quad_bil + (q + 1) * rows, :] = quad_bil[:, q * width : (q + 1) * width]

    emb = emb_ref[...]
    radial_split = split(rbf[...])
    radial = dot3(radial_split, (rad[0], rad[1]))
    pre_grad = (table_own[...] + table_recv[...]) * silu_grad(pre_ref[...])
    trip_split, quad_split = split(pre_grad[:trip_width]), split(pre_grad[trip_width:])
    trip_radial, quad_radial = radial[:, :width], radial[:, width:]
    total[at_trip:at_quad, :] += dot3(trip_split, emb * trip_radial)
    total[at_quad:at_quad_bil, :] += dot3(quad_split, emb * quad_radial)
    trip_mixed = dot3(trip_split, (down_t[0], down_t[1]), TN)
    quad_mixed = dot3(quad_split, (down_q[0], down_q[1]), TN)
    grad = sum_grad[...] + trip_mixed * trip_radial + quad_mixed * quad_radial
    half = width // 2
    grad_own[...] = jnp.where(zero, grad[:, :half], grad[:, half:])
    grad_send[...] = jnp.where(zero, grad[:, half:], grad[:, :half])
    total[0:at_quad_rad, :] += dot3(radial_split, trip_mixed * emb, TN)
    total[at_quad_rad:at_trip, :] += dot3(radial_split, quad_mixed * emb, TN)

    @pl.when(step == pl.num_programs(0) - 1)
    def _():
        give_halves(role, total, keep, send, codes)


def fold_kernel(source, target):
    target[...] = jnp.sum(source[...], axis=0)


def fold(blocks, name, after=()):
    return call(fold_kernel, name, (1,), [whole(blocks.shape)], [whole(blocks.shape[1:])], [out(*blocks.shape[1:])], [], (blocks,), after=after, limit=SMALL_LIMIT)[0]


def exchange(blocks):
    return lax.all_to_all(blocks, "edge", split_axis=0, concat_axis=0, tiled=True)


def scatter_blocks(rows):
    return exchange(rows.reshape(lax.axis_size("edge"), -1, rows.shape[1]))


def partners(bits, axis="edge"):
    return [(i, i ^ bits) for i in range(lax.axis_size(axis))]


def edge_stages():
    size, shift, stages = lax.axis_size("edge"), 0, []
    while size > 1:
        radix = 8 if size == 8 else 4 if size % 4 == 0 else 2
        stages.append((shift, radix))
        shift += radix.bit_length() - 1
        size //= radix
    return stages


def padded_rows(rows):
    unit = 2 * 8 * lax.axis_size("edge")
    return -(-rows // unit) * unit


def spread(piece, codes, stage):
    shift, radix = stage
    pieces = [piece] + [lax.ppermute(piece, "edge", partners(j << shift)) for j in range(1, radix)]
    return pieces, [[c ^ (j << shift) for c in codes] for j in range(radix)]


def stage_codes(stages):
    codes = [0]
    for shift, radix in reversed(stages):
        codes = [c ^ (j << shift) for j in range(radix) for c in codes]
    return codes


def phase_kernel(*refs, jobs):
    ins, outs = list(refs[: sum(count for _, count, _ in jobs)]), list(refs[sum(count for _, count, _ in jobs) :])
    for kind, count, blocks in jobs:
        parts, ins = ins[:count], ins[count:]
        targets, outs = outs[:blocks], outs[blocks:]
        if kind == "join":
            rows = parts[0].shape[0]
            for n, part in enumerate(parts):
                targets[0][n * rows : (n + 1) * rows, :] = part[...]
        else:
            rows = parts[0].shape[0] // blocks
            for n, target in enumerate(targets):
                total = parts[0][n * rows : (n + 1) * rows, :]
                for part in parts[1:]:
                    total = total + part[n * rows : (n + 1) * rows, :]
                target[...] = total


def phase(jobs, name, after=()):
    ins, shapes = [], []
    for kind, parts, blocks in jobs:
        rows, width = parts[0].shape
        ins += parts
        shapes += [(len(parts) * rows, width)] if kind == "join" else [(rows // blocks, width)] * blocks
    got = call(
        functools.partial(phase_kernel, jobs=[(kind, len(parts), blocks) for kind, parts, blocks in jobs]), name, (1,),
        [whole(x.shape) for x in ins], [whole(x) for x in shapes], [out(*x) for x in shapes], [], tuple(ins), after=after, limit=SMALL_LIMIT,
    )
    results = []
    for _, _, blocks in jobs:
        results.append(got[:blocks])
        got = got[blocks:]
    return results


def send_blocks(blocks, stage):
    shift, radix = stage
    return [blocks[0]] + [lax.ppermute(blocks[j], "edge", partners(j << shift)) for j in range(1, radix)]


def middle_stages(parts, stages, name):
    for at, stage in enumerate(stages):
        parts = send_blocks(phase([("add", parts, stage[1])], f"{name}{at}")[0], stage)
    return parts


def middle_gathers(piece, stages, name):
    codes = [0]
    for at, stage in enumerate(reversed(stages)):
        pieces, lists = spread(piece, codes, stage)
        piece, codes = phase([("join", pieces, 1)], f"{name}{at}")[0][0], sum(lists, [])
    return piece, codes


def unpack_kernel(place_at, *refs, count, codes, layout):
    ins, outs, total = refs[:count], refs[count:-1], refs[-1]
    half = total.shape[0] // 2
    for n, source in enumerate(ins):
        side, listed = codes[n]
        first = jnp.where(place_at[0] == 0, side, 1 - side) * half
        rows = source.shape[0] // len(listed)
        for at, code in enumerate(listed):
            block = place_at[1] ^ code
            total[pl.ds(pl.multiple_of(first + block * rows, 8), rows), :] = source[at * rows : (at + 1) * rows, :]
    at = 0
    for target, kind in zip(outs, layout):
        height, breadth = target.shape
        width = total.shape[1]
        if kind == "plain":
            target[...] = total[at : at + height, :]
            at += height
        elif kind == "rows":
            parts = width // breadth
            rows = height // parts
            for q in range(parts):
                target[q * rows : (q + 1) * rows, :] = total[at : at + rows, q * breadth : (q + 1) * breadth]
            at += rows
        else:
            for q in range(breadth // width):
                target[:, q * width : (q + 1) * width] = total[at : at + height, :]
                at += height


def unpack(pieces, codes, place_at, shapes, layout, name, after=()):
    count = 2 * len(pieces)
    pieces = pieces + [swap(p) for p in pieces]
    codes = [(0, c) for c in codes] + [(1, c) for c in codes]
    rows = sum(p.shape[0] for p in pieces)
    return call(
        functools.partial(unpack_kernel, count=count, codes=codes, layout=layout), name, (1,), [whole(p.shape) for p in pieces],
        [whole(s) for s in shapes], [out(*s) for s in shapes], [pltpu.VMEM((rows, pieces[0].shape[1]), f32)], (place_at, *pieces), scalars=1, after=after, limit=SMALL_LIMIT,
    )


def whole(shape):
    return pl.BlockSpec(shape, lambda *_: (0,) * len(shape))


def rows_of(tile, width):
    return pl.BlockSpec((tile, width), lambda i, *_: (i, 0))


def columns_of(rows, tile):
    return pl.BlockSpec((rows, tile), lambda i, *_: (0, i))


def out(*shape):
    return jax.ShapeDtypeStruct(shape, f32)


def call(body, name, grid, in_specs, out_specs, out_shape, scratch, args, scalars=0, flops=0, after=(), aliases={}, limit=VMEM_LIMIT):
    first, count = len(args), len(after)

    def run(*refs):
        body(*refs[:first], *refs[first + count :])

    args = (*args, *after)
    in_specs = in_specs + [pl.BlockSpec(memory_space=pl.ANY)] * count
    return pl.pallas_call(
        run,
        name=name,
        grid_spec=pltpu.PrefetchScalarGridSpec(
            num_scalar_prefetch=scalars, grid=grid, in_specs=in_specs, out_specs=out_specs, scratch_shapes=scratch
        ),
        out_shape=out_shape,
        compiler_params=pltpu.CompilerParams(vmem_limit_bytes=limit, dimension_semantics=("arbitrary",) * len(grid)),
        cost_estimate=pl.CostEstimate(flops=max(flops, 1000), bytes_accessed=1000, transcendentals=0),
        input_output_aliases=aliases,
    )(*args)


def streamed(x):
    return pltpu.with_memory_space_constraint(x, pltpu.HBM)


def swap(x):
    return lax.ppermute(x, "pair", [(0, 1), (1, 0)])


def local(
    edge_embed, atom_embed, edge_rbf, edge_src, edge_dst, halo_send, trip_index, trip_cos, trip_live,
    quad_index, quad_cos, quad_dih, quad_live, quad_target,
    w_quad_rbf, w_quad_down, w_quad_bil, w_quad_up, w_trip_rbf, w_trip_down, w_trip_bil, w_trip_up,
    w_res_one, w_res_two, w_atom_edge, w_edge_rbf, w_edge_atom, w_out,
    cot_edge, cot_atom, cot_feat,
):
    peers = lax.axis_size("edge")
    role = lax.axis_index("pair")
    role_arg = role.astype(i32).reshape(1)
    place_at = jnp.stack([role, lax.axis_index("edge")]).astype(i32)
    stages = edge_stages()
    plane, line = stages[0], stages[1:]
    codes = stage_codes(stages)
    edges, half_width = edge_embed.shape
    half = edges // 2
    width = 2 * half_width
    atoms, half_atom = atom_embed.shape
    radial_width = edge_rbf.shape[1]
    slots = trip_index.shape[1]
    quad_count, quad_slots = quad_index.shape
    half_quad = quad_count // 2
    halo_count = halo_send.shape[0]
    trip_width = w_trip_down.shape[1]
    quad_width = w_quad_down.shape[1]
    narrow = trip_width + quad_width
    orders = w_trip_bil.shape[0] // trip_width
    atom_width = 2 * half_atom
    tile = half // 2
    grid = (half // tile,)

    def other_rows(x):
        return lax.dynamic_slice_in_dim(x, (1 - role) * half, half, axis=0)

    emb_recv = swap(other_rows(edge_embed))
    cot_recv = swap(other_rows(cot_edge))
    small_own = jnp.concatenate([atom_embed, cot_atom, cot_feat], axis=0)
    small_recv = swap(small_own)
    target = quad_target.reshape(1, quad_count)
    ends = jnp.stack([edge_src, edge_dst])
    halo_out = atom_embed[halo_send].reshape(peers, -1)
    t_index, t_cos, t_live = (streamed(x.T) for x in (trip_index, trip_cos, trip_live))
    q_index, q_cos, q_dih, q_live = (streamed(x.T) for x in (quad_index, quad_cos, quad_dih, quad_live))
    w_down_t, w_down_q, w_bil_t, w_bil_q = (streamed(x.T) for x in (w_trip_down, w_quad_down, w_trip_bil, w_quad_bil))
    w_trip_rbf, w_quad_rbf, w_trip_up, w_quad_up = (streamed(x) for x in (w_trip_rbf, w_quad_rbf, w_trip_up, w_quad_up))
    w_res_one, w_res_two, w_atom_edge, w_edge_rbf, w_edge_atom, w_out = (
        streamed(x) for x in (w_res_one, w_res_two, w_atom_edge, w_edge_rbf, w_edge_atom, w_out)
    )
    edge_mine, cot_mine, rbf_mine = streamed(edge_embed), streamed(cot_edge), streamed(edge_rbf)

    mine = pl.BlockSpec((tile, half_width), lambda i, r: (r[0] * grid[0] + i, 0))
    mine_rbf = pl.BlockSpec((tile, radial_width), lambda i, r: (r[0] * grid[0] + i, 0))
    mine_ends = pl.BlockSpec((2, tile), lambda i, r: (0, r[0] * grid[0] + i))
    mine_slots = pl.BlockSpec((slots, tile), lambda i, r: (0, r[0] * grid[0] + i))
    mine_quad = pl.BlockSpec((quad_slots, half_quad), lambda i, r: (0, r[0]))
    down_scratch = [
        pltpu.VMEM((2, radial_width, 2 * width), bf16), pltpu.VMEM((2, trip_width, width), bf16), pltpu.VMEM((2, quad_width, width), bf16),
    ]
    down_weights = (w_trip_rbf, w_quad_rbf, w_down_t, w_down_q)
    emb, pre, table = call(
        down_kernel, "down", grid,
        [mine, rows_of(tile, half_width), mine_rbf] + [whole(w.shape) for w in down_weights],
        [rows_of(tile, width), columns_of(narrow, tile), columns_of(narrow, tile)],
        [out(half, width), out(narrow, half), out(narrow, half)], down_scratch,
        (role_arg, edge_mine, emb_recv, rbf_mine, *down_weights), scalars=1, flops=4 * 10**9, limit=32 * 2**20,
    )
    table_recv = swap(table)

    bil_rows = w_bil_q.shape[1]
    z_quad, quad_rows = call(
        functools.partial(quad_forward_kernel, orders=orders, base=trip_width), "quad_forward", (1,),
        [whole(table.shape)] * 2 + [mine_quad] * 4 + [whole(w_bil_q.shape)],
        [whole((bil_rows, half_quad)), whole((quad_width, half_quad))],
        [out(bil_rows, half_quad), out(quad_width, half_quad)],
        [pltpu.VMEM((quad_slots, quad_width, half_quad), f32)] * 2 + [pltpu.VMEM((orders, quad_slots, half_quad), f32)],
        (role_arg, table, table_recv, q_index, q_cos, q_dih, q_live, w_bil_q), scalars=1, flops=2 * 10**9, limit=SMALL_LIMIT,
    )
    cap = quad_count // peers
    cut = quad_width * cap

    def by_peer(x):
        return x.reshape(quad_width, -1, cap).transpose(1, 0, 2).reshape(-1, cut)

    def by_entry(x):
        return x.reshape(-1, quad_width, cap).transpose(1, 0, 2).reshape(quad_width, -1)

    quad_sent = lax.dynamic_update_slice_in_dim(jnp.zeros((peers, cut), f32), by_peer(quad_rows), role * (peers // 2), axis=0)
    routed = exchange(jnp.concatenate([quad_sent, halo_out], axis=1))
    quad_own = by_entry(routed[:, :cut])
    halo_own = routed[:, cut:].reshape(halo_count, half_atom)
    quad_recv = swap(quad_own)
    halo_recv = swap(halo_own)

    bil_rows = w_bil_t.shape[1]
    steps = grid[0] // 2
    table_shape = (2 * CLASSES * trip_width, edges // CLASSES)

    def halves_of(rows):
        return [
            pl.BlockSpec((rows, tile), lambda i, *_: (0, jnp.minimum(i, steps - 1))),
            pl.BlockSpec((rows, tile), lambda i, *_: (0, jnp.maximum(i - steps, 0))),
        ]

    def slots_at(first):
        return [pl.BlockSpec((slots, tile), lambda i, r: (0, r[0] * grid[0] + first + i))] * 3

    def triplet_forward(first, after):
        return call(
            functools.partial(triplet_forward_kernel, orders=orders), f"triplet_forward{first}", (steps,),
            [whole(table.shape)] * 2 + slots_at(first) + [whole(w_bil_t.shape)],
            [columns_of(bil_rows, tile), columns_of(trip_width, tile)],
            [out(bil_rows, half // 2), out(trip_width, half // 2)],
            [
                pltpu.VMEM(table_shape, bf16),
                pltpu.VMEM((2, slots, trip_width, LANES), f32),
                pltpu.VMEM((orders, slots, tile), f32),
                pltpu.VMEM((2, *w_bil_t.shape), bf16),
            ],
            (role_arg, table, table_recv, t_index, t_cos, t_live, w_bil_t), scalars=1, flops=5 * 10**9, after=after,
        )

    z_one, mid_one = triplet_forward(0, [])
    z_two, mid_two = triplet_forward(steps, [quad_own, halo_own, mid_one])

    atom_recv = small_recv[:atoms]
    pool_rows = atoms + halo_count
    square = pltpu.VMEM((2, width, width), bf16)
    up_scratch = pltpu.VMEM((2, narrow, width), bf16)
    rad_scratch = pltpu.VMEM((2, radial_width, width), bf16)
    main_weights = (w_trip_up, w_quad_up, w_res_one, w_res_two, w_atom_edge, w_edge_rbf)
    main_small = (target, quad_own, quad_recv, atom_embed, atom_recv, halo_own, halo_recv)
    mid, joined, pre_one, pre_two, pre_six, new_own, new_send, coll_own = call(
        main_forward_kernel, "main_forward", grid,
        [rows_of(tile, width), *halves_of(trip_width), mine_rbf, mine_ends]
        + [whole(x.shape) for x in main_small + main_weights],
        [columns_of(narrow, tile)] + [rows_of(tile, width)] * 4 + [mine, rows_of(tile, half_width), whole((atoms, width))],
        [out(narrow, half)] + [out(half, width)] * 4 + [out(edges, half_width), out(half, half_width), out(atoms, width)],
        [up_scratch, square, square, square, rad_scratch, pltpu.VMEM((2, pool_rows + atoms, width), bf16), pltpu.VMEM((2 * quad_width, quad_count), bf16)],
        (role_arg, emb, mid_one, mid_two, rbf_mine, ends, *main_small, *main_weights), scalars=1, flops=8 * 10**9,
    )
    coll_recv = swap(coll_own)
    new_recv = swap(new_send)

    edge_rows = padded_rows(w_atom_edge.shape[0] + radial_width + w_edge_atom.size // width + w_out.size // width)
    atom_args = (coll_own, coll_recv, small_own, small_recv, halo_own, halo_recv, w_atom_edge, w_edge_rbf, w_edge_atom, w_out)
    res_grad, edge_keep, edge_send, pool_grad_own, pool_grad_send, atom_out, feat_out = call(
        functools.partial(edge_backward_kernel, scale=(atoms / edges) ** 0.5, codes=codes), "edge_backward", grid,
        [rows_of(tile, width)] * 3 + [mine_rbf, mine_ends, mine, rows_of(tile, half_width)] + [whole(x.shape) for x in atom_args],
        [rows_of(tile, width), whole((edge_rows // 2, width)), whole((edge_rows // 2, width)),
         whole((pool_rows, half_atom)), whole((pool_rows, half_atom)), whole((atoms, half_atom)), whole((atoms, half_atom))],
        [out(half, width), out(edge_rows // 2, width), out(edge_rows // 2, width),
         out(pool_rows, half_atom), out(pool_rows, half_atom), out(atoms, half_atom), out(atoms, half_atom)],
        [square, rad_scratch, pltpu.VMEM((2, atoms, width), bf16), pltpu.VMEM((pool_rows + atoms, width), f32), pltpu.VMEM((atoms, atom_width), f32),
         pltpu.VMEM((edge_rows, width), f32)],
        (place_at, joined, pre_two, pre_six, rbf_mine, ends, cot_mine, cot_recv, *atom_args), scalars=1, flops=8 * 10**9,
    )
    edge_blocks = phase([("add", [edge_keep, swap(edge_send)], plane[1])], "phase_one")[0]
    edge_parts = middle_stages(send_blocks(edge_blocks, plane), line[:-1], "edge_middle")

    res_rows = padded_rows(2 * width + narrow + w_bil_t.size // width)
    res_weights = (w_trip_up, w_quad_up, w_res_one, w_res_two)
    sum_grad, mid_grad, res_keep, res_send, back_part = call(
        functools.partial(residual_backward_kernel, codes=codes), "residual_backward", grid,
        [rows_of(tile, width)] * 3 + [columns_of(narrow, tile), *halves_of(bil_rows), whole(target.shape), rows_of(tile, width)]
        + [whole(w.shape) for w in res_weights],
        [rows_of(tile, width), columns_of(narrow, tile), whole((res_rows // 2, width)), whole((res_rows // 2, width)), whole((quad_width, quad_count))],
        [out(half, width), out(narrow, half), out(res_rows // 2, width), out(res_rows // 2, width), out(quad_width, quad_count)],
        [up_scratch, square, square, pltpu.VMEM((res_rows, width), f32), pltpu.VMEM(w_bil_t.shape, f32)],
        (place_at, joined, pre_one, pre_two, mid, z_one, z_two, target, res_grad, *res_weights), scalars=1, flops=8 * 10**9, after=edge_blocks,
    )
    sums_shape = (2 * CLASSES * trip_width, edges // CLASSES)

    def triplet_backward(first, held, after):
        return call(
            functools.partial(triplet_backward_kernel, orders=orders), f"triplet_backward{first}", (steps,),
            [pl.BlockSpec((narrow, tile), lambda i, r: (0, first + i))] + slots_at(first) + [whole(w_bil_t.shape)] + [whole(h.shape) for h in held],
            [whole(sums_shape)],
            [out(*sums_shape)],
            [
                pltpu.VMEM((bil_rows, tile), f32),
                pltpu.VMEM((2, slots, trip_width, LANES), f32),
                pltpu.VMEM((orders, slots, tile), f32),
                pltpu.VMEM((2, *w_bil_t.shape), bf16),
            ],
            (role_arg, mid_grad, t_index, t_cos, t_live, w_bil_t, *held), scalars=1, flops=6 * 10**9, after=after,
        )

    edge_blocks, (res_send,), (back_part,), (pool_grad_send,) = phase(
        [("add", edge_parts, line[-1][1]), ("join", [res_send], 1), ("join", [back_part], 1), ("join", [pool_grad_send], 1)], "phase_two", [sum_grad]
    )
    edge_parts = send_blocks(edge_blocks, line[-1])
    res_recv = swap(res_send)
    held = triplet_backward(0, [], edge_blocks)
    (edge_piece,), res_blocks, (pool_grad,), (back_sum,) = phase(
        [
            ("add", edge_parts, 1),
            ("add", [res_keep, res_recv], plane[1]),
            ("add", [pool_grad_own, swap(pool_grad_send)], 1),
            ("add", [back_part, swap(back_part)], 1),
        ],
        "phase_three", held,
    )
    returned_sent = jnp.concatenate([by_peer(back_sum), pool_grad[atoms:].reshape(peers, -1)], axis=1)
    edge_piece, edge_codes = middle_gathers(edge_piece, line[1:], "edge_middle_gather")
    edge_pieces, edge_lists = spread(edge_piece, edge_codes, line[0])
    res_parts = middle_stages(send_blocks(res_blocks, plane), line[:-1], "res_middle")
    returned = exchange(returned_sent)
    (trip_sums,) = triplet_backward(steps, held, [edge_piece, *res_blocks, returned_sent])
    (edge_piece,), res_blocks = phase([("join", edge_pieces, 1), ("add", res_parts, line[-1][1])], "phase_four", [trip_sums])
    edge_pieces, edge_codes = spread(edge_piece, sum(edge_lists, []), plane)
    res_parts = send_blocks(res_blocks, line[-1])
    back_rows = lax.dynamic_slice_in_dim(returned[:, :cut], role * (peers // 2), peers // 2, axis=0)
    back_own = by_entry(back_rows)
    halo_back = returned[:, cut:].reshape(halo_count, half_atom)
    bil_rows = w_bil_q.shape[1]
    quad_bil, table_keep, table_send = call(
        functools.partial(quad_backward_kernel, orders=orders), "quad_backward", (1,),
        [whole(back_own.shape), whole(z_quad.shape)] + [mine_quad] * 4 + [whole(w_bil_q.shape), whole(trip_sums.shape)],
        [whole(w_bil_q.shape), whole((narrow, half)), whole((narrow, half))],
        [out(*w_bil_q.shape), out(narrow, half), out(narrow, half)],
        [pltpu.VMEM((bil_rows, half_quad), f32), pltpu.VMEM((quad_slots, quad_width, half_quad), f32), pltpu.VMEM((orders, quad_slots, half_quad), f32)],
        (role_arg, back_own, z_quad, q_index, q_cos, q_dih, q_live, w_bil_q, trip_sums), scalars=1, flops=2 * 10**9, limit=SMALL_LIMIT,
        after=[edge_piece, *res_blocks],
    )
    (res_piece,), (table_send,) = phase([("add", res_parts, 1), ("join", [table_send], 1)], "phase_quad", [table_keep])
    table_recv = swap(table_send)
    res_piece, res_codes = middle_gathers(res_piece, line[1:], "res_middle_gather")
    res_pieces, res_lists = spread(res_piece, res_codes, line[0])

    late_rows = padded_rows(2 * radial_width + narrow + w_bil_q.size // width)
    grad_own, grad_send, late_keep, late_send = call(
        functools.partial(final_kernel, codes=[0]), "final", grid,
        [rows_of(tile, width), mine_rbf] + [columns_of(narrow, tile)] * 3 + [rows_of(tile, width)]
        + [whole(x.shape) for x in (quad_bil,) + down_weights],
        [mine, rows_of(tile, half_width)] + [whole((late_rows // 2, width))] * 2,
        [out(edges, half_width), out(half, half_width)] + [out(late_rows // 2, width)] * 2,
        down_scratch + [pltpu.VMEM((late_rows, width), f32)],
        (place_at * jnp.array([1, 0], i32), emb, rbf_mine, pre, table_keep, table_recv, sum_grad, quad_bil, *down_weights), scalars=1, flops=6 * 10**9,
        after=[res_piece],
    )
    grad_recv = swap(grad_send)
    (res_piece,), (late_send,) = phase([("join", res_pieces, 1), ("join", [late_send], 1)], "phase_five", edge_pieces[1:])
    ((late_half,),) = phase([("add", [late_keep, swap(late_send)], 1)], "phase_late")
    late_blocks = scatter_blocks(late_half)
    res_pieces, res_codes = spread(res_piece, sum(res_lists, []), plane)
    edge_full = lax.dynamic_update_slice_in_dim(new_own, new_recv, (1 - role) * half, axis=0)
    g_atom_edge, g_edge_rbf, g_edge_atom, g_out = unpack(
        edge_pieces, edge_codes, place_at, [w_atom_edge.shape, w_edge_rbf.shape, w_edge_atom.shape, w_out.shape],
        ["plain", "plain", "rows", "rows"], "edge_unpack", [late_half],
    )
    late_piece = fold(late_blocks, "late_fold", [g_out, *res_pieces])
    late_all = exchange(jnp.broadcast_to(late_piece[None], late_blocks.shape)).reshape(late_half.shape)
    grad_full = lax.dynamic_update_slice_in_dim(grad_own, grad_recv, (1 - role) * half, axis=0)
    g_two, g_one, g_trip_up, g_quad_up, g_bil_t = unpack(
        res_pieces, res_codes, place_at, [w_res_two.shape, w_res_one.shape, w_trip_up.shape, w_quad_up.shape, w_bil_t.shape],
        ["plain"] * 4 + ["columns"], "res_unpack", [late_piece],
    )
    grad_atom = pool_grad[:atoms] + jnp.zeros((atoms, half_atom), f32).at[halo_send].add(halo_back)
    late_all = phase([("join", [late_all], 1)], "phase_six", [g_one, edge_full, grad_full, grad_atom])[0][0]
    g_trip_rbf, g_quad_rbf, g_down_t, g_down_q, g_bil_q = unpack(
        [late_all], [[0]], place_at * jnp.array([1, 0], i32), [w_trip_rbf.shape, w_quad_rbf.shape, w_down_t.shape, w_down_q.shape, w_bil_q.shape],
        ["plain"] * 4 + ["columns"], "late_unpack",
    )
    return (
        edge_full, atom_out, feat_out, grad_full, grad_atom,
        g_quad_rbf, g_down_q.T, g_bil_q.T, g_quad_up, g_trip_rbf, g_down_t.T, g_bil_t.T, g_trip_up,
        g_one, g_two, g_atom_edge, g_edge_rbf, g_edge_atom, g_out,
    )


def solution(mesh):
    whole_spec, rows_spec, both_spec = P(), P("edge"), P("edge", "pair")
    in_specs = (both_spec, both_spec) + (rows_spec,) * 12 + (whole_spec,) * 14 + (both_spec,) * 3
    out_specs = (both_spec,) * 5 + (whole_spec,) * 14
    return jax.shard_map(local, mesh=mesh, in_specs=in_specs, out_specs=out_specs, check_vma=False)
```

```python
import functools

import jax
import jax.numpy as jnp
from jax import lax
from jax.experimental import pallas as pl
from jax.experimental.pallas import tpu as pltpu
from jax.sharding import PartitionSpec as P

f32, bf16, i32 = jnp.float32, jnp.bfloat16, jnp.int32
root_third = 0.5773502691896258
root_half = 0.7071067811865476
LANES = 128
CLASSES = 4
VMEM_LIMIT = 30 * 2**20
SMALL_LIMIT = 24 * 2**20


def split(x):
    high = x.astype(bf16)
    return high, (x - high.astype(f32)).astype(bf16)


def dot(left, right, dims):
    return lax.dot_general(left, right, (dims, ((), ())), preferred_element_type=f32)


NN = ((1,), (0,))
NT = ((1,), (1,))
TN = ((0,), (0,))


def dot3(left, right, dims=NN):
    lh, ll = left if isinstance(left, tuple) else split(left)
    rh, rl = right if isinstance(right, tuple) else split(right)
    at, to = dims[0][0], dims[1][0]
    depth, rows = lh.shape[at], lh.shape[1 - at]
    if (at == 0 or depth % LANES == 0) and (to == 0 or depth % LANES == 0):
        if 3 * depth <= 2 * LANES:
            return dot(jnp.concatenate([lh, lh, ll], axis=at), jnp.concatenate([rh, rl, rh], axis=to), dims)
        if 2 * depth <= 2 * LANES:
            return dot(jnp.concatenate([lh, ll], axis=at), jnp.concatenate([rh, rh], axis=to), dims) + dot(lh, rl, dims)
    if at == 1 and rows <= LANES:
        both = dot(jnp.concatenate([lh, ll], axis=0), rh, dims)
        return both[:rows] + both[rows:] + dot(lh, rl, dims)
    return dot(lh, rh, dims) + dot(lh, rl, dims) + dot(ll, rh, dims)


def pick(onehot, right, dims=NN):
    rh, rl = right if isinstance(right, tuple) else split(right)
    return dot(onehot, rh, dims) + dot(onehot, rl, dims)


def sigmoid(v):
    return 0.5 * jnp.tanh(0.5 * v) + 0.5


def silu(v):
    return v * sigmoid(v)


def silu_grad(v):
    s = sigmoid(v)
    return s * (1.0 + v * (1.0 - s))


def as_bf16(mask):
    return mask.astype(f32).astype(bf16)


def legendre_steps(cosine, orders):
    before, now = jnp.ones_like(cosine), cosine
    yield before
    yield now
    for order in range(1, orders - 1):
        before, now = now, ((2 * order + 1) / (order + 1)) * cosine * now - (order / (order + 1)) * before
        yield now


def class_table(own, other, classes):
    per = classes // 2
    step = own.shape[1] // per
    parts = []
    for block in (own, other):
        high, low = split(block)
        for q in range(per):
            parts += [high[:, q * step : (q + 1) * step], low[:, q * step : (q + 1) * step]]
    return jnp.concatenate(parts, axis=0)


def gather_classes(table, index, classes, width):
    step = table.shape[1]
    shift = step.bit_length() - 1
    slots = index.shape[1]
    onehot = as_bf16(lax.broadcasted_iota(i32, (step, slots), 0) == (index & (step - 1)))
    found = dot(table, onehot, NN)
    kind = index >> shift
    out = found[0:width] + found[width : 2 * width]
    for q in range(1, classes):
        base = q * 2 * width
        out = jnp.where(kind >= q, found[base : base + width] + found[base + width : base + 2 * width], out)
    return out


def scatter_classes(values, indices, classes, step):
    shift = step.bit_length() - 1
    lefts, rights = [], []
    for value, index in zip(values, indices):
        width, slots = value.shape
        high, low = split(value)
        both = jnp.concatenate([high, low], axis=0)
        kind = jnp.broadcast_to(index >> shift, (2 * width, slots))
        lefts.append(jnp.concatenate([jnp.where(kind == q, both, jnp.zeros((), bf16)) for q in range(classes)], axis=0))
        rights.append(as_bf16(lax.broadcasted_iota(i32, (step, slots), 0) == (index & (step - 1))))
    return dot(jnp.concatenate(lefts, axis=1), jnp.concatenate(rights, axis=1), NT)


def unfold_classes(sums, classes, width):
    parts = []
    for q in range(classes):
        base = q * 2 * width
        parts.append(sums[base : base + width] + sums[base + width : base + 2 * width])
    return jnp.concatenate(parts, axis=1)


def joined_halves(zero, mine, theirs, axis=1):
    return jnp.concatenate([jnp.where(zero, mine, theirs), jnp.where(zero, theirs, mine)], axis=axis)


def down_kernel(role, own, recv, rbf, w_trip_rad, w_quad_rad, w_trip, w_quad, emb_out, pre_out, table_out, rad, down_t, down_q):
    width = w_trip_rad.shape[1]

    @pl.when(pl.program_id(0) == 0)
    def _():
        rad[0, :, :width], rad[1, :, :width] = split(w_trip_rad[...])
        rad[0, :, width:], rad[1, :, width:] = split(w_quad_rad[...])
        down_t[0], down_t[1] = split(w_trip[...])
        down_q[0], down_q[1] = split(w_quad[...])

    emb = joined_halves(role[0] == 0, own[...], recv[...])
    emb_out[...] = emb
    radial = dot3(rbf[...], (rad[0], rad[1]))
    pre = jnp.concatenate(
        [
            dot3((down_t[0], down_t[1]), emb * radial[:, :width], NT),
            dot3((down_q[0], down_q[1]), emb * radial[:, width:], NT),
        ],
        axis=0,
    )
    pre_out[...] = pre
    table_out[...] = silu(pre)


def quad_forward_kernel(role, own, other, index, cosine, dihedral, live, w_bil, z_out, rows_out, sel, sel2, basis, *, orders, base):
    slots_k, rows = index.shape
    width = w_bil.shape[0]
    zero = role[0] == 0
    mine, theirs = own[base : base + width, :], other[base : base + width, :]
    table = class_table(jnp.where(zero, mine, theirs), jnp.where(zero, theirs, mine), 2 * CLASSES)
    alive = live[...].astype(f32)
    for order, series in enumerate(legendre_steps(cosine[...], orders)):
        basis[order] = series * alive
    for k in range(slots_k):
        picked = gather_classes(table, index[k : k + 1, :], 2 * CLASSES, width)
        sel[k] = picked
        sel2[k] = picked * dihedral[k : k + 1, :]
    groups = width // 8
    for t in range(rows // LANES):
        at = slice(t * LANES, (t + 1) * LANES)
        for part, source in enumerate((sel, sel2)):
            for order_at in range(0, orders, 8):
                sums = {}
                for k in range(slots_k):
                    chosen = [source[k, g * 8 : g * 8 + 8, at] for g in range(groups)]
                    for order in range(8):
                        weight = jnp.broadcast_to(basis[order_at + order, k : k + 1, at], (8, LANES))
                        for g in range(groups):
                            term = weight * chosen[g]
                            sums[order, g] = term if k == 0 else sums[order, g] + term
                for (order, g), total in sums.items():
                    row = (part * orders + order_at + order) * width + g * 8
                    z_out[row : row + 8, at] = total
    rows_out[...] = dot3(w_bil[...], z_out[...])


def triplet_forward_kernel(role, own, other, index, cosine, live, w_bil, z_out, mid_out, table, sel, basis, bil, *, orders):
    slots_k, tile = index.shape
    width = w_bil.shape[0]

    @pl.when(pl.program_id(0) == 0)
    def _():
        zero = role[0] == 0
        mine, theirs = own[0:width, :], other[0:width, :]
        table[...] = class_table(jnp.where(zero, mine, theirs), jnp.where(zero, theirs, mine), CLASSES)
        bil[0], bil[1] = split(w_bil[...])

    alive = live[...].astype(f32)
    for order, series in enumerate(legendre_steps(cosine[...], orders)):
        basis[order] = series * alive

    def gather(at, k, into):
        where_to = jnp.concatenate([index[k : k + 1, at], index[k + 1 : k + 2, at]], axis=1)
        found = gather_classes(table[...], where_to, CLASSES, width)
        sel[into, k] = found[:, :LANES]
        sel[into, k + 1] = found[:, LANES:]

    def combine(at, first, source):
        sums = {}
        for k in range(slots_k):
            chosen = [sel[source, k, g * 8 : g * 8 + 8, :] for g in (first, first + 1)]
            for order in range(orders):
                weight = jnp.broadcast_to(basis[order, k : k + 1, at], (8, LANES))
                for g in range(2):
                    term = weight * chosen[g]
                    sums[order, g] = term if k == 0 else sums[order, g] + term
        for (order, g), total in sums.items():
            row = order * width + (first + g) * 8
            z_out[row : row + 8, at] = total

    firsts = range(0, width // 8, 2)
    turns = slots_k // 2 // len(firsts)
    columns = lambda c: pl.ds(pl.multiple_of(c * LANES, LANES), LANES)
    for k in range(0, slots_k, 2):
        gather(columns(0), k, 0)

    def step_columns(c, carry):
        for n, first in enumerate(firsts):
            for k in range(n * turns, (n + 1) * turns):
                gather(columns(c), 2 * k, c & 1)
            combine(columns(c - 1), first, 1 - (c & 1))
        return carry

    lax.fori_loop(1, tile // LANES, step_columns, 0)
    for first in firsts:
        combine(columns(tile // LANES - 1), first, (tile // LANES - 1) & 1)
    mid_out[...] = dot3((bil[0], bil[1]), z_out[...])


def laid(pairs):
    return tuple(jnp.concatenate([p[n] for p in pairs], axis=0) for n in range(2))


def row_blocks(tile):
    return [slice(n * tile // 2, (n + 1) * tile // 2) for n in range(2)]


def edge_members(ends, pool_rows, atoms, tile):
    row = lax.broadcasted_iota(i32, (pool_rows + atoms, tile), 0)
    return as_bf16(row == jnp.where(row < pool_rows, ends[0:1, :], ends[1:2, :] + pool_rows))


def entry_members(role, target, step, tile, half):
    row = lax.broadcasted_iota(i32, (tile, target.shape[1]), 0) + (step * tile + role[0] * half)
    return as_bf16(row == target[...])


def main_forward_kernel(
    role, emb, mid_one, mid_two, rbf, ends, target, quad_own, quad_recv, atom_own, atom_recv, halo_own, halo_recv,
    w_trip_up, w_quad_up, w_one, w_two, w_edge, w_rbf,
    mid_out, joined_out, one_out, two_out, six_out, new_own, new_send, collected,
    up, one, two, three, rad, pool_w, quad_hl,
):
    step = pl.program_id(0)
    tile = emb.shape[0]
    half_rows = tile * pl.num_programs(0)
    atoms = atom_own.shape[0]
    pool_rows = atoms + halo_own.shape[0]
    atom_width = 2 * atom_own.shape[1]
    trip_width = w_trip_up.shape[0]
    zero = role[0] == 0

    @pl.when(step == 0)
    def _():
        up[0, :trip_width], up[1, :trip_width] = split(w_trip_up[...])
        up[0, trip_width:], up[1, trip_width:] = split(w_quad_up[...])
        one[0], one[1] = split(w_one[...])
        two[0], two[1] = split(w_two[...])
        three[0], three[1] = split(w_edge[2 * atom_width :, :])
        rad[0], rad[1] = split(w_rbf[...])
        atom_rows = joined_halves(zero, atom_own[...], atom_recv[...])
        pool = jnp.concatenate([atom_rows, joined_halves(zero, halo_own[...], halo_recv[...])], axis=0)
        projected = jnp.concatenate(
            [dot3(pool, w_edge[0:atom_width, :]), dot3(atom_rows, w_edge[atom_width : 2 * atom_width, :])], axis=0
        )
        pool_w[0], pool_w[1] = split(projected)
        high, low = split(quad_own[...] + quad_recv[...])
        quad_hl[...] = jnp.concatenate([high, low], axis=0)

    found = dot(quad_hl[...], entry_members(role, target, step, tile, half_rows), NT)
    width = found.shape[0] // 2
    mid_trip = jnp.where(step < pl.num_programs(0) // 2, mid_one[...], mid_two[...])
    mid = jnp.concatenate([mid_trip, found[:width] + found[width:]], axis=0)
    mid_out[...] = mid
    member = edge_members(ends, pool_rows, atoms, tile)
    blocks = row_blocks(tile)
    joined = [(emb[at, :] + dot3(mid[:, at], (up[0], up[1]), TN)) * root_third for at in blocks]
    pre_one = [dot3(x, (one[0], one[1])) for x in joined]
    pre_two = [dot3(silu(x), (two[0], two[1])) for x in pre_one]
    residual = [(x + silu(y)) * root_half for x, y in zip(joined, pre_two)]
    pre_six = [pick(member[:, at], (pool_w[0], pool_w[1]), TN) + dot3(x, (three[0], three[1])) for at, x in zip(blocks, residual)]
    edge_new = [(x + silu(y)) * root_half for x, y in zip(residual, pre_six)]
    half = emb.shape[1] // 2
    part = 0.0
    for n, at in enumerate(blocks):
        joined_out[at, :] = joined[n]
        one_out[at, :] = pre_one[n]
        two_out[at, :] = pre_two[n]
        six_out[at, :] = pre_six[n]
        new_own[at, :] = jnp.where(zero, edge_new[n][:, :half], edge_new[n][:, half:])
        new_send[at, :] = jnp.where(zero, edge_new[n][:, half:], edge_new[n][:, :half])
        part = part + pick(member[pool_rows:, at], edge_new[n] * dot3(rbf[at, :], (rad[0], rad[1])))

    @pl.when(step == 0)
    def _():
        collected[...] = part

    @pl.when(step > 0)
    def _():
        collected[...] += part


def give_halves(place_at, total, keep, send, codes):
    half = keep.shape[0]
    rows = half // len(codes)
    for side, target in ((place_at[0], keep), (1 - place_at[0], send)):
        for n, code in enumerate(codes):
            at = pl.multiple_of(side * half + (place_at[1] ^ code) * rows, 8)
            target[n * rows : (n + 1) * rows, :] = total[pl.ds(at, rows), :]


def side_by_side(x, width):
    parts = width // x.shape[1]
    rows = x.shape[0] // parts
    return jnp.concatenate([x[q * rows : (q + 1) * rows] for q in range(parts)], axis=1)


def edge_backward_kernel(
    role, joined, pre_two_ref, pre_six_ref, rbf, ends, cot_own, cot_recv,
    coll_own, coll_recv, small_own, small_recv, halo_own, halo_recv,
    w_edge, w_rbf, w_edge_atom, w_out,
    res_grad_out, keep, send, pool_grad_own, pool_grad_send, atom_out, feat_out,
    three, rad, coll_grad, pool_sum, direct, grads,
    *, scale, codes,
):
    step = pl.program_id(0)
    last = pl.num_programs(0) - 1
    tile, edge_width = joined.shape
    half = small_own.shape[1]
    atoms = small_own.shape[0] // 3
    atom_width = 2 * half
    pool_rows = atoms + halo_own.shape[0]
    zero = role[0] == 0
    at_rbf = w_edge.shape[0]
    at_atom = at_rbf + w_rbf.shape[0]
    at_last = at_atom + w_edge_atom.shape[0] * atom_width // edge_width
    at_end = at_last + atom_width * atom_width // edge_width

    @pl.when(step == 0)
    def _():
        three[0], three[1] = split(w_edge[2 * atom_width :, :])
        rad[0], rad[1] = split(w_rbf[...])
        mine, theirs = small_own[...], small_recv[...]
        atom_rows = joined_halves(zero, mine[:atoms], theirs[:atoms])
        cot_atom = joined_halves(zero, mine[atoms : 2 * atoms], theirs[atoms : 2 * atoms])
        cot_feat = joined_halves(zero, mine[2 * atoms :], theirs[2 * atoms :])
        total = (coll_own[...] + coll_recv[...]) * scale
        w_a, w_f = split(w_edge_atom[...]), split(w_out[...])
        pre_atom = dot3(total, w_a)
        atom_new = (atom_rows + silu(pre_atom)) * root_half
        pre_feat = dot3(atom_new, w_f)
        feature = silu(pre_feat)
        atom_out[...] = jnp.where(zero, atom_new[:, :half], atom_new[:, half:])
        feat_out[...] = jnp.where(zero, feature[:, :half], feature[:, half:])
        feat_grad = cot_feat * silu_grad(pre_feat)
        grads[at_last:at_end, :] = side_by_side(0.5 * dot3(atom_new, feat_grad, TN), edge_width)
        atom_grad = (cot_atom + dot3(feat_grad, w_f, NT)) * root_half
        direct[...] = 0.5 * atom_grad
        pre_grad = atom_grad * silu_grad(pre_atom)
        grads[at_atom:at_last, :] = side_by_side(0.5 * dot3(total, pre_grad, TN), edge_width)
        coll_grad[0], coll_grad[1] = split(dot3(pre_grad, w_a, NT) * scale)
        grads[0:at_atom, :] = jnp.zeros((at_atom, grads.shape[1]), f32)
        if grads.shape[0] > at_end:
            grads[at_end:, :] = jnp.zeros((grads.shape[0] - at_end, grads.shape[1]), f32)
        pool_sum[...] = jnp.zeros_like(pool_sum)

    member = edge_members(ends, pool_rows, atoms, tile)
    blocks = row_blocks(tile)
    six = [pre_six_ref[at, :] for at in blocks]
    s_six = [sigmoid(x) for x in six]
    residual = [(joined[at, :] + silu(pre_two_ref[at, :])) * root_half for at in blocks]
    edge_new = [(x + y * s) * root_half for x, y, s in zip(residual, six, s_six)]
    radial = split(rbf[...])
    weighted_grad = [pick(member[pool_rows:, at], (coll_grad[0], coll_grad[1]), TN) for at in blocks]
    new_grad = [
        (joined_halves(zero, cot_own[at, :], cot_recv[at, :]) + w * dot3((radial[0][at], radial[1][at]), (rad[0], rad[1]))) * root_half
        for at, w in zip(blocks, weighted_grad)
    ]
    six_split = [split(g * (s * (1.0 + y * (1.0 - s)))) for g, y, s in zip(new_grad, six, s_six)]
    for at, g, pair in zip(blocks, new_grad, six_split):
        res_grad_out[at, :] = (g + dot3(pair, (three[0], three[1]), NT)) * root_half
    grads[at_rbf:at_atom, :] += dot3(radial, laid([split(w * x) for w, x in zip(weighted_grad, edge_new)]), TN)
    six_all = laid(six_split)
    pool_sum[...] += pick(member, six_all)
    grads[2 * atom_width : at_rbf, :] += dot3(laid([split(x) for x in residual]), six_all, TN)

    @pl.when(step == last)
    def _():
        atom_rows = joined_halves(zero, small_own[:atoms, :], small_recv[:atoms, :])
        pool = jnp.concatenate([atom_rows, joined_halves(zero, halo_own[...], halo_recv[...])], axis=0)
        w_src, w_dst = split(w_edge[0:atom_width, :]), split(w_edge[atom_width : 2 * atom_width, :])
        src_split, dst_split = split(pool_sum[0:pool_rows, :]), split(pool_sum[pool_rows:, :])
        grads[0:atom_width, :] = dot3(pool, src_split, TN)
        grads[atom_width : 2 * atom_width, :] = dot3(atom_rows, dst_split, TN)
        from_src = dot3(src_split, w_src, NT)
        from_atoms = from_src[0:atoms] + dot3(dst_split, w_dst, NT) + direct[...]
        result = jnp.concatenate([from_atoms, from_src[atoms:]], axis=0)
        pool_grad_own[...] = jnp.where(zero, result[:, :half], result[:, half:])
        pool_grad_send[...] = jnp.where(zero, result[:, half:], result[:, :half])
        give_halves(role, grads, keep, send, codes)


def residual_backward_kernel(
    role, joined, pre_one_ref, pre_two_ref, mid_ref, z_one, z_two, target, res_grad_ref,
    w_trip_up, w_quad_up, w_one, w_two,
    sum_grad_out, mid_grad_out, keep, send, back,
    up, one, two, grads, bil_grad,
    *, codes,
):
    step = pl.program_id(0)
    tile, width = joined.shape
    half_rows = tile * pl.num_programs(0)
    trip_width = w_trip_up.shape[0]
    narrow = up.shape[1]
    at_bil = 2 * width + narrow

    @pl.when(step == 0)
    def _():
        up[0, :trip_width], up[1, :trip_width] = split(w_trip_up[...])
        up[0, trip_width:], up[1, trip_width:] = split(w_quad_up[...])
        one[0], one[1] = split(w_one[...])
        two[0], two[1] = split(w_two[...])
        grads[...] = jnp.zeros_like(grads)
        bil_grad[...] = jnp.zeros_like(bil_grad)
        back[...] = jnp.zeros_like(back)

    blocks = row_blocks(tile)

    res_grad = [res_grad_ref[at, :] for at in blocks]
    two_split = [split(grad * silu_grad(pre_two_ref[at, :])) for grad, at in zip(res_grad, blocks)]
    pre_one = [pre_one_ref[at, :] for at in blocks]
    s_one = [sigmoid(pre) for pre in pre_one]
    hidden = [split(pre * s) for pre, s in zip(pre_one, s_one)]
    one_split = [
        split(dot3(grad, (two[0], two[1]), NT) * (s * (1.0 + pre * (1.0 - s)))) for grad, pre, s in zip(two_split, pre_one, s_one)
    ]
    grads[0:width, :] += dot3(laid(hidden), laid(two_split), TN)
    sum_grad = [(grad + dot3(inner, (one[0], one[1]), NT)) * root_third for grad, inner in zip(res_grad, one_split)]
    grads[width : 2 * width, :] += dot3(joined[...], laid(one_split), TN)
    for at, grad in zip(blocks, sum_grad):
        sum_grad_out[at, :] = grad
    sum_split = laid([split(grad) for grad in sum_grad])
    grads[2 * width : at_bil, :] += dot3(mid_ref[...], sum_split, NN)
    mid_grad = dot3((up[0], up[1]), sum_split, NT)
    mid_grad_out[...] = mid_grad
    mid_high, mid_low = split(mid_grad)
    z = jnp.where(step < pl.num_programs(0) // 2, z_one[...], z_two[...])
    bil_grad[...] += dot3((mid_high[:trip_width], mid_low[:trip_width]), z, NT)
    found = dot(jnp.concatenate([mid_high[trip_width:], mid_low[trip_width:]], axis=0), entry_members(role, target, step, tile, half_rows), NN)
    rows = narrow - trip_width
    back[...] += found[:rows] + found[rows:]

    @pl.when(step == pl.num_programs(0) - 1)
    def _():
        for q in range(bil_grad.shape[1] // width):
            grads[at_bil + q * trip_width : at_bil + (q + 1) * trip_width, :] = bil_grad[:, q * width : (q + 1) * width]
        give_halves(role, grads, keep, send, codes)


def triplet_backward_kernel(role, mid_grad, index, cosine, live, w_bil, *refs, orders):
    held, (sums, zg, sg, basis, bil) = refs[:-5], refs[-5:]
    step = pl.program_id(0)
    slots_k, tile = index.shape
    width = w_bil.shape[0]
    classes_step = sums.shape[1]

    @pl.when(step == 0)
    def _():
        bil[0], bil[1] = split(w_bil[...])
        sums[...] = held[0][...] if held else jnp.zeros_like(sums)

    alive = live[...].astype(f32)
    for order, series in enumerate(legendre_steps(cosine[...], orders)):
        basis[order] = series * alive
    grad_split = split(mid_grad[0:width, :])
    zg[...] = dot3((bil[0], bil[1]), grad_split, TN)

    def combine(at, first, into):
        totals = {}
        for order in range(orders):
            row = order * width + first * 8
            got = [zg[row + g * 8 : row + g * 8 + 8, at] for g in range(2)]
            for k in range(slots_k):
                weight = jnp.broadcast_to(basis[order, k : k + 1, at], (8, LANES))
                for g in range(2):
                    term = weight * got[g]
                    totals[k, g] = term if order == 0 else totals[k, g] + term
        for (k, g), total in totals.items():
            sg[into, k, (first + g) * 8 : (first + g) * 8 + 8, :] = total

    def scatter(at, first, source):
        slots_at = range(first, first + slots_k // 2)
        sums[...] += scatter_classes(
            [sg[source, k] for k in slots_at], [index[k : k + 1, at] for k in slots_at], CLASSES, classes_step
        )

    firsts = range(0, width // 8, 2)
    columns = lambda c: pl.ds(pl.multiple_of(c * LANES, LANES), LANES)
    for first in firsts:
        combine(columns(0), first, 0)

    def step_columns(c, carry):
        for n, first in enumerate(firsts):
            if n % 2 == 0:
                scatter(columns(c - 1), n // 2 * (slots_k // 2), 1 - (c & 1))
            combine(columns(c), first, c & 1)
        return carry

    lax.fori_loop(1, tile // LANES, step_columns, 0)
    for n in range(2):
        scatter(columns(tile // LANES - 1), n * (slots_k // 2), (tile // LANES - 1) & 1)


def quad_backward_kernel(role, own, z, index, cosine, dihedral, live, w_bil, trip_sums, bil_grad, keep, send, zg, sg, basis, *, orders):
    slots_k, rows = index.shape
    width = w_bil.shape[0]
    edges = trip_sums.shape[1] * CLASSES
    trip_width = trip_sums.shape[0] // (2 * CLASSES)
    zero = role[0] == 0
    alive = live[...].astype(f32)
    for order, series in enumerate(legendre_steps(cosine[...], orders)):
        basis[order] = series * alive
    grad_split = split(own[...])
    bil_grad[...] = dot3(grad_split, z[...], NT)
    zg[...] = dot3(w_bil[...], grad_split, TN)
    groups = width // 8
    for t in range(rows // LANES):
        at = slice(t * LANES, (t + 1) * LANES)
        for g in range(groups):
            plain, turned = {}, {}
            for order in range(orders):
                one = zg[order * width + g * 8 : order * width + g * 8 + 8, at]
                two = zg[(orders + order) * width + g * 8 : (orders + order) * width + g * 8 + 8, at]
                for k in range(slots_k):
                    weight = jnp.broadcast_to(basis[order, k : k + 1, at], (8, LANES))
                    plain[k] = weight * one if order == 0 else plain[k] + weight * one
                    turned[k] = weight * two if order == 0 else turned[k] + weight * two
            for k in range(slots_k):
                sg[k, g * 8 : g * 8 + 8, at] = plain[k] + turned[k] * jnp.broadcast_to(dihedral[k : k + 1, at], (8, LANES))
    step = edges // (2 * CLASSES)
    sums = scatter_classes([sg[k] for k in range(slots_k)], [index[k : k + 1, :] for k in range(slots_k)], 2 * CLASSES, step)
    total = jnp.concatenate([unfold_classes(trip_sums[...], CLASSES, trip_width), unfold_classes(sums, 2 * CLASSES, width)], axis=0)
    half = edges // 2
    keep[...] = jnp.where(zero, total[:, :half], total[:, half:])
    send[...] = jnp.where(zero, total[:, half:], total[:, :half])


def final_kernel(
    role, emb_ref, rbf, pre_ref, table_own, table_recv, sum_grad, quad_bil, w_trip_rad, w_quad_rad, w_trip, w_quad,
    grad_own, grad_send, keep, send,
    rad, down_t, down_q, total,
    *, codes,
):
    step = pl.program_id(0)
    zero = role[0] == 0
    radial_rows, width = w_trip_rad.shape
    trip_width, quad_width = w_trip.shape[0], w_quad.shape[0]
    at_quad_rad = radial_rows
    at_trip = 2 * radial_rows
    at_quad = at_trip + trip_width
    at_quad_bil = at_quad + quad_width
    at_end = at_quad_bil + quad_width * quad_bil.shape[1] // width

    @pl.when(step == 0)
    def _():
        rad[0, :, :width], rad[1, :, :width] = split(w_trip_rad[...])
        rad[0, :, width:], rad[1, :, width:] = split(w_quad_rad[...])
        down_t[0], down_t[1] = split(w_trip[...])
        down_q[0], down_q[1] = split(w_quad[...])
        total[...] = jnp.zeros_like(total)
        rows = quad_bil.shape[0]
        for q in range(quad_bil.shape[1] // width):
            total[at_quad_bil + q * rows : at_quad_bil + (q + 1) * rows, :] = quad_bil[:, q * width : (q + 1) * width]

    emb = emb_ref[...]
    radial_split = split(rbf[...])
    radial = dot3(radial_split, (rad[0], rad[1]))
    pre_grad = (table_own[...] + table_recv[...]) * silu_grad(pre_ref[...])
    trip_split, quad_split = split(pre_grad[:trip_width]), split(pre_grad[trip_width:])
    trip_radial, quad_radial = radial[:, :width], radial[:, width:]
    total[at_trip:at_quad, :] += dot3(trip_split, emb * trip_radial)
    total[at_quad:at_quad_bil, :] += dot3(quad_split, emb * quad_radial)
    trip_mixed = dot3(trip_split, (down_t[0], down_t[1]), TN)
    quad_mixed = dot3(quad_split, (down_q[0], down_q[1]), TN)
    grad = sum_grad[...] + trip_mixed * trip_radial + quad_mixed * quad_radial
    half = width // 2
    grad_own[...] = jnp.where(zero, grad[:, :half], grad[:, half:])
    grad_send[...] = jnp.where(zero, grad[:, half:], grad[:, :half])
    total[0:at_quad_rad, :] += dot3(radial_split, trip_mixed * emb, TN)
    total[at_quad_rad:at_trip, :] += dot3(radial_split, quad_mixed * emb, TN)

    @pl.when(step == pl.num_programs(0) - 1)
    def _():
        give_halves(role, total, keep, send, codes)


def fold_kernel(source, target):
    target[...] = jnp.sum(source[...], axis=0)


def fold(blocks, name, after=(), whole_after=()):
    return call(fold_kernel, name, (1,), [whole(blocks.shape)], [whole(blocks.shape[1:])], [out(*blocks.shape[1:])], [], (blocks,), after=after, whole_after=whole_after, limit=SMALL_LIMIT)[0]


def exchange(blocks):
    return lax.all_to_all(blocks, "edge", split_axis=0, concat_axis=0, tiled=True)


def scatter_blocks(rows):
    return exchange(rows.reshape(lax.axis_size("edge"), -1, rows.shape[1]))


def partners(bits, axis="edge"):
    return [(i, i ^ bits) for i in range(lax.axis_size(axis))]


def edge_stages():
    size, shift, stages = lax.axis_size("edge"), 0, []
    while size > 1:
        radix = 8 if size == 8 else 4 if size % 4 == 0 else 2
        stages.append((shift, radix))
        shift += radix.bit_length() - 1
        size //= radix
    return stages


def padded_rows(rows):
    unit = 2 * 8 * lax.axis_size("edge")
    return -(-rows // unit) * unit


def spread(piece, codes, stage):
    shift, radix = stage
    pieces = [piece] + [lax.ppermute(piece, "edge", partners(j << shift)) for j in range(1, radix)]
    return pieces, [[c ^ (j << shift) for c in codes] for j in range(radix)]


def stage_codes(stages):
    codes = [0]
    for shift, radix in reversed(stages):
        codes = [c ^ (j << shift) for j in range(radix) for c in codes]
    return codes


def phase_kernel(*refs, jobs):
    ins, outs = list(refs[: sum(count for _, count, _ in jobs)]), list(refs[sum(count for _, count, _ in jobs) :])
    for kind, count, blocks in jobs:
        parts, ins = ins[:count], ins[count:]
        targets, outs = outs[:blocks], outs[blocks:]
        if kind == "join":
            rows = parts[0].shape[0]
            for n, part in enumerate(parts):
                targets[0][n * rows : (n + 1) * rows, :] = part[...]
        else:
            rows = parts[0].shape[0] // blocks
            for n, target in enumerate(targets):
                total = parts[0][n * rows : (n + 1) * rows, :]
                for part in parts[1:]:
                    total = total + part[n * rows : (n + 1) * rows, :]
                target[...] = total


def phase(jobs, name, after=(), whole_after=()):
    ins, shapes = [], []
    for kind, parts, blocks in jobs:
        rows, width = parts[0].shape
        ins += parts
        shapes += [(len(parts) * rows, width)] if kind == "join" else [(rows // blocks, width)] * blocks
    got = call(
        functools.partial(phase_kernel, jobs=[(kind, len(parts), blocks) for kind, parts, blocks in jobs]), name, (1,),
        [whole(x.shape) for x in ins], [whole(x) for x in shapes], [out(*x) for x in shapes], [], tuple(ins), after=after, whole_after=whole_after, limit=SMALL_LIMIT,
    )
    results = []
    for _, _, blocks in jobs:
        results.append(got[:blocks])
        got = got[blocks:]
    return results


def send_blocks(blocks, stage):
    shift, radix = stage
    return [blocks[0]] + [lax.ppermute(blocks[j], "edge", partners(j << shift)) for j in range(1, radix)]


def middle_stages(parts, stages, name):
    for at, stage in enumerate(stages):
        parts = send_blocks(phase([("add", parts, stage[1])], f"{name}{at}")[0], stage)
    return parts


def middle_gathers(piece, stages, name):
    codes = [0]
    for at, stage in enumerate(reversed(stages)):
        pieces, lists = spread(piece, codes, stage)
        piece, codes = phase([("join", pieces, 1)], f"{name}{at}")[0][0], sum(lists, [])
    return piece, codes


def unpack_kernel(place_at, *refs, count, codes, layout):
    ins, outs, total = refs[:count], refs[count:-1], refs[-1]
    half = total.shape[0] // 2
    for n, source in enumerate(ins):
        side, listed = codes[n]
        first = jnp.where(place_at[0] == 0, side, 1 - side) * half
        rows = source.shape[0] // len(listed)
        for at, code in enumerate(listed):
            block = place_at[1] ^ code
            total[pl.ds(pl.multiple_of(first + block * rows, 8), rows), :] = source[at * rows : (at + 1) * rows, :]
    at = 0
    for target, kind in zip(outs, layout):
        height, breadth = target.shape
        width = total.shape[1]
        if kind == "plain":
            target[...] = total[at : at + height, :]
            at += height
        elif kind == "rows":
            parts = width // breadth
            rows = height // parts
            for q in range(parts):
                target[q * rows : (q + 1) * rows, :] = total[at : at + rows, q * breadth : (q + 1) * breadth]
            at += rows
        else:
            for q in range(breadth // width):
                target[:, q * width : (q + 1) * width] = total[at : at + height, :]
                at += height


def unpack(pieces, codes, place_at, shapes, layout, name, after=()):
    count = 2 * len(pieces)
    pieces = pieces + [swap(p) for p in pieces]
    codes = [(0, c) for c in codes] + [(1, c) for c in codes]
    rows = sum(p.shape[0] for p in pieces)
    return call(
        functools.partial(unpack_kernel, count=count, codes=codes, layout=layout), name, (1,), [whole(p.shape) for p in pieces],
        [whole(s) for s in shapes], [out(*s) for s in shapes], [pltpu.VMEM((rows, pieces[0].shape[1]), f32)], (place_at, *pieces), scalars=1, whole_after=after, limit=SMALL_LIMIT,
    )


def whole(shape):
    return pl.BlockSpec(shape, lambda *_: (0,) * len(shape))


def rows_of(tile, width):
    return pl.BlockSpec((tile, width), lambda i, *_: (i, 0))


def columns_of(rows, tile):
    return pl.BlockSpec((rows, tile), lambda i, *_: (0, i))


def out(*shape):
    return jax.ShapeDtypeStruct(shape, f32)


def tip(x):
    x = x.reshape(-1, x.shape[-1])
    return x[: min(8, x.shape[0]), : min(LANES, x.shape[1])]


def call(body, name, grid, in_specs, out_specs, out_shape, scratch, args, scalars=0, flops=0, after=(), whole_after=(), limit=VMEM_LIMIT):
    after = [tip(x) for x in after] + list(whole_after)
    first, count = len(args), len(after)

    def run(*refs):
        body(*refs[:first], *refs[first + count :])

    args = (*args, *after)
    in_specs = in_specs + [pl.BlockSpec(memory_space=pl.ANY)] * count
    return pl.pallas_call(
        run,
        name=name,
        grid_spec=pltpu.PrefetchScalarGridSpec(
            num_scalar_prefetch=scalars, grid=grid, in_specs=in_specs, out_specs=out_specs, scratch_shapes=scratch
        ),
        out_shape=out_shape,
        compiler_params=pltpu.CompilerParams(vmem_limit_bytes=limit, dimension_semantics=("arbitrary",) * len(grid)),
        cost_estimate=pl.CostEstimate(flops=max(flops, 1000), bytes_accessed=1000, transcendentals=0),
    )(*args)


def streamed(x):
    return pltpu.with_memory_space_constraint(x, pltpu.HBM)


def swap(x):
    return lax.ppermute(x, "pair", [(0, 1), (1, 0)])


def local(
    edge_embed, atom_embed, edge_rbf, edge_src, edge_dst, halo_send, trip_index, trip_cos, trip_live,
    quad_index, quad_cos, quad_dih, quad_live, quad_target,
    w_quad_rbf, w_quad_down, w_quad_bil, w_quad_up, w_trip_rbf, w_trip_down, w_trip_bil, w_trip_up,
    w_res_one, w_res_two, w_atom_edge, w_edge_rbf, w_edge_atom, w_out,
    cot_edge, cot_atom, cot_feat,
):
    peers = lax.axis_size("edge")
    role = lax.axis_index("pair")
    role_arg = role.astype(i32).reshape(1)
    place_at = jnp.stack([role, lax.axis_index("edge")]).astype(i32)
    stages = edge_stages()
    plane, line = stages[0], stages[1:]
    codes = stage_codes(stages)
    edges, half_width = edge_embed.shape
    half = edges // 2
    width = 2 * half_width
    atoms, half_atom = atom_embed.shape
    radial_width = edge_rbf.shape[1]
    slots = trip_index.shape[1]
    quad_count, quad_slots = quad_index.shape
    half_quad = quad_count // 2
    halo_count = halo_send.shape[0]
    trip_width = w_trip_down.shape[1]
    quad_width = w_quad_down.shape[1]
    narrow = trip_width + quad_width
    orders = w_trip_bil.shape[0] // trip_width
    atom_width = 2 * half_atom
    tile = half // 2
    grid = (half // tile,)

    def other_rows(x):
        return lax.dynamic_slice_in_dim(x, (1 - role) * half, half, axis=0)

    emb_recv = swap(other_rows(edge_embed))
    cot_recv = swap(other_rows(cot_edge))
    small_own = jnp.concatenate([atom_embed, cot_atom, cot_feat], axis=0)
    small_recv = swap(small_own)
    target = quad_target.reshape(1, quad_count)
    ends = jnp.stack([edge_src, edge_dst])
    halo_out = atom_embed[halo_send].reshape(peers, -1)
    t_index, t_cos, t_live = (streamed(x.T) for x in (trip_index, trip_cos, trip_live))
    q_index, q_cos, q_dih, q_live = (streamed(x.T) for x in (quad_index, quad_cos, quad_dih, quad_live))
    w_down_t, w_down_q, w_bil_t, w_bil_q = (streamed(x.T) for x in (w_trip_down, w_quad_down, w_trip_bil, w_quad_bil))
    w_trip_rbf, w_quad_rbf, w_trip_up, w_quad_up = (streamed(x) for x in (w_trip_rbf, w_quad_rbf, w_trip_up, w_quad_up))
    w_res_one, w_res_two, w_atom_edge, w_edge_rbf, w_edge_atom, w_out = (
        streamed(x) for x in (w_res_one, w_res_two, w_atom_edge, w_edge_rbf, w_edge_atom, w_out)
    )
    edge_mine, cot_mine, rbf_mine = streamed(edge_embed), streamed(cot_edge), streamed(edge_rbf)

    mine = pl.BlockSpec((tile, half_width), lambda i, r: (r[0] * grid[0] + i, 0))
    mine_rbf = pl.BlockSpec((tile, radial_width), lambda i, r: (r[0] * grid[0] + i, 0))
    mine_ends = pl.BlockSpec((2, tile), lambda i, r: (0, r[0] * grid[0] + i))
    mine_slots = pl.BlockSpec((slots, tile), lambda i, r: (0, r[0] * grid[0] + i))
    mine_quad = pl.BlockSpec((quad_slots, half_quad), lambda i, r: (0, r[0]))
    down_scratch = [
        pltpu.VMEM((2, radial_width, 2 * width), bf16), pltpu.VMEM((2, trip_width, width), bf16), pltpu.VMEM((2, quad_width, width), bf16),
    ]
    down_weights = (w_trip_rbf, w_quad_rbf, w_down_t, w_down_q)
    emb, pre, table = call(
        down_kernel, "down", grid,
        [mine, rows_of(tile, half_width), mine_rbf] + [whole(w.shape) for w in down_weights],
        [rows_of(tile, width), columns_of(narrow, tile), columns_of(narrow, tile)],
        [out(half, width), out(narrow, half), out(narrow, half)], down_scratch,
        (role_arg, edge_mine, emb_recv, rbf_mine, *down_weights), scalars=1, flops=4 * 10**9, limit=32 * 2**20,
    )
    table_recv = swap(table)

    bil_rows = w_bil_q.shape[1]
    z_quad, quad_rows = call(
        functools.partial(quad_forward_kernel, orders=orders, base=trip_width), "quad_forward", (1,),
        [whole(table.shape)] * 2 + [mine_quad] * 4 + [whole(w_bil_q.shape)],
        [whole((bil_rows, half_quad)), whole((quad_width, half_quad))],
        [out(bil_rows, half_quad), out(quad_width, half_quad)],
        [pltpu.VMEM((quad_slots, quad_width, half_quad), f32)] * 2 + [pltpu.VMEM((orders, quad_slots, half_quad), f32)],
        (role_arg, table, table_recv, q_index, q_cos, q_dih, q_live, w_bil_q), scalars=1, flops=2 * 10**9, limit=SMALL_LIMIT,
    )
    cap = quad_count // peers
    cut = quad_width * cap

    def by_peer(x):
        return x.reshape(quad_width, -1, cap).transpose(1, 0, 2).reshape(-1, cut)

    def by_entry(x):
        return x.reshape(-1, quad_width, cap).transpose(1, 0, 2).reshape(quad_width, -1)

    quad_sent = lax.dynamic_update_slice_in_dim(jnp.zeros((peers, cut), f32), by_peer(quad_rows), role * (peers // 2), axis=0)
    routed = exchange(jnp.concatenate([quad_sent, halo_out], axis=1))
    quad_own = by_entry(routed[:, :cut])
    halo_own = routed[:, cut:].reshape(halo_count, half_atom)
    quad_recv = swap(quad_own)
    halo_recv = swap(halo_own)

    bil_rows = w_bil_t.shape[1]
    steps = grid[0] // 2
    table_shape = (2 * CLASSES * trip_width, edges // CLASSES)

    def halves_of(rows):
        return [
            pl.BlockSpec((rows, tile), lambda i, *_: (0, jnp.minimum(i, steps - 1))),
            pl.BlockSpec((rows, tile), lambda i, *_: (0, jnp.maximum(i - steps, 0))),
        ]

    def slots_at(first):
        return [pl.BlockSpec((slots, tile), lambda i, r: (0, r[0] * grid[0] + first + i))] * 3

    def triplet_forward(first, after):
        return call(
            functools.partial(triplet_forward_kernel, orders=orders), f"triplet_forward{first}", (steps,),
            [whole(table.shape)] * 2 + slots_at(first) + [whole(w_bil_t.shape)],
            [columns_of(bil_rows, tile), columns_of(trip_width, tile)],
            [out(bil_rows, half // 2), out(trip_width, half // 2)],
            [
                pltpu.VMEM(table_shape, bf16),
                pltpu.VMEM((2, slots, trip_width, LANES), f32),
                pltpu.VMEM((orders, slots, tile), f32),
                pltpu.VMEM((2, *w_bil_t.shape), bf16),
            ],
            (role_arg, table, table_recv, t_index, t_cos, t_live, w_bil_t), scalars=1, flops=5 * 10**9, after=after,
        )

    z_one, mid_one = triplet_forward(0, [])
    z_two, mid_two = triplet_forward(steps, [quad_own, halo_own, mid_one])

    atom_recv = small_recv[:atoms]
    pool_rows = atoms + halo_count
    square = pltpu.VMEM((2, width, width), bf16)
    up_scratch = pltpu.VMEM((2, narrow, width), bf16)
    rad_scratch = pltpu.VMEM((2, radial_width, width), bf16)
    main_weights = (w_trip_up, w_quad_up, w_res_one, w_res_two, w_atom_edge, w_edge_rbf)
    main_small = (target, quad_own, quad_recv, atom_embed, atom_recv, halo_own, halo_recv)
    mid, joined, pre_one, pre_two, pre_six, new_own, new_send, coll_own = call(
        main_forward_kernel, "main_forward", grid,
        [rows_of(tile, width), *halves_of(trip_width), mine_rbf, mine_ends]
        + [whole(x.shape) for x in main_small + main_weights],
        [columns_of(narrow, tile)] + [rows_of(tile, width)] * 4 + [mine, rows_of(tile, half_width), whole((atoms, width))],
        [out(narrow, half)] + [out(half, width)] * 4 + [out(edges, half_width), out(half, half_width), out(atoms, width)],
        [up_scratch, square, square, square, rad_scratch, pltpu.VMEM((2, pool_rows + atoms, width), bf16), pltpu.VMEM((2 * quad_width, quad_count), bf16)],
        (role_arg, emb, mid_one, mid_two, rbf_mine, ends, *main_small, *main_weights), scalars=1, flops=8 * 10**9,
    )
    coll_recv = swap(coll_own)
    new_recv = swap(new_send)

    edge_rows = padded_rows(w_atom_edge.shape[0] + radial_width + w_edge_atom.size // width + w_out.size // width)
    atom_args = (coll_own, coll_recv, small_own, small_recv, halo_own, halo_recv, w_atom_edge, w_edge_rbf, w_edge_atom, w_out)
    res_grad, edge_keep, edge_send, pool_grad_own, pool_grad_send, atom_out, feat_out = call(
        functools.partial(edge_backward_kernel, scale=(atoms / edges) ** 0.5, codes=codes), "edge_backward", grid,
        [rows_of(tile, width)] * 3 + [mine_rbf, mine_ends, mine, rows_of(tile, half_width)] + [whole(x.shape) for x in atom_args],
        [rows_of(tile, width), whole((edge_rows // 2, width)), whole((edge_rows // 2, width)),
         whole((pool_rows, half_atom)), whole((pool_rows, half_atom)), whole((atoms, half_atom)), whole((atoms, half_atom))],
        [out(half, width), out(edge_rows // 2, width), out(edge_rows // 2, width),
         out(pool_rows, half_atom), out(pool_rows, half_atom), out(atoms, half_atom), out(atoms, half_atom)],
        [square, rad_scratch, pltpu.VMEM((2, atoms, width), bf16), pltpu.VMEM((pool_rows + atoms, width), f32), pltpu.VMEM((atoms, atom_width), f32),
         pltpu.VMEM((edge_rows, width), f32)],
        (place_at, joined, pre_two, pre_six, rbf_mine, ends, cot_mine, cot_recv, *atom_args), scalars=1, flops=8 * 10**9,
    )
    edge_blocks = phase([("add", [edge_keep, swap(edge_send)], plane[1])], "phase_one")[0]
    edge_parts = middle_stages(send_blocks(edge_blocks, plane), line[:-1], "edge_middle")

    res_rows = padded_rows(2 * width + narrow + w_bil_t.size // width)
    res_weights = (w_trip_up, w_quad_up, w_res_one, w_res_two)
    sum_grad, mid_grad, res_keep, res_send, back_part = call(
        functools.partial(residual_backward_kernel, codes=codes), "residual_backward", grid,
        [rows_of(tile, width)] * 3 + [columns_of(narrow, tile), *halves_of(bil_rows), whole(target.shape), rows_of(tile, width)]
        + [whole(w.shape) for w in res_weights],
        [rows_of(tile, width), columns_of(narrow, tile), whole((res_rows // 2, width)), whole((res_rows // 2, width)), whole((quad_width, quad_count))],
        [out(half, width), out(narrow, half), out(res_rows // 2, width), out(res_rows // 2, width), out(quad_width, quad_count)],
        [up_scratch, square, square, pltpu.VMEM((res_rows, width), f32), pltpu.VMEM(w_bil_t.shape, f32)],
        (place_at, joined, pre_one, pre_two, mid, z_one, z_two, target, res_grad, *res_weights), scalars=1, flops=8 * 10**9, after=edge_blocks,
    )
    sums_shape = (2 * CLASSES * trip_width, edges // CLASSES)

    def triplet_backward(first, held, after):
        return call(
            functools.partial(triplet_backward_kernel, orders=orders), f"triplet_backward{first}", (steps,),
            [pl.BlockSpec((narrow, tile), lambda i, r: (0, first + i))] + slots_at(first) + [whole(w_bil_t.shape)] + [whole(h.shape) for h in held],
            [whole(sums_shape)],
            [out(*sums_shape)],
            [
                pltpu.VMEM((bil_rows, tile), f32),
                pltpu.VMEM((2, slots, trip_width, LANES), f32),
                pltpu.VMEM((orders, slots, tile), f32),
                pltpu.VMEM((2, *w_bil_t.shape), bf16),
            ],
            (role_arg, mid_grad, t_index, t_cos, t_live, w_bil_t, *held), scalars=1, flops=6 * 10**9, after=after,
        )

    edge_blocks, (res_send,), (back_part,), (pool_grad_send,) = phase(
        [("add", edge_parts, line[-1][1]), ("join", [res_send], 1), ("join", [back_part], 1), ("join", [pool_grad_send], 1)], "phase_two", [sum_grad]
    )
    edge_parts = send_blocks(edge_blocks, line[-1])
    res_recv = swap(res_send)
    held = triplet_backward(0, [], edge_blocks)
    (edge_piece,), res_blocks, (pool_grad,), (back_sum,) = phase(
        [
            ("add", edge_parts, 1),
            ("add", [res_keep, res_recv], plane[1]),
            ("add", [pool_grad_own, swap(pool_grad_send)], 1),
            ("add", [back_part, swap(back_part)], 1),
        ],
        "phase_three", held,
    )
    returned_sent = jnp.concatenate([by_peer(back_sum), pool_grad[atoms:].reshape(peers, -1)], axis=1)
    edge_piece, edge_codes = middle_gathers(edge_piece, line[1:], "edge_middle_gather")
    edge_pieces, edge_lists = spread(edge_piece, edge_codes, line[0])
    res_parts = middle_stages(send_blocks(res_blocks, plane), line[:-1], "res_middle")
    returned = exchange(returned_sent)
    (trip_sums,) = triplet_backward(steps, held, [edge_piece, *res_blocks, returned_sent])
    (edge_piece,), res_blocks = phase([("join", edge_pieces, 1), ("add", res_parts, line[-1][1])], "phase_four", [trip_sums])
    edge_pieces, edge_codes = spread(edge_piece, sum(edge_lists, []), plane)
    res_parts = send_blocks(res_blocks, line[-1])
    back_rows = lax.dynamic_slice_in_dim(returned[:, :cut], role * (peers // 2), peers // 2, axis=0)
    back_own = by_entry(back_rows)
    halo_back = returned[:, cut:].reshape(halo_count, half_atom)
    bil_rows = w_bil_q.shape[1]
    quad_bil, table_keep, table_send = call(
        functools.partial(quad_backward_kernel, orders=orders), "quad_backward", (1,),
        [whole(back_own.shape), whole(z_quad.shape)] + [mine_quad] * 4 + [whole(w_bil_q.shape), whole(trip_sums.shape)],
        [whole(w_bil_q.shape), whole((narrow, half)), whole((narrow, half))],
        [out(*w_bil_q.shape), out(narrow, half), out(narrow, half)],
        [pltpu.VMEM((bil_rows, half_quad), f32), pltpu.VMEM((quad_slots, quad_width, half_quad), f32), pltpu.VMEM((orders, quad_slots, half_quad), f32)],
        (role_arg, back_own, z_quad, q_index, q_cos, q_dih, q_live, w_bil_q, trip_sums), scalars=1, flops=2 * 10**9, limit=SMALL_LIMIT,
        after=[edge_piece, *res_blocks],
    )
    (res_piece,), (table_send,) = phase([("add", res_parts, 1), ("join", [table_send], 1)], "phase_quad", [table_keep])
    table_recv = swap(table_send)
    res_piece, res_codes = middle_gathers(res_piece, line[1:], "res_middle_gather")
    res_pieces, res_lists = spread(res_piece, res_codes, line[0])

    late_rows = padded_rows(2 * radial_width + narrow + w_bil_q.size // width)
    grad_own, grad_send, late_keep, late_send = call(
        functools.partial(final_kernel, codes=[0]), "final", grid,
        [rows_of(tile, width), mine_rbf] + [columns_of(narrow, tile)] * 3 + [rows_of(tile, width)]
        + [whole(x.shape) for x in (quad_bil,) + down_weights],
        [mine, rows_of(tile, half_width)] + [whole((late_rows // 2, width))] * 2,
        [out(edges, half_width), out(half, half_width)] + [out(late_rows // 2, width)] * 2,
        down_scratch + [pltpu.VMEM((late_rows, width), f32)],
        (place_at * jnp.array([1, 0], i32), emb, rbf_mine, pre, table_keep, table_recv, sum_grad, quad_bil, *down_weights), scalars=1, flops=6 * 10**9,
        after=[res_piece],
    )
    grad_recv = swap(grad_send)
    (res_piece,), (late_send,) = phase([("join", res_pieces, 1), ("join", [late_send], 1)], "phase_five", edge_pieces[1:])
    ((late_half,),) = phase([("add", [late_keep, swap(late_send)], 1)], "phase_late")
    late_blocks = scatter_blocks(late_half)
    res_pieces, res_codes = spread(res_piece, sum(res_lists, []), plane)
    edge_full = lax.dynamic_update_slice_in_dim(new_own, new_recv, (1 - role) * half, axis=0)
    g_atom_edge, g_edge_rbf, g_edge_atom, g_out = unpack(
        edge_pieces, edge_codes, place_at, [w_atom_edge.shape, w_edge_rbf.shape, w_edge_atom.shape, w_out.shape],
        ["plain", "plain", "rows", "rows"], "edge_unpack", [late_half],
    )
    late_piece = fold(late_blocks, "late_fold", res_pieces, [g_out])
    late_all = exchange(jnp.broadcast_to(late_piece[None], late_blocks.shape)).reshape(late_half.shape)
    grad_full = lax.dynamic_update_slice_in_dim(grad_own, grad_recv, (1 - role) * half, axis=0)
    g_two, g_one, g_trip_up, g_quad_up, g_bil_t = unpack(
        res_pieces, res_codes, place_at, [w_res_two.shape, w_res_one.shape, w_trip_up.shape, w_quad_up.shape, w_bil_t.shape],
        ["plain"] * 4 + ["columns"], "res_unpack", [late_piece],
    )
    grad_atom = pool_grad[:atoms] + jnp.zeros((atoms, half_atom), f32).at[halo_send].add(halo_back)
    late_all = phase([("join", [late_all], 1)], "phase_six", [], [g_one, edge_full, grad_full, grad_atom])[0][0]
    g_trip_rbf, g_quad_rbf, g_down_t, g_down_q, g_bil_q = unpack(
        [late_all], [[0]], place_at * jnp.array([1, 0], i32), [w_trip_rbf.shape, w_quad_rbf.shape, w_down_t.shape, w_down_q.shape, w_bil_q.shape],
        ["plain"] * 4 + ["columns"], "late_unpack",
    )
    return (
        edge_full, atom_out, feat_out, grad_full, grad_atom,
        g_quad_rbf, g_down_q.T, g_bil_q.T, g_quad_up, g_trip_rbf, g_down_t.T, g_bil_t.T, g_trip_up,
        g_one, g_two, g_atom_edge, g_edge_rbf, g_edge_atom, g_out,
    )


def solution(mesh):
    whole_spec, rows_spec, both_spec = P(), P("edge"), P("edge", "pair")
    in_specs = (both_spec, both_spec) + (rows_spec,) * 12 + (whole_spec,) * 14 + (both_spec,) * 3
    out_specs = (both_spec,) * 5 + (whole_spec,) * 14
    return jax.shard_map(local, mesh=mesh, in_specs=in_specs, out_specs=out_specs, check_vma=False)
```

```python
import functools

import jax
import jax.numpy as jnp
from jax import lax
from jax.experimental import pallas as pl
from jax.experimental.pallas import tpu as pltpu
from jax.sharding import PartitionSpec as P

f32, bf16, i32 = jnp.float32, jnp.bfloat16, jnp.int32
root_third = 0.5773502691896258
root_half = 0.7071067811865476
LANES = 128
CLASSES = 4
VMEM_LIMIT = 30 * 2**20
SMALL_LIMIT = 24 * 2**20


def split(x):
    high = x.astype(bf16)
    return high, (x - high.astype(f32)).astype(bf16)


def dot(left, right, dims):
    return lax.dot_general(left, right, (dims, ((), ())), preferred_element_type=f32)


NN = ((1,), (0,))
NT = ((1,), (1,))
TN = ((0,), (0,))


def dot3(left, right, dims=NN):
    lh, ll = left if isinstance(left, tuple) else split(left)
    rh, rl = right if isinstance(right, tuple) else split(right)
    at, to = dims[0][0], dims[1][0]
    depth, rows = lh.shape[at], lh.shape[1 - at]
    if (at == 0 or depth % LANES == 0) and (to == 0 or depth % LANES == 0):
        if 3 * depth <= 2 * LANES:
            return dot(jnp.concatenate([lh, lh, ll], axis=at), jnp.concatenate([rh, rl, rh], axis=to), dims)
        if 2 * depth <= 2 * LANES:
            return dot(jnp.concatenate([lh, ll], axis=at), jnp.concatenate([rh, rh], axis=to), dims) + dot(lh, rl, dims)
    if at == 1 and rows <= LANES:
        both = dot(jnp.concatenate([lh, ll], axis=0), rh, dims)
        return both[:rows] + both[rows:] + dot(lh, rl, dims)
    return dot(lh, rh, dims) + dot(lh, rl, dims) + dot(ll, rh, dims)


def pick(onehot, right, dims=NN):
    rh, rl = right if isinstance(right, tuple) else split(right)
    return dot(onehot, rh, dims) + dot(onehot, rl, dims)


def sigmoid(v):
    return 0.5 * jnp.tanh(0.5 * v) + 0.5


def silu(v):
    return v * sigmoid(v)


def silu_grad(v):
    s = sigmoid(v)
    return s * (1.0 + v * (1.0 - s))


def as_bf16(mask):
    return mask.astype(f32).astype(bf16)


def legendre_steps(cosine, orders):
    before, now = jnp.ones_like(cosine), cosine
    yield before
    yield now
    for order in range(1, orders - 1):
        before, now = now, ((2 * order + 1) / (order + 1)) * cosine * now - (order / (order + 1)) * before
        yield now


def class_table(own, other, classes):
    per = classes // 2
    step = own.shape[1] // per
    parts = []
    for block in (own, other):
        high, low = split(block)
        for q in range(per):
            parts += [high[:, q * step : (q + 1) * step], low[:, q * step : (q + 1) * step]]
    return jnp.concatenate(parts, axis=0)


def gather_classes(table, index, classes, width):
    step = table.shape[1]
    shift = step.bit_length() - 1
    slots = index.shape[1]
    onehot = as_bf16(lax.broadcasted_iota(i32, (step, slots), 0) == (index & (step - 1)))
    found = dot(table, onehot, NN)
    kind = index >> shift
    out = found[0:width] + found[width : 2 * width]
    for q in range(1, classes):
        base = q * 2 * width
        out = jnp.where(kind >= q, found[base : base + width] + found[base + width : base + 2 * width], out)
    return out


def scatter_classes(values, indices, classes, step):
    shift = step.bit_length() - 1
    lefts, rights = [], []
    for value, index in zip(values, indices):
        width, slots = value.shape
        high, low = split(value)
        both = jnp.concatenate([high, low], axis=0)
        kind = jnp.broadcast_to(index >> shift, (2 * width, slots))
        lefts.append(jnp.concatenate([jnp.where(kind == q, both, jnp.zeros((), bf16)) for q in range(classes)], axis=0))
        rights.append(as_bf16(lax.broadcasted_iota(i32, (step, slots), 0) == (index & (step - 1))))
    return dot(jnp.concatenate(lefts, axis=1), jnp.concatenate(rights, axis=1), NT)


def unfold_classes(sums, classes, width):
    parts = []
    for q in range(classes):
        base = q * 2 * width
        parts.append(sums[base : base + width] + sums[base + width : base + 2 * width])
    return jnp.concatenate(parts, axis=1)


def joined_halves(zero, mine, theirs, axis=1):
    return jnp.concatenate([jnp.where(zero, mine, theirs), jnp.where(zero, theirs, mine)], axis=axis)


def down_kernel(role, own, recv, rbf, w_trip_rad, w_quad_rad, w_trip, w_quad, emb_out, pre_out, table_out, rad, down_t, down_q):
    width = w_trip_rad.shape[1]

    @pl.when(pl.program_id(0) == 0)
    def _():
        rad[0, :, :width], rad[1, :, :width] = split(w_trip_rad[...])
        rad[0, :, width:], rad[1, :, width:] = split(w_quad_rad[...])
        down_t[0], down_t[1] = split(w_trip[...])
        down_q[0], down_q[1] = split(w_quad[...])

    emb = joined_halves(role[0] == 0, own[...], recv[...])
    emb_out[...] = emb
    radial = dot3(rbf[...], (rad[0], rad[1]))
    pre = jnp.concatenate(
        [
            dot3((down_t[0], down_t[1]), emb * radial[:, :width], NT),
            dot3((down_q[0], down_q[1]), emb * radial[:, width:], NT),
        ],
        axis=0,
    )
    pre_out[...] = pre
    table_out[...] = silu(pre)


def quad_forward_kernel(role, own, other, index, cosine, dihedral, live, w_bil, z_out, rows_out, sel, sel2, basis, *, orders, base):
    slots_k, rows = index.shape
    width = w_bil.shape[0]
    zero = role[0] == 0
    mine, theirs = own[base : base + width, :], other[base : base + width, :]
    table = class_table(jnp.where(zero, mine, theirs), jnp.where(zero, theirs, mine), 2 * CLASSES)
    alive = live[...].astype(f32)
    for order, series in enumerate(legendre_steps(cosine[...], orders)):
        basis[order] = series * alive
    for k in range(slots_k):
        picked = gather_classes(table, index[k : k + 1, :], 2 * CLASSES, width)
        sel[k] = picked
        sel2[k] = picked * dihedral[k : k + 1, :]
    groups = width // 8
    for t in range(rows // LANES):
        at = slice(t * LANES, (t + 1) * LANES)
        for part, source in enumerate((sel, sel2)):
            for order_at in range(0, orders, 8):
                sums = {}
                for k in range(slots_k):
                    chosen = [source[k, g * 8 : g * 8 + 8, at] for g in range(groups)]
                    for order in range(8):
                        weight = jnp.broadcast_to(basis[order_at + order, k : k + 1, at], (8, LANES))
                        for g in range(groups):
                            term = weight * chosen[g]
                            sums[order, g] = term if k == 0 else sums[order, g] + term
                for (order, g), total in sums.items():
                    row = (part * orders + order_at + order) * width + g * 8
                    z_out[row : row + 8, at] = total
    rows_out[...] = dot3(w_bil[...], z_out[...])


def triplet_forward_kernel(role, own, other, index, cosine, live, w_bil, z_out, mid_out, table, sel, basis, bil, *, orders):
    slots_k, tile = index.shape
    width = w_bil.shape[0]

    @pl.when(pl.program_id(0) == 0)
    def _():
        zero = role[0] == 0
        mine, theirs = own[0:width, :], other[0:width, :]
        table[...] = class_table(jnp.where(zero, mine, theirs), jnp.where(zero, theirs, mine), CLASSES)
        bil[0], bil[1] = split(w_bil[...])

    alive = live[...].astype(f32)
    for order, series in enumerate(legendre_steps(cosine[...], orders)):
        basis[order] = series * alive

    def gather(at, k, into):
        where_to = jnp.concatenate([index[k : k + 1, at], index[k + 1 : k + 2, at]], axis=1)
        found = gather_classes(table[...], where_to, CLASSES, width)
        sel[into, k] = found[:, :LANES]
        sel[into, k + 1] = found[:, LANES:]

    def combine(at, first, source):
        sums = {}
        for k in range(slots_k):
            chosen = [sel[source, k, g * 8 : g * 8 + 8, :] for g in (first, first + 1)]
            for order in range(orders):
                weight = jnp.broadcast_to(basis[order, k : k + 1, at], (8, LANES))
                for g in range(2):
                    term = weight * chosen[g]
                    sums[order, g] = term if k == 0 else sums[order, g] + term
        for (order, g), total in sums.items():
            row = order * width + (first + g) * 8
            z_out[row : row + 8, at] = total

    firsts = range(0, width // 8, 2)
    turns = slots_k // 2 // len(firsts)
    columns = lambda c: pl.ds(pl.multiple_of(c * LANES, LANES), LANES)
    for k in range(0, slots_k, 2):
        gather(columns(0), k, 0)

    def step_columns(c, carry):
        for n, first in enumerate(firsts):
            for k in range(n * turns, (n + 1) * turns):
                gather(columns(c), 2 * k, c & 1)
            combine(columns(c - 1), first, 1 - (c & 1))
        return carry

    lax.fori_loop(1, tile // LANES, step_columns, 0)
    for first in firsts:
        combine(columns(tile // LANES - 1), first, (tile // LANES - 1) & 1)
    mid_out[...] = dot3((bil[0], bil[1]), z_out[...])


def laid(pairs):
    return tuple(jnp.concatenate([p[n] for p in pairs], axis=0) for n in range(2))


def row_blocks(tile):
    return [slice(n * tile // 2, (n + 1) * tile // 2) for n in range(2)]


def edge_members(ends, pool_rows, atoms, tile):
    row = lax.broadcasted_iota(i32, (pool_rows + atoms, tile), 0)
    return as_bf16(row == jnp.where(row < pool_rows, ends[0:1, :], ends[1:2, :] + pool_rows))


def entry_members(role, target, step, tile, half):
    row = lax.broadcasted_iota(i32, (tile, target.shape[1]), 0) + (step * tile + role[0] * half)
    return as_bf16(row == target[...])


def main_forward_kernel(
    role, emb, mid_one, mid_two, rbf, ends, target, quad_own, quad_recv, atom_own, atom_recv, halo_own, halo_recv,
    w_trip_up, w_quad_up, w_one, w_two, w_edge, w_rbf,
    mid_out, joined_out, one_out, two_out, six_out, new_own, new_send, collected,
    up, one, two, three, rad, pool_w, quad_hl,
):
    step = pl.program_id(0)
    tile = emb.shape[0]
    half_rows = tile * pl.num_programs(0)
    atoms = atom_own.shape[0]
    pool_rows = atoms + halo_own.shape[0]
    atom_width = 2 * atom_own.shape[1]
    trip_width = w_trip_up.shape[0]
    zero = role[0] == 0

    @pl.when(step == 0)
    def _():
        up[0, :trip_width], up[1, :trip_width] = split(w_trip_up[...])
        up[0, trip_width:], up[1, trip_width:] = split(w_quad_up[...])
        one[0], one[1] = split(w_one[...])
        two[0], two[1] = split(w_two[...])
        three[0], three[1] = split(w_edge[2 * atom_width :, :])
        rad[0], rad[1] = split(w_rbf[...])
        atom_rows = joined_halves(zero, atom_own[...], atom_recv[...])
        pool = jnp.concatenate([atom_rows, joined_halves(zero, halo_own[...], halo_recv[...])], axis=0)
        projected = jnp.concatenate(
            [dot3(pool, w_edge[0:atom_width, :]), dot3(atom_rows, w_edge[atom_width : 2 * atom_width, :])], axis=0
        )
        pool_w[0], pool_w[1] = split(projected)
        high, low = split(quad_own[...] + quad_recv[...])
        quad_hl[...] = jnp.concatenate([high, low], axis=0)

    found = dot(quad_hl[...], entry_members(role, target, step, tile, half_rows), NT)
    width = found.shape[0] // 2
    mid_trip = jnp.where(step < pl.num_programs(0) // 2, mid_one[...], mid_two[...])
    mid = jnp.concatenate([mid_trip, found[:width] + found[width:]], axis=0)
    mid_out[...] = mid
    member = edge_members(ends, pool_rows, atoms, tile)
    blocks = row_blocks(tile)
    joined = [(emb[at, :] + dot3(mid[:, at], (up[0], up[1]), TN)) * root_third for at in blocks]
    pre_one = [dot3(x, (one[0], one[1])) for x in joined]
    pre_two = [dot3(silu(x), (two[0], two[1])) for x in pre_one]
    residual = [(x + silu(y)) * root_half for x, y in zip(joined, pre_two)]
    pre_six = [pick(member[:, at], (pool_w[0], pool_w[1]), TN) + dot3(x, (three[0], three[1])) for at, x in zip(blocks, residual)]
    edge_new = [(x + silu(y)) * root_half for x, y in zip(residual, pre_six)]
    half = emb.shape[1] // 2
    part = 0.0
    for n, at in enumerate(blocks):
        joined_out[at, :] = joined[n]
        one_out[at, :] = pre_one[n]
        two_out[at, :] = pre_two[n]
        six_out[at, :] = pre_six[n]
        new_own[at, :] = jnp.where(zero, edge_new[n][:, :half], edge_new[n][:, half:])
        new_send[at, :] = jnp.where(zero, edge_new[n][:, half:], edge_new[n][:, :half])
        part = part + pick(member[pool_rows:, at], edge_new[n] * dot3(rbf[at, :], (rad[0], rad[1])))

    @pl.when(step == 0)
    def _():
        collected[...] = part

    @pl.when(step > 0)
    def _():
        collected[...] += part


def give_halves(place_at, total, keep, send, codes):
    half = keep.shape[0]
    rows = half // len(codes)
    for side, target in ((place_at[0], keep), (1 - place_at[0], send)):
        for n, code in enumerate(codes):
            at = pl.multiple_of(side * half + (place_at[1] ^ code) * rows, 8)
            target[n * rows : (n + 1) * rows, :] = total[pl.ds(at, rows), :]


def side_by_side(x, width):
    parts = width // x.shape[1]
    rows = x.shape[0] // parts
    return jnp.concatenate([x[q * rows : (q + 1) * rows] for q in range(parts)], axis=1)


def edge_backward_kernel(
    role, joined, pre_two_ref, pre_six_ref, rbf, ends, cot_own, cot_recv,
    coll_own, coll_recv, small_own, small_recv, halo_own, halo_recv,
    w_edge, w_rbf, w_edge_atom, w_out,
    res_grad_out, keep, send, pool_grad_own, pool_grad_send, atom_out, feat_out,
    three, rad, coll_grad, pool_sum, direct, grads,
    *, scale, codes,
):
    step = pl.program_id(0)
    last = pl.num_programs(0) - 1
    tile, edge_width = joined.shape
    half = small_own.shape[1]
    atoms = small_own.shape[0] // 3
    atom_width = 2 * half
    pool_rows = atoms + halo_own.shape[0]
    zero = role[0] == 0
    at_rbf = w_edge.shape[0]
    at_atom = at_rbf + w_rbf.shape[0]
    at_last = at_atom + w_edge_atom.shape[0] * atom_width // edge_width
    at_end = at_last + atom_width * atom_width // edge_width

    @pl.when(step == 0)
    def _():
        three[0], three[1] = split(w_edge[2 * atom_width :, :])
        rad[0], rad[1] = split(w_rbf[...])
        mine, theirs = small_own[...], small_recv[...]
        atom_rows = joined_halves(zero, mine[:atoms], theirs[:atoms])
        cot_atom = joined_halves(zero, mine[atoms : 2 * atoms], theirs[atoms : 2 * atoms])
        cot_feat = joined_halves(zero, mine[2 * atoms :], theirs[2 * atoms :])
        total = (coll_own[...] + coll_recv[...]) * scale
        w_a, w_f = split(w_edge_atom[...]), split(w_out[...])
        pre_atom = dot3(total, w_a)
        atom_new = (atom_rows + silu(pre_atom)) * root_half
        pre_feat = dot3(atom_new, w_f)
        feature = silu(pre_feat)
        atom_out[...] = jnp.where(zero, atom_new[:, :half], atom_new[:, half:])
        feat_out[...] = jnp.where(zero, feature[:, :half], feature[:, half:])
        feat_grad = cot_feat * silu_grad(pre_feat)
        grads[at_last:at_end, :] = side_by_side(0.5 * dot3(atom_new, feat_grad, TN), edge_width)
        atom_grad = (cot_atom + dot3(feat_grad, w_f, NT)) * root_half
        direct[...] = 0.5 * atom_grad
        pre_grad = atom_grad * silu_grad(pre_atom)
        grads[at_atom:at_last, :] = side_by_side(0.5 * dot3(total, pre_grad, TN), edge_width)
        coll_grad[0], coll_grad[1] = split(dot3(pre_grad, w_a, NT) * scale)
        grads[0:at_atom, :] = jnp.zeros((at_atom, grads.shape[1]), f32)
        if grads.shape[0] > at_end:
            grads[at_end:, :] = jnp.zeros((grads.shape[0] - at_end, grads.shape[1]), f32)
        pool_sum[...] = jnp.zeros_like(pool_sum)

    member = edge_members(ends, pool_rows, atoms, tile)
    blocks = row_blocks(tile)
    six = [pre_six_ref[at, :] for at in blocks]
    s_six = [sigmoid(x) for x in six]
    residual = [(joined[at, :] + silu(pre_two_ref[at, :])) * root_half for at in blocks]
    edge_new = [(x + y * s) * root_half for x, y, s in zip(residual, six, s_six)]
    radial = split(rbf[...])
    weighted_grad = [pick(member[pool_rows:, at], (coll_grad[0], coll_grad[1]), TN) for at in blocks]
    new_grad = [
        (joined_halves(zero, cot_own[at, :], cot_recv[at, :]) + w * dot3((radial[0][at], radial[1][at]), (rad[0], rad[1]))) * root_half
        for at, w in zip(blocks, weighted_grad)
    ]
    six_split = [split(g * (s * (1.0 + y * (1.0 - s)))) for g, y, s in zip(new_grad, six, s_six)]
    for at, g, pair in zip(blocks, new_grad, six_split):
        res_grad_out[at, :] = (g + dot3(pair, (three[0], three[1]), NT)) * root_half
    grads[at_rbf:at_atom, :] += dot3(radial, laid([split(w * x) for w, x in zip(weighted_grad, edge_new)]), TN)
    six_all = laid(six_split)
    pool_sum[...] += pick(member, six_all)
    grads[2 * atom_width : at_rbf, :] += dot3(laid([split(x) for x in residual]), six_all, TN)

    @pl.when(step == last)
    def _():
        atom_rows = joined_halves(zero, small_own[:atoms, :], small_recv[:atoms, :])
        pool = jnp.concatenate([atom_rows, joined_halves(zero, halo_own[...], halo_recv[...])], axis=0)
        w_src, w_dst = split(w_edge[0:atom_width, :]), split(w_edge[atom_width : 2 * atom_width, :])
        src_split, dst_split = split(pool_sum[0:pool_rows, :]), split(pool_sum[pool_rows:, :])
        grads[0:atom_width, :] = dot3(pool, src_split, TN)
        grads[atom_width : 2 * atom_width, :] = dot3(atom_rows, dst_split, TN)
        from_src = dot3(src_split, w_src, NT)
        from_atoms = from_src[0:atoms] + dot3(dst_split, w_dst, NT) + direct[...]
        result = jnp.concatenate([from_atoms, from_src[atoms:]], axis=0)
        pool_grad_own[...] = jnp.where(zero, result[:, :half], result[:, half:])
        pool_grad_send[...] = jnp.where(zero, result[:, half:], result[:, :half])
        give_halves(role, grads, keep, send, codes)


def residual_backward_kernel(
    role, joined, pre_one_ref, pre_two_ref, mid_ref, z_one, z_two, target, res_grad_ref,
    w_trip_up, w_quad_up, w_one, w_two,
    sum_grad_out, mid_grad_out, keep, send, back,
    up, one, two, grads, bil_grad,
    *, codes,
):
    step = pl.program_id(0)
    tile, width = joined.shape
    half_rows = tile * pl.num_programs(0)
    trip_width = w_trip_up.shape[0]
    narrow = up.shape[1]
    at_bil = 2 * width + narrow

    @pl.when(step == 0)
    def _():
        up[0, :trip_width], up[1, :trip_width] = split(w_trip_up[...])
        up[0, trip_width:], up[1, trip_width:] = split(w_quad_up[...])
        one[0], one[1] = split(w_one[...])
        two[0], two[1] = split(w_two[...])
        grads[...] = jnp.zeros_like(grads)
        bil_grad[...] = jnp.zeros_like(bil_grad)
        back[...] = jnp.zeros_like(back)

    blocks = row_blocks(tile)

    res_grad = [res_grad_ref[at, :] for at in blocks]
    two_split = [split(grad * silu_grad(pre_two_ref[at, :])) for grad, at in zip(res_grad, blocks)]
    pre_one = [pre_one_ref[at, :] for at in blocks]
    s_one = [sigmoid(pre) for pre in pre_one]
    hidden = [split(pre * s) for pre, s in zip(pre_one, s_one)]
    one_split = [
        split(dot3(grad, (two[0], two[1]), NT) * (s * (1.0 + pre * (1.0 - s)))) for grad, pre, s in zip(two_split, pre_one, s_one)
    ]
    grads[0:width, :] += dot3(laid(hidden), laid(two_split), TN)
    sum_grad = [(grad + dot3(inner, (one[0], one[1]), NT)) * root_third for grad, inner in zip(res_grad, one_split)]
    grads[width : 2 * width, :] += dot3(joined[...], laid(one_split), TN)
    for at, grad in zip(blocks, sum_grad):
        sum_grad_out[at, :] = grad
    sum_split = laid([split(grad) for grad in sum_grad])
    grads[2 * width : at_bil, :] += dot3(mid_ref[...], sum_split, NN)
    mid_grad = dot3((up[0], up[1]), sum_split, NT)
    mid_grad_out[...] = mid_grad
    mid_high, mid_low = split(mid_grad)
    z = jnp.where(step < pl.num_programs(0) // 2, z_one[...], z_two[...])
    bil_grad[...] += dot3((mid_high[:trip_width], mid_low[:trip_width]), z, NT)
    found = dot(jnp.concatenate([mid_high[trip_width:], mid_low[trip_width:]], axis=0), entry_members(role, target, step, tile, half_rows), NN)
    rows = narrow - trip_width
    back[...] += found[:rows] + found[rows:]

    @pl.when(step == pl.num_programs(0) - 1)
    def _():
        for q in range(bil_grad.shape[1] // width):
            grads[at_bil + q * trip_width : at_bil + (q + 1) * trip_width, :] = bil_grad[:, q * width : (q + 1) * width]
        give_halves(role, grads, keep, send, codes)


def triplet_backward_kernel(role, mid_grad, index, cosine, live, w_bil, *refs, orders):
    held, (sums, zg, sg, basis, bil) = refs[:-5], refs[-5:]
    step = pl.program_id(0)
    slots_k, tile = index.shape
    width = w_bil.shape[0]
    classes_step = sums.shape[1]

    @pl.when(step == 0)
    def _():
        bil[0], bil[1] = split(w_bil[...])
        sums[...] = held[0][...] if held else jnp.zeros_like(sums)

    alive = live[...].astype(f32)
    for order, series in enumerate(legendre_steps(cosine[...], orders)):
        basis[order] = series * alive
    grad_split = split(mid_grad[0:width, :])
    zg[...] = dot3((bil[0], bil[1]), grad_split, TN)

    def combine(at, first, into):
        totals = {}
        for order in range(orders):
            row = order * width + first * 8
            got = [zg[row + g * 8 : row + g * 8 + 8, at] for g in range(2)]
            for k in range(slots_k):
                weight = jnp.broadcast_to(basis[order, k : k + 1, at], (8, LANES))
                for g in range(2):
                    term = weight * got[g]
                    totals[k, g] = term if order == 0 else totals[k, g] + term
        for (k, g), total in totals.items():
            sg[into, k, (first + g) * 8 : (first + g) * 8 + 8, :] = total

    def scatter(at, first, source):
        slots_at = range(first, first + slots_k // 2)
        sums[...] += scatter_classes(
            [sg[source, k] for k in slots_at], [index[k : k + 1, at] for k in slots_at], CLASSES, classes_step
        )

    firsts = range(0, width // 8, 2)
    columns = lambda c: pl.ds(pl.multiple_of(c * LANES, LANES), LANES)
    for first in firsts:
        combine(columns(0), first, 0)

    def step_columns(c, carry):
        for n, first in enumerate(firsts):
            if n % 2 == 0:
                scatter(columns(c - 1), n // 2 * (slots_k // 2), 1 - (c & 1))
            combine(columns(c), first, c & 1)
        return carry

    lax.fori_loop(1, tile // LANES, step_columns, 0)
    for n in range(2):
        scatter(columns(tile // LANES - 1), n * (slots_k // 2), (tile // LANES - 1) & 1)


def quad_backward_kernel(role, own, z, index, cosine, dihedral, live, w_bil, trip_sums, bil_grad, keep, send, zg, sg, basis, *, orders):
    slots_k, rows = index.shape
    width = w_bil.shape[0]
    edges = trip_sums.shape[1] * CLASSES
    trip_width = trip_sums.shape[0] // (2 * CLASSES)
    zero = role[0] == 0
    alive = live[...].astype(f32)
    for order, series in enumerate(legendre_steps(cosine[...], orders)):
        basis[order] = series * alive
    grad_split = split(own[...])
    bil_grad[...] = dot3(grad_split, z[...], NT)
    zg[...] = dot3(w_bil[...], grad_split, TN)
    groups = width // 8
    for t in range(rows // LANES):
        at = slice(t * LANES, (t + 1) * LANES)
        for g in range(groups):
            plain, turned = {}, {}
            for order in range(orders):
                one = zg[order * width + g * 8 : order * width + g * 8 + 8, at]
                two = zg[(orders + order) * width + g * 8 : (orders + order) * width + g * 8 + 8, at]
                for k in range(slots_k):
                    weight = jnp.broadcast_to(basis[order, k : k + 1, at], (8, LANES))
                    plain[k] = weight * one if order == 0 else plain[k] + weight * one
                    turned[k] = weight * two if order == 0 else turned[k] + weight * two
            for k in range(slots_k):
                sg[k, g * 8 : g * 8 + 8, at] = plain[k] + turned[k] * jnp.broadcast_to(dihedral[k : k + 1, at], (8, LANES))
    step = edges // (2 * CLASSES)
    sums = scatter_classes([sg[k] for k in range(slots_k)], [index[k : k + 1, :] for k in range(slots_k)], 2 * CLASSES, step)
    total = jnp.concatenate([unfold_classes(trip_sums[...], CLASSES, trip_width), unfold_classes(sums, 2 * CLASSES, width)], axis=0)
    half = edges // 2
    keep[...] = jnp.where(zero, total[:, :half], total[:, half:])
    send[...] = jnp.where(zero, total[:, half:], total[:, :half])


def final_kernel(
    role, emb_ref, rbf, pre_ref, table_own, table_recv, sum_grad, quad_bil, w_trip_rad, w_quad_rad, w_trip, w_quad,
    grad_own, grad_send, keep, send,
    rad, down_t, down_q, total,
    *, codes,
):
    step = pl.program_id(0)
    zero = role[0] == 0
    radial_rows, width = w_trip_rad.shape
    trip_width, quad_width = w_trip.shape[0], w_quad.shape[0]
    at_quad_rad = radial_rows
    at_trip = 2 * radial_rows
    at_quad = at_trip + trip_width
    at_quad_bil = at_quad + quad_width
    at_end = at_quad_bil + quad_width * quad_bil.shape[1] // width

    @pl.when(step == 0)
    def _():
        rad[0, :, :width], rad[1, :, :width] = split(w_trip_rad[...])
        rad[0, :, width:], rad[1, :, width:] = split(w_quad_rad[...])
        down_t[0], down_t[1] = split(w_trip[...])
        down_q[0], down_q[1] = split(w_quad[...])
        total[...] = jnp.zeros_like(total)
        rows = quad_bil.shape[0]
        for q in range(quad_bil.shape[1] // width):
            total[at_quad_bil + q * rows : at_quad_bil + (q + 1) * rows, :] = quad_bil[:, q * width : (q + 1) * width]

    emb = emb_ref[...]
    radial_split = split(rbf[...])
    radial = dot3(radial_split, (rad[0], rad[1]))
    pre_grad = (table_own[...] + table_recv[...]) * silu_grad(pre_ref[...])
    trip_split, quad_split = split(pre_grad[:trip_width]), split(pre_grad[trip_width:])
    trip_radial, quad_radial = radial[:, :width], radial[:, width:]
    total[at_trip:at_quad, :] += dot3(trip_split, emb * trip_radial)
    total[at_quad:at_quad_bil, :] += dot3(quad_split, emb * quad_radial)
    trip_mixed = dot3(trip_split, (down_t[0], down_t[1]), TN)
    quad_mixed = dot3(quad_split, (down_q[0], down_q[1]), TN)
    grad = sum_grad[...] + trip_mixed * trip_radial + quad_mixed * quad_radial
    half = width // 2
    grad_own[...] = jnp.where(zero, grad[:, :half], grad[:, half:])
    grad_send[...] = jnp.where(zero, grad[:, half:], grad[:, :half])
    total[0:at_quad_rad, :] += dot3(radial_split, trip_mixed * emb, TN)
    total[at_quad_rad:at_trip, :] += dot3(radial_split, quad_mixed * emb, TN)

    @pl.when(step == pl.num_programs(0) - 1)
    def _():
        give_halves(role, total, keep, send, codes)


def fold_kernel(source, target):
    target[...] = jnp.sum(source[...], axis=0)


def fold(blocks, name, after=(), whole_after=()):
    return call(fold_kernel, name, (1,), [whole(blocks.shape)], [whole(blocks.shape[1:])], [out(*blocks.shape[1:])], [], (blocks,), after=after, whole_after=whole_after, limit=SMALL_LIMIT)[0]


def exchange(blocks):
    return lax.all_to_all(blocks, "edge", split_axis=0, concat_axis=0, tiled=True)


def scatter_blocks(rows):
    return exchange(rows.reshape(lax.axis_size("edge"), -1, rows.shape[1]))


def partners(bits, axis="edge"):
    return [(i, i ^ bits) for i in range(lax.axis_size(axis))]


def edge_stages():
    size, shift, stages = lax.axis_size("edge"), 0, []
    while size > 1:
        radix = 8 if size == 8 else 4 if size % 4 == 0 else 2
        stages.append((shift, radix))
        shift += radix.bit_length() - 1
        size //= radix
    return stages


def padded_rows(rows):
    unit = 2 * 8 * lax.axis_size("edge")
    return -(-rows // unit) * unit


def spread(piece, codes, stage):
    shift, radix = stage
    pieces = [piece] + [lax.ppermute(piece, "edge", partners(j << shift)) for j in range(1, radix)]
    return pieces, [[c ^ (j << shift) for c in codes] for j in range(radix)]


def stage_codes(stages):
    codes = [0]
    for shift, radix in reversed(stages):
        codes = [c ^ (j << shift) for j in range(radix) for c in codes]
    return codes


def phase_kernel(*refs, jobs):
    ins, outs = list(refs[: sum(count for _, count, _ in jobs)]), list(refs[sum(count for _, count, _ in jobs) :])
    for kind, count, blocks in jobs:
        parts, ins = ins[:count], ins[count:]
        targets, outs = outs[:blocks], outs[blocks:]
        if kind == "join":
            rows = parts[0].shape[0]
            for n, part in enumerate(parts):
                targets[0][n * rows : (n + 1) * rows, :] = part[...]
        else:
            rows = parts[0].shape[0] // blocks
            for n, target in enumerate(targets):
                total = parts[0][n * rows : (n + 1) * rows, :]
                for part in parts[1:]:
                    total = total + part[n * rows : (n + 1) * rows, :]
                target[...] = total


def phase(jobs, name, after=(), whole_after=()):
    ins, shapes = [], []
    for kind, parts, blocks in jobs:
        rows, width = parts[0].shape
        ins += parts
        shapes += [(len(parts) * rows, width)] if kind == "join" else [(rows // blocks, width)] * blocks
    got = call(
        functools.partial(phase_kernel, jobs=[(kind, len(parts), blocks) for kind, parts, blocks in jobs]), name, (1,),
        [whole(x.shape) for x in ins], [whole(x) for x in shapes], [out(*x) for x in shapes], [], tuple(ins), after=after, whole_after=whole_after, limit=SMALL_LIMIT,
    )
    results = []
    for _, _, blocks in jobs:
        results.append(got[:blocks])
        got = got[blocks:]
    return results


def send_blocks(blocks, stage):
    shift, radix = stage
    return [blocks[0]] + [lax.ppermute(blocks[j], "edge", partners(j << shift)) for j in range(1, radix)]


def middle_stages(parts, stages, name):
    for at, stage in enumerate(stages):
        parts = send_blocks(phase([("add", parts, stage[1])], f"{name}{at}")[0], stage)
    return parts


def middle_gathers(piece, stages, name):
    codes = [0]
    for at, stage in enumerate(reversed(stages)):
        pieces, lists = spread(piece, codes, stage)
        piece, codes = phase([("join", pieces, 1)], f"{name}{at}")[0][0], sum(lists, [])
    return piece, codes


def unpack_kernel(place_at, *refs, count, codes, layout):
    ins, outs, total = refs[:count], refs[count:-1], refs[-1]
    half = total.shape[0] // 2
    for n, source in enumerate(ins):
        side, listed = codes[n]
        first = jnp.where(place_at[0] == 0, side, 1 - side) * half
        rows = source.shape[0] // len(listed)
        for at, code in enumerate(listed):
            block = place_at[1] ^ code
            total[pl.ds(pl.multiple_of(first + block * rows, 8), rows), :] = source[at * rows : (at + 1) * rows, :]
    at = 0
    for target, kind in zip(outs, layout):
        height, breadth = target.shape
        width = total.shape[1]
        if kind == "plain":
            target[...] = total[at : at + height, :]
            at += height
        elif kind == "rows":
            parts = width // breadth
            rows = height // parts
            for q in range(parts):
                target[q * rows : (q + 1) * rows, :] = total[at : at + rows, q * breadth : (q + 1) * breadth]
            at += rows
        else:
            for q in range(breadth // width):
                target[:, q * width : (q + 1) * width] = total[at : at + height, :]
                at += height


def unpack(pieces, codes, place_at, shapes, layout, name, after=()):
    count = 2 * len(pieces)
    pieces = pieces + [swap(p) for p in pieces]
    codes = [(0, c) for c in codes] + [(1, c) for c in codes]
    rows = sum(p.shape[0] for p in pieces)
    return call(
        functools.partial(unpack_kernel, count=count, codes=codes, layout=layout), name, (1,), [whole(p.shape) for p in pieces],
        [whole(s) for s in shapes], [out(*s) for s in shapes], [pltpu.VMEM((rows, pieces[0].shape[1]), f32)], (place_at, *pieces), scalars=1, whole_after=after, limit=SMALL_LIMIT,
    )


def whole(shape):
    return pl.BlockSpec(shape, lambda *_: (0,) * len(shape))


def rows_of(tile, width):
    return pl.BlockSpec((tile, width), lambda i, *_: (i, 0))


def columns_of(rows, tile):
    return pl.BlockSpec((rows, tile), lambda i, *_: (0, i))


def out(*shape):
    return jax.ShapeDtypeStruct(shape, f32)


def kept(*shape):
    return pltpu.HBM(shape, f32)


def tip(x):
    x = x.reshape(-1, x.shape[-1])
    return x[: min(8, x.shape[0]), : min(LANES, x.shape[1])]


def call(body, name, grid, in_specs, out_specs, out_shape, scratch, args, scalars=0, flops=0, after=(), whole_after=(), limit=VMEM_LIMIT):
    after = [tip(x) for x in after] + list(whole_after)
    first, count = len(args), len(after)

    def run(*refs):
        body(*refs[:first], *refs[first + count :])

    args = (*args, *after)
    in_specs = in_specs + [pl.BlockSpec(memory_space=pl.ANY)] * count
    return pl.pallas_call(
        run,
        name=name,
        grid_spec=pltpu.PrefetchScalarGridSpec(
            num_scalar_prefetch=scalars, grid=grid, in_specs=in_specs, out_specs=out_specs, scratch_shapes=scratch
        ),
        out_shape=out_shape,
        compiler_params=pltpu.CompilerParams(vmem_limit_bytes=limit, dimension_semantics=("arbitrary",) * len(grid)),
        cost_estimate=pl.CostEstimate(flops=max(flops, 1000), bytes_accessed=1000, transcendentals=0),
    )(*args)


def streamed(x):
    return pltpu.with_memory_space_constraint(x, pltpu.HBM)


def swap(x):
    return lax.ppermute(x, "pair", [(0, 1), (1, 0)])


def local(
    edge_embed, atom_embed, edge_rbf, edge_src, edge_dst, halo_send, trip_index, trip_cos, trip_live,
    quad_index, quad_cos, quad_dih, quad_live, quad_target,
    w_quad_rbf, w_quad_down, w_quad_bil, w_quad_up, w_trip_rbf, w_trip_down, w_trip_bil, w_trip_up,
    w_res_one, w_res_two, w_atom_edge, w_edge_rbf, w_edge_atom, w_out,
    cot_edge, cot_atom, cot_feat,
):
    peers = lax.axis_size("edge")
    role = lax.axis_index("pair")
    role_arg = role.astype(i32).reshape(1)
    place_at = jnp.stack([role, lax.axis_index("edge")]).astype(i32)
    stages = edge_stages()
    plane, line = stages[0], stages[1:]
    codes = stage_codes(stages)
    edges, half_width = edge_embed.shape
    half = edges // 2
    width = 2 * half_width
    atoms, half_atom = atom_embed.shape
    radial_width = edge_rbf.shape[1]
    slots = trip_index.shape[1]
    quad_count, quad_slots = quad_index.shape
    half_quad = quad_count // 2
    halo_count = halo_send.shape[0]
    trip_width = w_trip_down.shape[1]
    quad_width = w_quad_down.shape[1]
    narrow = trip_width + quad_width
    orders = w_trip_bil.shape[0] // trip_width
    atom_width = 2 * half_atom
    tile = half // 2
    grid = (half // tile,)

    def other_rows(x):
        return lax.dynamic_slice_in_dim(x, (1 - role) * half, half, axis=0)

    emb_recv = swap(other_rows(edge_embed))
    cot_recv = swap(other_rows(cot_edge))
    small_own = jnp.concatenate([atom_embed, cot_atom, cot_feat], axis=0)
    small_recv = swap(small_own)
    target = quad_target.reshape(1, quad_count)
    ends = jnp.stack([edge_src, edge_dst])
    halo_out = atom_embed[halo_send].reshape(peers, -1)
    t_index, t_cos, t_live = (streamed(x.T) for x in (trip_index, trip_cos, trip_live))
    q_index, q_cos, q_dih, q_live = (streamed(x.T) for x in (quad_index, quad_cos, quad_dih, quad_live))
    w_down_t, w_down_q, w_bil_t, w_bil_q = (streamed(x.T) for x in (w_trip_down, w_quad_down, w_trip_bil, w_quad_bil))
    w_trip_rbf, w_quad_rbf, w_trip_up, w_quad_up = (streamed(x) for x in (w_trip_rbf, w_quad_rbf, w_trip_up, w_quad_up))
    w_res_one, w_res_two, w_atom_edge, w_edge_rbf, w_edge_atom, w_out = (
        streamed(x) for x in (w_res_one, w_res_two, w_atom_edge, w_edge_rbf, w_edge_atom, w_out)
    )
    edge_mine, cot_mine, rbf_mine = streamed(edge_embed), streamed(cot_edge), streamed(edge_rbf)

    mine = pl.BlockSpec((tile, half_width), lambda i, r: (r[0] * grid[0] + i, 0))
    mine_rbf = pl.BlockSpec((tile, radial_width), lambda i, r: (r[0] * grid[0] + i, 0))
    mine_ends = pl.BlockSpec((2, tile), lambda i, r: (0, r[0] * grid[0] + i))
    mine_slots = pl.BlockSpec((slots, tile), lambda i, r: (0, r[0] * grid[0] + i))
    mine_quad = pl.BlockSpec((quad_slots, half_quad), lambda i, r: (0, r[0]))
    down_scratch = [
        pltpu.VMEM((2, radial_width, 2 * width), bf16), pltpu.VMEM((2, trip_width, width), bf16), pltpu.VMEM((2, quad_width, width), bf16),
    ]
    down_weights = (w_trip_rbf, w_quad_rbf, w_down_t, w_down_q)
    emb, pre, table = call(
        down_kernel, "down", grid,
        [mine, rows_of(tile, half_width), mine_rbf] + [whole(w.shape) for w in down_weights],
        [rows_of(tile, width), columns_of(narrow, tile), columns_of(narrow, tile)],
        [kept(half, width), out(narrow, half), out(narrow, half)], down_scratch,
        (role_arg, edge_mine, emb_recv, rbf_mine, *down_weights), scalars=1, flops=4 * 10**9, limit=32 * 2**20,
    )
    table_recv = swap(table)

    bil_rows = w_bil_q.shape[1]
    z_quad, quad_rows = call(
        functools.partial(quad_forward_kernel, orders=orders, base=trip_width), "quad_forward", (1,),
        [whole(table.shape)] * 2 + [mine_quad] * 4 + [whole(w_bil_q.shape)],
        [whole((bil_rows, half_quad)), whole((quad_width, half_quad))],
        [out(bil_rows, half_quad), out(quad_width, half_quad)],
        [pltpu.VMEM((quad_slots, quad_width, half_quad), f32)] * 2 + [pltpu.VMEM((orders, quad_slots, half_quad), f32)],
        (role_arg, table, table_recv, q_index, q_cos, q_dih, q_live, w_bil_q), scalars=1, flops=2 * 10**9, limit=SMALL_LIMIT,
    )
    cap = quad_count // peers
    cut = quad_width * cap

    def by_peer(x):
        return x.reshape(quad_width, -1, cap).transpose(1, 0, 2).reshape(-1, cut)

    def by_entry(x):
        return x.reshape(-1, quad_width, cap).transpose(1, 0, 2).reshape(quad_width, -1)

    quad_sent = lax.dynamic_update_slice_in_dim(jnp.zeros((peers, cut), f32), by_peer(quad_rows), role * (peers // 2), axis=0)
    routed = exchange(jnp.concatenate([quad_sent, halo_out], axis=1))
    quad_own = by_entry(routed[:, :cut])
    halo_own = routed[:, cut:].reshape(halo_count, half_atom)
    quad_recv = swap(quad_own)
    halo_recv = swap(halo_own)

    bil_rows = w_bil_t.shape[1]
    steps = grid[0] // 2
    table_shape = (2 * CLASSES * trip_width, edges // CLASSES)

    def halves_of(rows):
        return [
            pl.BlockSpec((rows, tile), lambda i, *_: (0, jnp.minimum(i, steps - 1))),
            pl.BlockSpec((rows, tile), lambda i, *_: (0, jnp.maximum(i - steps, 0))),
        ]

    def slots_at(first):
        return [pl.BlockSpec((slots, tile), lambda i, r: (0, r[0] * grid[0] + first + i))] * 3

    def triplet_forward(first, after):
        return call(
            functools.partial(triplet_forward_kernel, orders=orders), f"triplet_forward{first}", (steps,),
            [whole(table.shape)] * 2 + slots_at(first) + [whole(w_bil_t.shape)],
            [columns_of(bil_rows, tile), columns_of(trip_width, tile)],
            [out(bil_rows, half // 2), out(trip_width, half // 2)],
            [
                pltpu.VMEM(table_shape, bf16),
                pltpu.VMEM((2, slots, trip_width, LANES), f32),
                pltpu.VMEM((orders, slots, tile), f32),
                pltpu.VMEM((2, *w_bil_t.shape), bf16),
            ],
            (role_arg, table, table_recv, t_index, t_cos, t_live, w_bil_t), scalars=1, flops=5 * 10**9, after=after,
        )

    z_one, mid_one = triplet_forward(0, [])
    z_two, mid_two = triplet_forward(steps, [quad_own, halo_own, mid_one])

    atom_recv = small_recv[:atoms]
    pool_rows = atoms + halo_count
    square = pltpu.VMEM((2, width, width), bf16)
    up_scratch = pltpu.VMEM((2, narrow, width), bf16)
    rad_scratch = pltpu.VMEM((2, radial_width, width), bf16)
    main_weights = (w_trip_up, w_quad_up, w_res_one, w_res_two, w_atom_edge, w_edge_rbf)
    main_small = (target, quad_own, quad_recv, atom_embed, atom_recv, halo_own, halo_recv)
    mid, joined, pre_one, pre_two, pre_six, new_own, new_send, coll_own = call(
        main_forward_kernel, "main_forward", grid,
        [rows_of(tile, width), *halves_of(trip_width), mine_rbf, mine_ends]
        + [whole(x.shape) for x in main_small + main_weights],
        [columns_of(narrow, tile)] + [rows_of(tile, width)] * 4 + [mine, rows_of(tile, half_width), whole((atoms, width))],
        [out(narrow, half)] + [out(half, width)] * 4 + [kept(edges, half_width), out(half, half_width), out(atoms, width)],
        [up_scratch, square, square, square, rad_scratch, pltpu.VMEM((2, pool_rows + atoms, width), bf16), pltpu.VMEM((2 * quad_width, quad_count), bf16)],
        (role_arg, emb, mid_one, mid_two, rbf_mine, ends, *main_small, *main_weights), scalars=1, flops=8 * 10**9,
    )
    coll_recv = swap(coll_own)
    new_recv = swap(new_send)

    edge_rows = padded_rows(w_atom_edge.shape[0] + radial_width + w_edge_atom.size // width + w_out.size // width)
    atom_args = (coll_own, coll_recv, small_own, small_recv, halo_own, halo_recv, w_atom_edge, w_edge_rbf, w_edge_atom, w_out)
    res_grad, edge_keep, edge_send, pool_grad_own, pool_grad_send, atom_out, feat_out = call(
        functools.partial(edge_backward_kernel, scale=(atoms / edges) ** 0.5, codes=codes), "edge_backward", grid,
        [rows_of(tile, width)] * 3 + [mine_rbf, mine_ends, mine, rows_of(tile, half_width)] + [whole(x.shape) for x in atom_args],
        [rows_of(tile, width), whole((edge_rows // 2, width)), whole((edge_rows // 2, width)),
         whole((pool_rows, half_atom)), whole((pool_rows, half_atom)), whole((atoms, half_atom)), whole((atoms, half_atom))],
        [out(half, width), out(edge_rows // 2, width), out(edge_rows // 2, width),
         out(pool_rows, half_atom), out(pool_rows, half_atom), out(atoms, half_atom), out(atoms, half_atom)],
        [square, rad_scratch, pltpu.VMEM((2, atoms, width), bf16), pltpu.VMEM((pool_rows + atoms, width), f32), pltpu.VMEM((atoms, atom_width), f32),
         pltpu.VMEM((edge_rows, width), f32)],
        (place_at, joined, pre_two, pre_six, rbf_mine, ends, cot_mine, cot_recv, *atom_args), scalars=1, flops=8 * 10**9,
    )
    edge_blocks = phase([("add", [edge_keep, swap(edge_send)], plane[1])], "phase_one")[0]
    edge_parts = middle_stages(send_blocks(edge_blocks, plane), line[:-1], "edge_middle")

    res_rows = padded_rows(2 * width + narrow + w_bil_t.size // width)
    res_weights = (w_trip_up, w_quad_up, w_res_one, w_res_two)
    sum_grad, mid_grad, res_keep, res_send, back_part = call(
        functools.partial(residual_backward_kernel, codes=codes), "residual_backward", grid,
        [rows_of(tile, width)] * 3 + [columns_of(narrow, tile), *halves_of(bil_rows), whole(target.shape), rows_of(tile, width)]
        + [whole(w.shape) for w in res_weights],
        [rows_of(tile, width), columns_of(narrow, tile), whole((res_rows // 2, width)), whole((res_rows // 2, width)), whole((quad_width, quad_count))],
        [kept(half, width), out(narrow, half), out(res_rows // 2, width), out(res_rows // 2, width), out(quad_width, quad_count)],
        [up_scratch, square, square, pltpu.VMEM((res_rows, width), f32), pltpu.VMEM(w_bil_t.shape, f32)],
        (place_at, joined, pre_one, pre_two, mid, z_one, z_two, target, res_grad, *res_weights), scalars=1, flops=8 * 10**9, after=edge_blocks,
    )
    sums_shape = (2 * CLASSES * trip_width, edges // CLASSES)

    def triplet_backward(first, held, after):
        return call(
            functools.partial(triplet_backward_kernel, orders=orders), f"triplet_backward{first}", (steps,),
            [pl.BlockSpec((narrow, tile), lambda i, r: (0, first + i))] + slots_at(first) + [whole(w_bil_t.shape)] + [whole(h.shape) for h in held],
            [whole(sums_shape)],
            [out(*sums_shape)],
            [
                pltpu.VMEM((bil_rows, tile), f32),
                pltpu.VMEM((2, slots, trip_width, LANES), f32),
                pltpu.VMEM((orders, slots, tile), f32),
                pltpu.VMEM((2, *w_bil_t.shape), bf16),
            ],
            (role_arg, mid_grad, t_index, t_cos, t_live, w_bil_t, *held), scalars=1, flops=6 * 10**9, after=after,
        )

    edge_blocks, (res_send,), (back_part,), (pool_grad_send,) = phase(
        [("add", edge_parts, line[-1][1]), ("join", [res_send], 1), ("join", [back_part], 1), ("join", [pool_grad_send], 1)], "phase_two", [sum_grad]
    )
    edge_parts = send_blocks(edge_blocks, line[-1])
    res_recv = swap(res_send)
    held = triplet_backward(0, [], edge_blocks)
    (edge_piece,), res_blocks, (pool_grad,), (back_sum,) = phase(
        [
            ("add", edge_parts, 1),
            ("add", [res_keep, res_recv], plane[1]),
            ("add", [pool_grad_own, swap(pool_grad_send)], 1),
            ("add", [back_part, swap(back_part)], 1),
        ],
        "phase_three", held,
    )
    returned_sent = jnp.concatenate([by_peer(back_sum), pool_grad[atoms:].reshape(peers, -1)], axis=1)
    edge_piece, edge_codes = middle_gathers(edge_piece, line[1:], "edge_middle_gather")
    edge_pieces, edge_lists = spread(edge_piece, edge_codes, line[0])
    res_parts = middle_stages(send_blocks(res_blocks, plane), line[:-1], "res_middle")
    returned = exchange(returned_sent)
    (trip_sums,) = triplet_backward(steps, held, [edge_piece, *res_blocks, returned_sent])
    (edge_piece,), res_blocks = phase([("join", edge_pieces, 1), ("add", res_parts, line[-1][1])], "phase_four", [trip_sums])
    edge_pieces, edge_codes = spread(edge_piece, sum(edge_lists, []), plane)
    res_parts = send_blocks(res_blocks, line[-1])
    back_rows = lax.dynamic_slice_in_dim(returned[:, :cut], role * (peers // 2), peers // 2, axis=0)
    back_own = by_entry(back_rows)
    halo_back = returned[:, cut:].reshape(halo_count, half_atom)
    bil_rows = w_bil_q.shape[1]
    quad_bil, table_keep, table_send = call(
        functools.partial(quad_backward_kernel, orders=orders), "quad_backward", (1,),
        [whole(back_own.shape), whole(z_quad.shape)] + [mine_quad] * 4 + [whole(w_bil_q.shape), whole(trip_sums.shape)],
        [whole(w_bil_q.shape), whole((narrow, half)), whole((narrow, half))],
        [out(*w_bil_q.shape), out(narrow, half), out(narrow, half)],
        [pltpu.VMEM((bil_rows, half_quad), f32), pltpu.VMEM((quad_slots, quad_width, half_quad), f32), pltpu.VMEM((orders, quad_slots, half_quad), f32)],
        (role_arg, back_own, z_quad, q_index, q_cos, q_dih, q_live, w_bil_q, trip_sums), scalars=1, flops=2 * 10**9, limit=SMALL_LIMIT,
        after=[edge_piece, *res_blocks],
    )
    (res_piece,), (table_send,) = phase([("add", res_parts, 1), ("join", [table_send], 1)], "phase_quad", [table_keep])
    table_recv = swap(table_send)
    res_piece, res_codes = middle_gathers(res_piece, line[1:], "res_middle_gather")
    res_pieces, res_lists = spread(res_piece, res_codes, line[0])

    late_rows = padded_rows(2 * radial_width + narrow + w_bil_q.size // width)
    grad_own, grad_send, late_keep, late_send = call(
        functools.partial(final_kernel, codes=[0]), "final", grid,
        [rows_of(tile, width), mine_rbf] + [columns_of(narrow, tile)] * 3 + [rows_of(tile, width)]
        + [whole(x.shape) for x in (quad_bil,) + down_weights],
        [mine, rows_of(tile, half_width)] + [whole((late_rows // 2, width))] * 2,
        [kept(edges, half_width), out(half, half_width)] + [out(late_rows // 2, width)] * 2,
        down_scratch + [pltpu.VMEM((late_rows, width), f32)],
        (place_at * jnp.array([1, 0], i32), emb, rbf_mine, pre, table_keep, table_recv, sum_grad, quad_bil, *down_weights), scalars=1, flops=6 * 10**9,
        after=[res_piece],
    )
    grad_recv = swap(grad_send)
    (res_piece,), (late_send,) = phase([("join", res_pieces, 1), ("join", [late_send], 1)], "phase_five", edge_pieces[1:])
    ((late_half,),) = phase([("add", [late_keep, swap(late_send)], 1)], "phase_late")
    late_blocks = scatter_blocks(late_half)
    res_pieces, res_codes = spread(res_piece, sum(res_lists, []), plane)
    edge_full = lax.dynamic_update_slice_in_dim(new_own, new_recv, (1 - role) * half, axis=0)
    g_atom_edge, g_edge_rbf, g_edge_atom, g_out = unpack(
        edge_pieces, edge_codes, place_at, [w_atom_edge.shape, w_edge_rbf.shape, w_edge_atom.shape, w_out.shape],
        ["plain", "plain", "rows", "rows"], "edge_unpack", [late_half],
    )
    late_piece = fold(late_blocks, "late_fold", res_pieces, [g_out])
    late_all = exchange(jnp.broadcast_to(late_piece[None], late_blocks.shape)).reshape(late_half.shape)
    grad_full = lax.dynamic_update_slice_in_dim(grad_own, grad_recv, (1 - role) * half, axis=0)
    g_two, g_one, g_trip_up, g_quad_up, g_bil_t = unpack(
        res_pieces, res_codes, place_at, [w_res_two.shape, w_res_one.shape, w_trip_up.shape, w_quad_up.shape, w_bil_t.shape],
        ["plain"] * 4 + ["columns"], "res_unpack", [late_piece],
    )
    grad_atom = pool_grad[:atoms] + jnp.zeros((atoms, half_atom), f32).at[halo_send].add(halo_back)
    late_all = phase([("join", [late_all], 1)], "phase_six", [], [g_one, edge_full, grad_full, grad_atom])[0][0]
    g_trip_rbf, g_quad_rbf, g_down_t, g_down_q, g_bil_q = unpack(
        [late_all], [[0]], place_at * jnp.array([1, 0], i32), [w_trip_rbf.shape, w_quad_rbf.shape, w_down_t.shape, w_down_q.shape, w_bil_q.shape],
        ["plain"] * 4 + ["columns"], "late_unpack",
    )
    return (
        edge_full, atom_out, feat_out, grad_full, grad_atom,
        g_quad_rbf, g_down_q.T, g_bil_q.T, g_quad_up, g_trip_rbf, g_down_t.T, g_bil_t.T, g_trip_up,
        g_one, g_two, g_atom_edge, g_edge_rbf, g_edge_atom, g_out,
    )


def solution(mesh):
    whole_spec, rows_spec, both_spec = P(), P("edge"), P("edge", "pair")
    in_specs = (both_spec, both_spec) + (rows_spec,) * 12 + (whole_spec,) * 14 + (both_spec,) * 3
    out_specs = (both_spec,) * 5 + (whole_spec,) * 14
    return jax.shard_map(local, mesh=mesh, in_specs=in_specs, out_specs=out_specs, check_vma=False)
```

```python
import functools

import jax
import jax.numpy as jnp
from jax import lax
from jax.experimental import pallas as pl
from jax.experimental.pallas import tpu as pltpu
from jax.sharding import PartitionSpec as P

f32, bf16, i32 = jnp.float32, jnp.bfloat16, jnp.int32
root_third = 0.5773502691896258
root_half = 0.7071067811865476
LANES = 128
CLASSES = 4
VMEM_LIMIT = 30 * 2**20
SMALL_LIMIT = 24 * 2**20


def split(x):
    high = x.astype(bf16)
    return high, (x - high.astype(f32)).astype(bf16)


def dot(left, right, dims):
    return lax.dot_general(left, right, (dims, ((), ())), preferred_element_type=f32)


NN = ((1,), (0,))
NT = ((1,), (1,))
TN = ((0,), (0,))


def dot3(left, right, dims=NN):
    lh, ll = left if isinstance(left, tuple) else split(left)
    rh, rl = right if isinstance(right, tuple) else split(right)
    at, to = dims[0][0], dims[1][0]
    depth, rows = lh.shape[at], lh.shape[1 - at]
    if (at == 0 or depth % LANES == 0) and (to == 0 or depth % LANES == 0):
        if 3 * depth <= 2 * LANES:
            return dot(jnp.concatenate([lh, lh, ll], axis=at), jnp.concatenate([rh, rl, rh], axis=to), dims)
        if 2 * depth <= 2 * LANES:
            return dot(jnp.concatenate([lh, ll], axis=at), jnp.concatenate([rh, rh], axis=to), dims) + dot(lh, rl, dims)
    if at == 1 and rows <= LANES:
        both = dot(jnp.concatenate([lh, ll], axis=0), rh, dims)
        return both[:rows] + both[rows:] + dot(lh, rl, dims)
    return dot(lh, rh, dims) + dot(lh, rl, dims) + dot(ll, rh, dims)


def pick(onehot, right, dims=NN):
    rh, rl = right if isinstance(right, tuple) else split(right)
    return dot(onehot, rh, dims) + dot(onehot, rl, dims)


def sigmoid(v):
    return 0.5 * jnp.tanh(0.5 * v) + 0.5


def silu(v):
    return v * sigmoid(v)


def silu_grad(v):
    s = sigmoid(v)
    return s * (1.0 + v * (1.0 - s))


def as_bf16(mask):
    return mask.astype(f32).astype(bf16)


def legendre_steps(cosine, orders):
    before, now = jnp.ones_like(cosine), cosine
    yield before
    yield now
    for order in range(1, orders - 1):
        before, now = now, ((2 * order + 1) / (order + 1)) * cosine * now - (order / (order + 1)) * before
        yield now


def class_table(own, other, classes):
    per = classes // 2
    step = own.shape[1] // per
    parts = []
    for block in (own, other):
        high, low = split(block)
        for q in range(per):
            parts += [high[:, q * step : (q + 1) * step], low[:, q * step : (q + 1) * step]]
    return jnp.concatenate(parts, axis=0)


def gather_classes(table, index, classes, width):
    step = table.shape[1]
    shift = step.bit_length() - 1
    slots = index.shape[1]
    onehot = as_bf16(lax.broadcasted_iota(i32, (step, slots), 0) == (index & (step - 1)))
    found = dot(table, onehot, NN)
    kind = index >> shift
    out = found[0:width] + found[width : 2 * width]
    for q in range(1, classes):
        base = q * 2 * width
        out = jnp.where(kind >= q, found[base : base + width] + found[base + width : base + 2 * width], out)
    return out


def scatter_classes(values, indices, classes, step):
    shift = step.bit_length() - 1
    lefts, rights = [], []
    for value, index in zip(values, indices):
        width, slots = value.shape
        high, low = split(value)
        both = jnp.concatenate([high, low], axis=0)
        kind = jnp.broadcast_to(index >> shift, (2 * width, slots))
        lefts.append(jnp.concatenate([jnp.where(kind == q, both, jnp.zeros((), bf16)) for q in range(classes)], axis=0))
        rights.append(as_bf16(lax.broadcasted_iota(i32, (step, slots), 0) == (index & (step - 1))))
    return dot(jnp.concatenate(lefts, axis=1), jnp.concatenate(rights, axis=1), NT)


def unfold_classes(sums, classes, width):
    parts = []
    for q in range(classes):
        base = q * 2 * width
        parts.append(sums[base : base + width] + sums[base + width : base + 2 * width])
    return jnp.concatenate(parts, axis=1)


def joined_halves(zero, mine, theirs, axis=1):
    return jnp.concatenate([jnp.where(zero, mine, theirs), jnp.where(zero, theirs, mine)], axis=axis)


def down_kernel(role, own, recv, rbf, w_trip_rad, w_quad_rad, w_trip, w_quad, emb_out, pre_out, table_out, rad, down_t, down_q):
    width = w_trip_rad.shape[1]

    @pl.when(pl.program_id(0) == 0)
    def _():
        rad[0, :, :width], rad[1, :, :width] = split(w_trip_rad[...])
        rad[0, :, width:], rad[1, :, width:] = split(w_quad_rad[...])
        down_t[0], down_t[1] = split(w_trip[...])
        down_q[0], down_q[1] = split(w_quad[...])

    emb = joined_halves(role[0] == 0, own[...], recv[...])
    emb_out[...] = emb
    radial = dot3(rbf[...], (rad[0], rad[1]))
    pre = jnp.concatenate(
        [
            dot3((down_t[0], down_t[1]), emb * radial[:, :width], NT),
            dot3((down_q[0], down_q[1]), emb * radial[:, width:], NT),
        ],
        axis=0,
    )
    pre_out[...] = pre
    table_out[...] = silu(pre)


def quad_forward_kernel(role, own, other, index, cosine, dihedral, live, w_bil, z_out, rows_out, sel, sel2, basis, *, orders, base):
    slots_k, rows = index.shape
    width = w_bil.shape[0]
    zero = role[0] == 0
    mine, theirs = own[base : base + width, :], other[base : base + width, :]
    table = class_table(jnp.where(zero, mine, theirs), jnp.where(zero, theirs, mine), 2 * CLASSES)
    alive = live[...].astype(f32)
    for order, series in enumerate(legendre_steps(cosine[...], orders)):
        basis[order] = series * alive
    for k in range(slots_k):
        picked = gather_classes(table, index[k : k + 1, :], 2 * CLASSES, width)
        sel[k] = picked
        sel2[k] = picked * dihedral[k : k + 1, :]
    groups = width // 8
    for t in range(rows // LANES):
        at = slice(t * LANES, (t + 1) * LANES)
        for part, source in enumerate((sel, sel2)):
            for order_at in range(0, orders, 8):
                sums = {}
                for k in range(slots_k):
                    chosen = [source[k, g * 8 : g * 8 + 8, at] for g in range(groups)]
                    for order in range(8):
                        weight = jnp.broadcast_to(basis[order_at + order, k : k + 1, at], (8, LANES))
                        for g in range(groups):
                            term = weight * chosen[g]
                            sums[order, g] = term if k == 0 else sums[order, g] + term
                for (order, g), total in sums.items():
                    row = (part * orders + order_at + order) * width + g * 8
                    z_out[row : row + 8, at] = total
    rows_out[...] = dot3(w_bil[...], z_out[...])


def triplet_forward_kernel(role, own, other, index, cosine, live, w_bil, z_out, mid_out, table, sel, basis, bil, *, orders):
    slots_k, tile = index.shape
    width = w_bil.shape[0]

    @pl.when(pl.program_id(0) == 0)
    def _():
        zero = role[0] == 0
        mine, theirs = own[0:width, :], other[0:width, :]
        table[...] = class_table(jnp.where(zero, mine, theirs), jnp.where(zero, theirs, mine), CLASSES)
        bil[0], bil[1] = split(w_bil[...])

    alive = live[...].astype(f32)
    for order, series in enumerate(legendre_steps(cosine[...], orders)):
        basis[order] = series * alive

    def gather(at, k, into):
        where_to = jnp.concatenate([index[k : k + 1, at], index[k + 1 : k + 2, at]], axis=1)
        found = gather_classes(table[...], where_to, CLASSES, width)
        sel[into, k] = found[:, :LANES]
        sel[into, k + 1] = found[:, LANES:]

    def combine(at, first, source):
        sums = {}
        for k in range(slots_k):
            chosen = [sel[source, k, g * 8 : g * 8 + 8, :] for g in (first, first + 1)]
            for order in range(orders):
                weight = jnp.broadcast_to(basis[order, k : k + 1, at], (8, LANES))
                for g in range(2):
                    term = weight * chosen[g]
                    sums[order, g] = term if k == 0 else sums[order, g] + term
        for (order, g), total in sums.items():
            row = order * width + (first + g) * 8
            z_out[row : row + 8, at] = total

    firsts = range(0, width // 8, 2)
    turns = slots_k // 2 // len(firsts)
    columns = lambda c: pl.ds(pl.multiple_of(c * LANES, LANES), LANES)
    for k in range(0, slots_k, 2):
        gather(columns(0), k, 0)

    def step_columns(c, carry):
        for n, first in enumerate(firsts):
            for k in range(n * turns, (n + 1) * turns):
                gather(columns(c), 2 * k, c & 1)
            combine(columns(c - 1), first, 1 - (c & 1))
        return carry

    lax.fori_loop(1, tile // LANES, step_columns, 0)
    for first in firsts:
        combine(columns(tile // LANES - 1), first, (tile // LANES - 1) & 1)
    mid_out[...] = dot3((bil[0], bil[1]), z_out[...])


def laid(pairs):
    return tuple(jnp.concatenate([p[n] for p in pairs], axis=0) for n in range(2))


def row_blocks(tile):
    return [slice(n * tile // 2, (n + 1) * tile // 2) for n in range(2)]


def edge_members(ends, pool_rows, atoms, tile):
    row = lax.broadcasted_iota(i32, (pool_rows + atoms, tile), 0)
    return as_bf16(row == jnp.where(row < pool_rows, ends[0:1, :], ends[1:2, :] + pool_rows))


def entry_members(role, target, step, tile, half):
    row = lax.broadcasted_iota(i32, (tile, target.shape[1]), 0) + (step * tile + role[0] * half)
    return as_bf16(row == target[...])


def main_forward_kernel(
    role, emb, mid_one, mid_two, rbf, ends, target, quad_own, quad_recv, atom_own, atom_recv, halo_own, halo_recv,
    w_trip_up, w_quad_up, w_one, w_two, w_edge, w_rbf,
    mid_out, joined_out, one_out, two_out, six_out, new_own, new_send, collected,
    up, one, two, three, rad, pool_w, quad_hl,
):
    step = pl.program_id(0)
    tile = emb.shape[0]
    half_rows = tile * pl.num_programs(0)
    atoms = atom_own.shape[0]
    pool_rows = atoms + halo_own.shape[0]
    atom_width = 2 * atom_own.shape[1]
    trip_width = w_trip_up.shape[0]
    zero = role[0] == 0

    @pl.when(step == 0)
    def _():
        up[0, :trip_width], up[1, :trip_width] = split(w_trip_up[...])
        up[0, trip_width:], up[1, trip_width:] = split(w_quad_up[...])
        one[0], one[1] = split(w_one[...])
        two[0], two[1] = split(w_two[...])
        three[0], three[1] = split(w_edge[2 * atom_width :, :])
        rad[0], rad[1] = split(w_rbf[...])
        atom_rows = joined_halves(zero, atom_own[...], atom_recv[...])
        pool = jnp.concatenate([atom_rows, joined_halves(zero, halo_own[...], halo_recv[...])], axis=0)
        projected = jnp.concatenate(
            [dot3(pool, w_edge[0:atom_width, :]), dot3(atom_rows, w_edge[atom_width : 2 * atom_width, :])], axis=0
        )
        pool_w[0], pool_w[1] = split(projected)
        high, low = split(quad_own[...] + quad_recv[...])
        quad_hl[...] = jnp.concatenate([high, low], axis=0)

    found = dot(quad_hl[...], entry_members(role, target, step, tile, half_rows), NT)
    width = found.shape[0] // 2
    mid_trip = jnp.where(step < pl.num_programs(0) // 2, mid_one[...], mid_two[...])
    mid = jnp.concatenate([mid_trip, found[:width] + found[width:]], axis=0)
    mid_out[...] = mid
    member = edge_members(ends, pool_rows, atoms, tile)
    blocks = row_blocks(tile)
    joined = [(emb[at, :] + dot3(mid[:, at], (up[0], up[1]), TN)) * root_third for at in blocks]
    pre_one = [dot3(x, (one[0], one[1])) for x in joined]
    pre_two = [dot3(silu(x), (two[0], two[1])) for x in pre_one]
    residual = [(x + silu(y)) * root_half for x, y in zip(joined, pre_two)]
    pre_six = [pick(member[:, at], (pool_w[0], pool_w[1]), TN) + dot3(x, (three[0], three[1])) for at, x in zip(blocks, residual)]
    edge_new = [(x + silu(y)) * root_half for x, y in zip(residual, pre_six)]
    half = emb.shape[1] // 2
    part = 0.0
    for n, at in enumerate(blocks):
        joined_out[at, :] = joined[n]
        one_out[at, :] = pre_one[n]
        two_out[at, :] = pre_two[n]
        six_out[at, :] = pre_six[n]
        new_own[at, :] = jnp.where(zero, edge_new[n][:, :half], edge_new[n][:, half:])
        new_send[at, :] = jnp.where(zero, edge_new[n][:, half:], edge_new[n][:, :half])
        part = part + pick(member[pool_rows:, at], edge_new[n] * dot3(rbf[at, :], (rad[0], rad[1])))

    @pl.when(step == 0)
    def _():
        collected[...] = part

    @pl.when(step > 0)
    def _():
        collected[...] += part


def give_halves(place_at, total, keep, send, codes):
    half = keep.shape[0]
    rows = half // len(codes)
    for side, target in ((place_at[0], keep), (1 - place_at[0], send)):
        for n, code in enumerate(codes):
            at = pl.multiple_of(side * half + (place_at[1] ^ code) * rows, 8)
            target[n * rows : (n + 1) * rows, :] = total[pl.ds(at, rows), :]


def side_by_side(x, width):
    parts = width // x.shape[1]
    rows = x.shape[0] // parts
    return jnp.concatenate([x[q * rows : (q + 1) * rows] for q in range(parts)], axis=1)


def edge_backward_kernel(
    role, joined, pre_two_ref, pre_six_ref, rbf, ends, cot_own, cot_recv,
    coll_own, coll_recv, small_own, small_recv, halo_own, halo_recv,
    w_edge, w_rbf, w_edge_atom, w_out,
    res_grad_out, keep, send, pool_grad_own, pool_grad_send, atom_out, feat_out,
    three, rad, coll_grad, pool_sum, direct, grads,
    *, scale, codes,
):
    step = pl.program_id(0)
    last = pl.num_programs(0) - 1
    tile, edge_width = joined.shape
    half = small_own.shape[1]
    atoms = small_own.shape[0] // 3
    atom_width = 2 * half
    pool_rows = atoms + halo_own.shape[0]
    zero = role[0] == 0
    at_rbf = w_edge.shape[0]
    at_atom = at_rbf + w_rbf.shape[0]
    at_last = at_atom + w_edge_atom.shape[0] * atom_width // edge_width
    at_end = at_last + atom_width * atom_width // edge_width

    @pl.when(step == 0)
    def _():
        three[0], three[1] = split(w_edge[2 * atom_width :, :])
        rad[0], rad[1] = split(w_rbf[...])
        mine, theirs = small_own[...], small_recv[...]
        atom_rows = joined_halves(zero, mine[:atoms], theirs[:atoms])
        cot_atom = joined_halves(zero, mine[atoms : 2 * atoms], theirs[atoms : 2 * atoms])
        cot_feat = joined_halves(zero, mine[2 * atoms :], theirs[2 * atoms :])
        total = (coll_own[...] + coll_recv[...]) * scale
        w_a, w_f = split(w_edge_atom[...]), split(w_out[...])
        pre_atom = dot3(total, w_a)
        atom_new = (atom_rows + silu(pre_atom)) * root_half
        pre_feat = dot3(atom_new, w_f)
        feature = silu(pre_feat)
        atom_out[...] = jnp.where(zero, atom_new[:, :half], atom_new[:, half:])
        feat_out[...] = jnp.where(zero, feature[:, :half], feature[:, half:])
        feat_grad = cot_feat * silu_grad(pre_feat)
        grads[at_last:at_end, :] = side_by_side(0.5 * dot3(atom_new, feat_grad, TN), edge_width)
        atom_grad = (cot_atom + dot3(feat_grad, w_f, NT)) * root_half
        direct[...] = 0.5 * atom_grad
        pre_grad = atom_grad * silu_grad(pre_atom)
        grads[at_atom:at_last, :] = side_by_side(0.5 * dot3(total, pre_grad, TN), edge_width)
        coll_grad[0], coll_grad[1] = split(dot3(pre_grad, w_a, NT) * scale)
        grads[0:at_atom, :] = jnp.zeros((at_atom, grads.shape[1]), f32)
        if grads.shape[0] > at_end:
            grads[at_end:, :] = jnp.zeros((grads.shape[0] - at_end, grads.shape[1]), f32)
        pool_sum[...] = jnp.zeros_like(pool_sum)

    member = edge_members(ends, pool_rows, atoms, tile)
    blocks = row_blocks(tile)
    six = [pre_six_ref[at, :] for at in blocks]
    s_six = [sigmoid(x) for x in six]
    residual = [(joined[at, :] + silu(pre_two_ref[at, :])) * root_half for at in blocks]
    edge_new = [(x + y * s) * root_half for x, y, s in zip(residual, six, s_six)]
    radial = split(rbf[...])
    weighted_grad = [pick(member[pool_rows:, at], (coll_grad[0], coll_grad[1]), TN) for at in blocks]
    new_grad = [
        (joined_halves(zero, cot_own[at, :], cot_recv[at, :]) + w * dot3((radial[0][at], radial[1][at]), (rad[0], rad[1]))) * root_half
        for at, w in zip(blocks, weighted_grad)
    ]
    six_split = [split(g * (s * (1.0 + y * (1.0 - s)))) for g, y, s in zip(new_grad, six, s_six)]
    for at, g, pair in zip(blocks, new_grad, six_split):
        res_grad_out[at, :] = (g + dot3(pair, (three[0], three[1]), NT)) * root_half
    grads[at_rbf:at_atom, :] += dot3(radial, laid([split(w * x) for w, x in zip(weighted_grad, edge_new)]), TN)
    six_all = laid(six_split)
    pool_sum[...] += pick(member, six_all)
    grads[2 * atom_width : at_rbf, :] += dot3(laid([split(x) for x in residual]), six_all, TN)

    @pl.when(step == last)
    def _():
        atom_rows = joined_halves(zero, small_own[:atoms, :], small_recv[:atoms, :])
        pool = jnp.concatenate([atom_rows, joined_halves(zero, halo_own[...], halo_recv[...])], axis=0)
        w_src, w_dst = split(w_edge[0:atom_width, :]), split(w_edge[atom_width : 2 * atom_width, :])
        src_split, dst_split = split(pool_sum[0:pool_rows, :]), split(pool_sum[pool_rows:, :])
        grads[0:atom_width, :] = dot3(pool, src_split, TN)
        grads[atom_width : 2 * atom_width, :] = dot3(atom_rows, dst_split, TN)
        from_src = dot3(src_split, w_src, NT)
        from_atoms = from_src[0:atoms] + dot3(dst_split, w_dst, NT) + direct[...]
        result = jnp.concatenate([from_atoms, from_src[atoms:]], axis=0)
        pool_grad_own[...] = jnp.where(zero, result[:, :half], result[:, half:])
        pool_grad_send[...] = jnp.where(zero, result[:, half:], result[:, :half])
        give_halves(role, grads, keep, send, codes)


def residual_backward_kernel(
    role, joined, pre_one_ref, pre_two_ref, mid_ref, z_one, z_two, target, res_grad_ref,
    w_trip_up, w_quad_up, w_one, w_two,
    sum_grad_out, mid_grad_out, keep, send, back,
    up, one, two, grads, bil_grad,
    *, codes,
):
    step = pl.program_id(0)
    tile, width = joined.shape
    half_rows = tile * pl.num_programs(0)
    trip_width = w_trip_up.shape[0]
    narrow = up.shape[1]
    at_bil = 2 * width + narrow

    @pl.when(step == 0)
    def _():
        up[0, :trip_width], up[1, :trip_width] = split(w_trip_up[...])
        up[0, trip_width:], up[1, trip_width:] = split(w_quad_up[...])
        one[0], one[1] = split(w_one[...])
        two[0], two[1] = split(w_two[...])
        grads[...] = jnp.zeros_like(grads)
        bil_grad[...] = jnp.zeros_like(bil_grad)
        back[...] = jnp.zeros_like(back)

    blocks = row_blocks(tile)

    res_grad = [res_grad_ref[at, :] for at in blocks]
    two_split = [split(grad * silu_grad(pre_two_ref[at, :])) for grad, at in zip(res_grad, blocks)]
    pre_one = [pre_one_ref[at, :] for at in blocks]
    s_one = [sigmoid(pre) for pre in pre_one]
    hidden = [split(pre * s) for pre, s in zip(pre_one, s_one)]
    one_split = [
        split(dot3(grad, (two[0], two[1]), NT) * (s * (1.0 + pre * (1.0 - s)))) for grad, pre, s in zip(two_split, pre_one, s_one)
    ]
    grads[0:width, :] += dot3(laid(hidden), laid(two_split), TN)
    sum_grad = [(grad + dot3(inner, (one[0], one[1]), NT)) * root_third for grad, inner in zip(res_grad, one_split)]
    grads[width : 2 * width, :] += dot3(joined[...], laid(one_split), TN)
    for at, grad in zip(blocks, sum_grad):
        sum_grad_out[at, :] = grad
    sum_split = laid([split(grad) for grad in sum_grad])
    grads[2 * width : at_bil, :] += dot3(mid_ref[...], sum_split, NN)
    mid_grad = dot3((up[0], up[1]), sum_split, NT)
    mid_grad_out[...] = mid_grad
    mid_high, mid_low = split(mid_grad)
    z = jnp.where(step < pl.num_programs(0) // 2, z_one[...], z_two[...])
    bil_grad[...] += dot3((mid_high[:trip_width], mid_low[:trip_width]), z, NT)
    found = dot(jnp.concatenate([mid_high[trip_width:], mid_low[trip_width:]], axis=0), entry_members(role, target, step, tile, half_rows), NN)
    rows = narrow - trip_width
    back[...] += found[:rows] + found[rows:]

    @pl.when(step == pl.num_programs(0) - 1)
    def _():
        for q in range(bil_grad.shape[1] // width):
            grads[at_bil + q * trip_width : at_bil + (q + 1) * trip_width, :] = bil_grad[:, q * width : (q + 1) * width]
        give_halves(role, grads, keep, send, codes)


def triplet_backward_kernel(role, mid_grad, index, cosine, live, w_bil, *refs, orders):
    held, (sums, zg, sg, basis, bil) = refs[:-5], refs[-5:]
    step = pl.program_id(0)
    slots_k, tile = index.shape
    width = w_bil.shape[0]
    classes_step = sums.shape[1]

    @pl.when(step == 0)
    def _():
        bil[0], bil[1] = split(w_bil[...])
        sums[...] = held[0][...] if held else jnp.zeros_like(sums)

    alive = live[...].astype(f32)
    for order, series in enumerate(legendre_steps(cosine[...], orders)):
        basis[order] = series * alive
    grad_split = split(mid_grad[0:width, :])
    zg[...] = dot3((bil[0], bil[1]), grad_split, TN)

    def combine(at, first, into):
        totals = {}
        for order in range(orders):
            row = order * width + first * 8
            got = [zg[row + g * 8 : row + g * 8 + 8, at] for g in range(2)]
            for k in range(slots_k):
                weight = jnp.broadcast_to(basis[order, k : k + 1, at], (8, LANES))
                for g in range(2):
                    term = weight * got[g]
                    totals[k, g] = term if order == 0 else totals[k, g] + term
        for (k, g), total in totals.items():
            sg[into, k, (first + g) * 8 : (first + g) * 8 + 8, :] = total

    def scatter(at, first, source):
        slots_at = range(first, first + slots_k // 2)
        sums[...] += scatter_classes(
            [sg[source, k] for k in slots_at], [index[k : k + 1, at] for k in slots_at], CLASSES, classes_step
        )

    firsts = range(0, width // 8, 2)
    columns = lambda c: pl.ds(pl.multiple_of(c * LANES, LANES), LANES)
    for first in firsts:
        combine(columns(0), first, 0)

    def step_columns(c, carry):
        for n, first in enumerate(firsts):
            if n % 2 == 0:
                scatter(columns(c - 1), n // 2 * (slots_k // 2), 1 - (c & 1))
            combine(columns(c), first, c & 1)
        return carry

    lax.fori_loop(1, tile // LANES, step_columns, 0)
    for n in range(2):
        scatter(columns(tile // LANES - 1), n * (slots_k // 2), (tile // LANES - 1) & 1)


def quad_backward_kernel(role, own, z, index, cosine, dihedral, live, w_bil, trip_sums, bil_grad, keep, send, zg, sg, basis, *, orders):
    slots_k, rows = index.shape
    width = w_bil.shape[0]
    edges = trip_sums.shape[1] * CLASSES
    trip_width = trip_sums.shape[0] // (2 * CLASSES)
    zero = role[0] == 0
    alive = live[...].astype(f32)
    for order, series in enumerate(legendre_steps(cosine[...], orders)):
        basis[order] = series * alive
    grad_split = split(own[...])
    bil_grad[...] = dot3(grad_split, z[...], NT)
    zg[...] = dot3(w_bil[...], grad_split, TN)
    groups = width // 8
    for t in range(rows // LANES):
        at = slice(t * LANES, (t + 1) * LANES)
        for g in range(groups):
            plain, turned = {}, {}
            for order in range(orders):
                one = zg[order * width + g * 8 : order * width + g * 8 + 8, at]
                two = zg[(orders + order) * width + g * 8 : (orders + order) * width + g * 8 + 8, at]
                for k in range(slots_k):
                    weight = jnp.broadcast_to(basis[order, k : k + 1, at], (8, LANES))
                    plain[k] = weight * one if order == 0 else plain[k] + weight * one
                    turned[k] = weight * two if order == 0 else turned[k] + weight * two
            for k in range(slots_k):
                sg[k, g * 8 : g * 8 + 8, at] = plain[k] + turned[k] * jnp.broadcast_to(dihedral[k : k + 1, at], (8, LANES))
    step = edges // (2 * CLASSES)
    sums = scatter_classes([sg[k] for k in range(slots_k)], [index[k : k + 1, :] for k in range(slots_k)], 2 * CLASSES, step)
    total = jnp.concatenate([unfold_classes(trip_sums[...], CLASSES, trip_width), unfold_classes(sums, 2 * CLASSES, width)], axis=0)
    half = edges // 2
    keep[...] = jnp.where(zero, total[:, :half], total[:, half:])
    send[...] = jnp.where(zero, total[:, half:], total[:, :half])


def final_kernel(
    role, emb_ref, rbf, pre_ref, table_own, table_recv, sum_grad, quad_bil, w_trip_rad, w_quad_rad, w_trip, w_quad,
    grad_own, grad_send, keep, send,
    rad, down_t, down_q, total,
    *, codes,
):
    step = pl.program_id(0)
    zero = role[0] == 0
    radial_rows, width = w_trip_rad.shape
    trip_width, quad_width = w_trip.shape[0], w_quad.shape[0]
    at_quad_rad = radial_rows
    at_trip = 2 * radial_rows
    at_quad = at_trip + trip_width
    at_quad_bil = at_quad + quad_width
    at_end = at_quad_bil + quad_width * quad_bil.shape[1] // width

    @pl.when(step == 0)
    def _():
        rad[0, :, :width], rad[1, :, :width] = split(w_trip_rad[...])
        rad[0, :, width:], rad[1, :, width:] = split(w_quad_rad[...])
        down_t[0], down_t[1] = split(w_trip[...])
        down_q[0], down_q[1] = split(w_quad[...])
        total[...] = jnp.zeros_like(total)
        rows = quad_bil.shape[0]
        for q in range(quad_bil.shape[1] // width):
            total[at_quad_bil + q * rows : at_quad_bil + (q + 1) * rows, :] = quad_bil[:, q * width : (q + 1) * width]

    emb = emb_ref[...]
    radial_split = split(rbf[...])
    radial = dot3(radial_split, (rad[0], rad[1]))
    pre_grad = (table_own[...] + table_recv[...]) * silu_grad(pre_ref[...])
    trip_split, quad_split = split(pre_grad[:trip_width]), split(pre_grad[trip_width:])
    trip_radial, quad_radial = radial[:, :width], radial[:, width:]
    total[at_trip:at_quad, :] += dot3(trip_split, emb * trip_radial)
    total[at_quad:at_quad_bil, :] += dot3(quad_split, emb * quad_radial)
    trip_mixed = dot3(trip_split, (down_t[0], down_t[1]), TN)
    quad_mixed = dot3(quad_split, (down_q[0], down_q[1]), TN)
    grad = sum_grad[...] + trip_mixed * trip_radial + quad_mixed * quad_radial
    half = width // 2
    grad_own[...] = jnp.where(zero, grad[:, :half], grad[:, half:])
    grad_send[...] = jnp.where(zero, grad[:, half:], grad[:, :half])
    total[0:at_quad_rad, :] += dot3(radial_split, trip_mixed * emb, TN)
    total[at_quad_rad:at_trip, :] += dot3(radial_split, quad_mixed * emb, TN)

    @pl.when(step == pl.num_programs(0) - 1)
    def _():
        give_halves(role, total, keep, send, codes)


def fold_kernel(source, target):
    target[...] = jnp.sum(source[...], axis=0)


def fold(blocks, name, after=(), whole_after=()):
    return call(fold_kernel, name, (1,), [whole(blocks.shape)], [whole(blocks.shape[1:])], [out(*blocks.shape[1:])], [], (blocks,), after=after, whole_after=whole_after, limit=SMALL_LIMIT)[0]


def exchange(blocks):
    return lax.all_to_all(blocks, "edge", split_axis=0, concat_axis=0, tiled=True)


def scatter_blocks(rows):
    return exchange(rows.reshape(lax.axis_size("edge"), -1, rows.shape[1]))


def partners(bits, axis="edge"):
    return [(i, i ^ bits) for i in range(lax.axis_size(axis))]


def edge_stages():
    size, shift, stages = lax.axis_size("edge"), 0, []
    while size > 1:
        radix = 8 if size == 8 else 4 if size % 4 == 0 else 2
        stages.append((shift, radix))
        shift += radix.bit_length() - 1
        size //= radix
    return stages


def padded_rows(rows):
    unit = 2 * 8 * lax.axis_size("edge")
    return -(-rows // unit) * unit


def spread(piece, codes, stage):
    shift, radix = stage
    pieces = [piece] + [lax.ppermute(piece, "edge", partners(j << shift)) for j in range(1, radix)]
    return pieces, [[c ^ (j << shift) for c in codes] for j in range(radix)]


def stage_codes(stages):
    codes = [0]
    for shift, radix in reversed(stages):
        codes = [c ^ (j << shift) for j in range(radix) for c in codes]
    return codes


def phase_kernel(*refs, jobs):
    ins, outs = list(refs[: sum(count for _, count, _ in jobs)]), list(refs[sum(count for _, count, _ in jobs) :])
    for kind, count, blocks in jobs:
        parts, ins = ins[:count], ins[count:]
        targets, outs = outs[:blocks], outs[blocks:]
        if kind == "join":
            rows = parts[0].shape[0]
            for n, part in enumerate(parts):
                targets[0][n * rows : (n + 1) * rows, :] = part[...]
        else:
            rows = parts[0].shape[0] // blocks
            for n, target in enumerate(targets):
                total = parts[0][n * rows : (n + 1) * rows, :]
                for part in parts[1:]:
                    total = total + part[n * rows : (n + 1) * rows, :]
                target[...] = total


def phase(jobs, name, after=(), whole_after=()):
    ins, shapes = [], []
    for kind, parts, blocks in jobs:
        rows, width = parts[0].shape
        ins += parts
        shapes += [(len(parts) * rows, width)] if kind == "join" else [(rows // blocks, width)] * blocks
    got = call(
        functools.partial(phase_kernel, jobs=[(kind, len(parts), blocks) for kind, parts, blocks in jobs]), name, (1,),
        [whole(x.shape) for x in ins], [whole(x) for x in shapes], [out(*x) for x in shapes], [], tuple(ins), after=after, whole_after=whole_after, limit=SMALL_LIMIT,
    )
    results = []
    for _, _, blocks in jobs:
        results.append(got[:blocks])
        got = got[blocks:]
    return results


def send_blocks(blocks, stage):
    shift, radix = stage
    return [blocks[0]] + [lax.ppermute(blocks[j], "edge", partners(j << shift)) for j in range(1, radix)]


def middle_stages(parts, stages, name):
    for at, stage in enumerate(stages):
        parts = send_blocks(phase([("add", parts, stage[1])], f"{name}{at}")[0], stage)
    return parts


def middle_gathers(piece, stages, name):
    codes = [0]
    for at, stage in enumerate(reversed(stages)):
        pieces, lists = spread(piece, codes, stage)
        piece, codes = phase([("join", pieces, 1)], f"{name}{at}")[0][0], sum(lists, [])
    return piece, codes


def unpack_kernel(place_at, *refs, count, codes, layout):
    ins, outs, total = refs[:count], refs[count:-1], refs[-1]
    half = total.shape[0] // 2
    for n, source in enumerate(ins):
        side, listed = codes[n]
        first = jnp.where(place_at[0] == 0, side, 1 - side) * half
        rows = source.shape[0] // len(listed)
        for at, code in enumerate(listed):
            block = place_at[1] ^ code
            total[pl.ds(pl.multiple_of(first + block * rows, 8), rows), :] = source[at * rows : (at + 1) * rows, :]
    at = 0
    for target, kind in zip(outs, layout):
        height, breadth = target.shape
        width = total.shape[1]
        if kind == "plain":
            target[...] = total[at : at + height, :]
            at += height
        elif kind == "rows":
            parts = width // breadth
            rows = height // parts
            for q in range(parts):
                target[q * rows : (q + 1) * rows, :] = total[at : at + rows, q * breadth : (q + 1) * breadth]
            at += rows
        else:
            for q in range(breadth // width):
                target[:, q * width : (q + 1) * width] = total[at : at + height, :]
                at += height


def unpack(pieces, codes, place_at, shapes, layout, name, after=()):
    count = 2 * len(pieces)
    pieces = pieces + [swap(p) for p in pieces]
    codes = [(0, c) for c in codes] + [(1, c) for c in codes]
    rows = sum(p.shape[0] for p in pieces)
    return call(
        functools.partial(unpack_kernel, count=count, codes=codes, layout=layout), name, (1,), [whole(p.shape) for p in pieces],
        [whole(s) for s in shapes], [out(*s) for s in shapes], [pltpu.VMEM((rows, pieces[0].shape[1]), f32)], (place_at, *pieces), scalars=1, whole_after=after, limit=SMALL_LIMIT,
    )


def whole(shape):
    return pl.BlockSpec(shape, lambda *_: (0,) * len(shape))


def rows_of(tile, width):
    return pl.BlockSpec((tile, width), lambda i, *_: (i, 0))


def columns_of(rows, tile):
    return pl.BlockSpec((rows, tile), lambda i, *_: (0, i))


def out(*shape):
    return jax.ShapeDtypeStruct(shape, f32)


def kept(*shape):
    return pltpu.HBM(shape, f32)


def tip(x):
    x = x.reshape(-1, x.shape[-1])
    return x[: min(8, x.shape[0]), : min(LANES, x.shape[1])]


def call(body, name, grid, in_specs, out_specs, out_shape, scratch, args, scalars=0, flops=0, after=(), whole_after=(), limit=VMEM_LIMIT):
    after = [tip(x) for x in after] + list(whole_after)
    first, count = len(args), len(after)

    def run(*refs):
        body(*refs[:first], *refs[first + count :])

    args = (*args, *after)
    in_specs = in_specs + [pl.BlockSpec(memory_space=pl.ANY)] * count
    return pl.pallas_call(
        run,
        name=name,
        grid_spec=pltpu.PrefetchScalarGridSpec(
            num_scalar_prefetch=scalars, grid=grid, in_specs=in_specs, out_specs=out_specs, scratch_shapes=scratch
        ),
        out_shape=out_shape,
        compiler_params=pltpu.CompilerParams(vmem_limit_bytes=limit, dimension_semantics=("arbitrary",) * len(grid)),
        cost_estimate=pl.CostEstimate(flops=max(flops, 1000), bytes_accessed=1000, transcendentals=0),
    )(*args)


def streamed(x):
    return pltpu.with_memory_space_constraint(x, pltpu.HBM)


def swap(x):
    return lax.ppermute(x, "pair", [(0, 1), (1, 0)])


def local(
    edge_embed, atom_embed, edge_rbf, edge_src, edge_dst, halo_send, trip_index, trip_cos, trip_live,
    quad_index, quad_cos, quad_dih, quad_live, quad_target,
    w_quad_rbf, w_quad_down, w_quad_bil, w_quad_up, w_trip_rbf, w_trip_down, w_trip_bil, w_trip_up,
    w_res_one, w_res_two, w_atom_edge, w_edge_rbf, w_edge_atom, w_out,
    cot_edge, cot_atom, cot_feat,
):
    peers = lax.axis_size("edge")
    role = lax.axis_index("pair")
    role_arg = role.astype(i32).reshape(1)
    place_at = jnp.stack([role, lax.axis_index("edge")]).astype(i32)
    stages = edge_stages()
    plane, line = stages[0], stages[1:]
    codes = stage_codes(stages)
    edges, half_width = edge_embed.shape
    half = edges // 2
    width = 2 * half_width
    atoms, half_atom = atom_embed.shape
    radial_width = edge_rbf.shape[1]
    slots = trip_index.shape[1]
    quad_count, quad_slots = quad_index.shape
    half_quad = quad_count // 2
    halo_count = halo_send.shape[0]
    trip_width = w_trip_down.shape[1]
    quad_width = w_quad_down.shape[1]
    narrow = trip_width + quad_width
    orders = w_trip_bil.shape[0] // trip_width
    atom_width = 2 * half_atom
    tile = half // 2
    grid = (half // tile,)

    def other_rows(x):
        return lax.dynamic_slice_in_dim(x, (1 - role) * half, half, axis=0)

    emb_recv = swap(other_rows(edge_embed))
    cot_recv = swap(other_rows(cot_edge))
    small_own = jnp.concatenate([atom_embed, cot_atom, cot_feat], axis=0)
    small_recv = swap(small_own)
    target = quad_target.reshape(1, quad_count)
    ends = jnp.stack([edge_src, edge_dst])
    halo_out = atom_embed[halo_send].reshape(peers, -1)
    t_index, t_cos, t_live = (streamed(x.T) for x in (trip_index, trip_cos, trip_live))
    q_index, q_cos, q_dih, q_live = (streamed(x.T) for x in (quad_index, quad_cos, quad_dih, quad_live))
    w_down_t, w_down_q, w_bil_t, w_bil_q = (streamed(x.T) for x in (w_trip_down, w_quad_down, w_trip_bil, w_quad_bil))
    w_trip_rbf, w_quad_rbf, w_trip_up, w_quad_up = (streamed(x) for x in (w_trip_rbf, w_quad_rbf, w_trip_up, w_quad_up))
    w_res_one, w_res_two, w_atom_edge, w_edge_rbf, w_edge_atom, w_out = (
        streamed(x) for x in (w_res_one, w_res_two, w_atom_edge, w_edge_rbf, w_edge_atom, w_out)
    )
    edge_mine, cot_mine, rbf_mine = streamed(edge_embed), streamed(cot_edge), streamed(edge_rbf)

    mine = pl.BlockSpec((tile, half_width), lambda i, r: (r[0] * grid[0] + i, 0))
    mine_rbf = pl.BlockSpec((tile, radial_width), lambda i, r: (r[0] * grid[0] + i, 0))
    mine_ends = pl.BlockSpec((2, tile), lambda i, r: (0, r[0] * grid[0] + i))
    mine_slots = pl.BlockSpec((slots, tile), lambda i, r: (0, r[0] * grid[0] + i))
    mine_quad = pl.BlockSpec((quad_slots, half_quad), lambda i, r: (0, r[0]))
    down_scratch = [
        pltpu.VMEM((2, radial_width, 2 * width), bf16), pltpu.VMEM((2, trip_width, width), bf16), pltpu.VMEM((2, quad_width, width), bf16),
    ]
    down_weights = (w_trip_rbf, w_quad_rbf, w_down_t, w_down_q)
    emb, pre, table = call(
        down_kernel, "down", grid,
        [mine, rows_of(tile, half_width), mine_rbf] + [whole(w.shape) for w in down_weights],
        [rows_of(tile, width), columns_of(narrow, tile), columns_of(narrow, tile)],
        [kept(half, width), out(narrow, half), out(narrow, half)], down_scratch,
        (role_arg, edge_mine, emb_recv, rbf_mine, *down_weights), scalars=1, flops=4 * 10**9, limit=32 * 2**20,
    )
    table_recv = swap(table)

    bil_rows = w_bil_q.shape[1]
    z_quad, quad_rows = call(
        functools.partial(quad_forward_kernel, orders=orders, base=trip_width), "quad_forward", (1,),
        [whole(table.shape)] * 2 + [mine_quad] * 4 + [whole(w_bil_q.shape)],
        [whole((bil_rows, half_quad)), whole((quad_width, half_quad))],
        [out(bil_rows, half_quad), out(quad_width, half_quad)],
        [pltpu.VMEM((quad_slots, quad_width, half_quad), f32)] * 2 + [pltpu.VMEM((orders, quad_slots, half_quad), f32)],
        (role_arg, table, table_recv, q_index, q_cos, q_dih, q_live, w_bil_q), scalars=1, flops=2 * 10**9, limit=SMALL_LIMIT,
    )
    cap = quad_count // peers
    cut = quad_width * cap

    def by_peer(x):
        return x.reshape(quad_width, -1, cap).transpose(1, 0, 2).reshape(-1, cut)

    def by_entry(x):
        return x.reshape(-1, quad_width, cap).transpose(1, 0, 2).reshape(quad_width, -1)

    quad_sent = lax.dynamic_update_slice_in_dim(jnp.zeros((peers, cut), f32), by_peer(quad_rows), role * (peers // 2), axis=0)
    routed = exchange(jnp.concatenate([quad_sent, halo_out], axis=1))
    quad_own = by_entry(routed[:, :cut])
    halo_own = routed[:, cut:].reshape(halo_count, half_atom)
    quad_recv = swap(quad_own)
    halo_recv = swap(halo_own)

    bil_rows = w_bil_t.shape[1]
    steps = grid[0] // 2
    table_shape = (2 * CLASSES * trip_width, edges // CLASSES)

    def halves_of(rows):
        return [
            pl.BlockSpec((rows, tile), lambda i, *_: (0, jnp.minimum(i, steps - 1))),
            pl.BlockSpec((rows, tile), lambda i, *_: (0, jnp.maximum(i - steps, 0))),
        ]

    def slots_at(first):
        return [pl.BlockSpec((slots, tile), lambda i, r: (0, r[0] * grid[0] + first + i))] * 3

    def triplet_forward(first, after):
        return call(
            functools.partial(triplet_forward_kernel, orders=orders), f"triplet_forward{first}", (steps,),
            [whole(table.shape)] * 2 + slots_at(first) + [whole(w_bil_t.shape)],
            [columns_of(bil_rows, tile), columns_of(trip_width, tile)],
            [out(bil_rows, half // 2), out(trip_width, half // 2)],
            [
                pltpu.VMEM(table_shape, bf16),
                pltpu.VMEM((2, slots, trip_width, LANES), f32),
                pltpu.VMEM((orders, slots, tile), f32),
                pltpu.VMEM((2, *w_bil_t.shape), bf16),
            ],
            (role_arg, table, table_recv, t_index, t_cos, t_live, w_bil_t), scalars=1, flops=5 * 10**9, after=after,
        )

    z_one, mid_one = triplet_forward(0, [])
    z_two, mid_two = triplet_forward(steps, [quad_own, halo_own, mid_one])

    atom_recv = small_recv[:atoms]
    pool_rows = atoms + halo_count
    square = pltpu.VMEM((2, width, width), bf16)
    up_scratch = pltpu.VMEM((2, narrow, width), bf16)
    rad_scratch = pltpu.VMEM((2, radial_width, width), bf16)
    main_weights = (w_trip_up, w_quad_up, w_res_one, w_res_two, w_atom_edge, w_edge_rbf)
    main_small = (target, quad_own, quad_recv, atom_embed, atom_recv, halo_own, halo_recv)
    mid, joined, pre_one, pre_two, pre_six, new_own, new_send, coll_own = call(
        main_forward_kernel, "main_forward", grid,
        [rows_of(tile, width), *halves_of(trip_width), mine_rbf, mine_ends]
        + [whole(x.shape) for x in main_small + main_weights],
        [columns_of(narrow, tile)] + [rows_of(tile, width)] * 4 + [mine, rows_of(tile, half_width), whole((atoms, width))],
        [out(narrow, half)] + [out(half, width)] * 4 + [kept(edges, half_width), out(half, half_width), out(atoms, width)],
        [up_scratch, square, square, square, rad_scratch, pltpu.VMEM((2, pool_rows + atoms, width), bf16), pltpu.VMEM((2 * quad_width, quad_count), bf16)],
        (role_arg, emb, mid_one, mid_two, rbf_mine, ends, *main_small, *main_weights), scalars=1, flops=8 * 10**9,
    )
    coll_recv = swap(coll_own)
    new_recv = swap(new_send)

    edge_rows = padded_rows(w_atom_edge.shape[0] + radial_width + w_edge_atom.size // width + w_out.size // width)
    atom_args = (coll_own, coll_recv, small_own, small_recv, halo_own, halo_recv, w_atom_edge, w_edge_rbf, w_edge_atom, w_out)
    res_grad, edge_keep, edge_send, pool_grad_own, pool_grad_send, atom_out, feat_out = call(
        functools.partial(edge_backward_kernel, scale=(atoms / edges) ** 0.5, codes=codes), "edge_backward", grid,
        [rows_of(tile, width)] * 3 + [mine_rbf, mine_ends, mine, rows_of(tile, half_width)] + [whole(x.shape) for x in atom_args],
        [rows_of(tile, width), whole((edge_rows // 2, width)), whole((edge_rows // 2, width)),
         whole((pool_rows, half_atom)), whole((pool_rows, half_atom)), whole((atoms, half_atom)), whole((atoms, half_atom))],
        [out(half, width), out(edge_rows // 2, width), out(edge_rows // 2, width),
         out(pool_rows, half_atom), out(pool_rows, half_atom), out(atoms, half_atom), out(atoms, half_atom)],
        [square, rad_scratch, pltpu.VMEM((2, atoms, width), bf16), pltpu.VMEM((pool_rows + atoms, width), f32), pltpu.VMEM((atoms, atom_width), f32),
         pltpu.VMEM((edge_rows, width), f32)],
        (place_at, joined, pre_two, pre_six, rbf_mine, ends, cot_mine, cot_recv, *atom_args), scalars=1, flops=8 * 10**9,
    )
    edge_blocks = phase([("add", [edge_keep, swap(edge_send)], plane[1])], "phase_one")[0]
    edge_parts = middle_stages(send_blocks(edge_blocks, plane), line[:-1], "edge_middle")

    res_rows = padded_rows(2 * width + narrow + w_bil_t.size // width)
    res_weights = (w_trip_up, w_quad_up, w_res_one, w_res_two)
    sum_grad, mid_grad, res_keep, res_send, back_part = call(
        functools.partial(residual_backward_kernel, codes=codes), "residual_backward", grid,
        [rows_of(tile, width)] * 3 + [columns_of(narrow, tile), *halves_of(bil_rows), whole(target.shape), rows_of(tile, width)]
        + [whole(w.shape) for w in res_weights],
        [rows_of(tile, width), columns_of(narrow, tile), whole((res_rows // 2, width)), whole((res_rows // 2, width)), whole((quad_width, quad_count))],
        [kept(half, width), out(narrow, half), out(res_rows // 2, width), out(res_rows // 2, width), out(quad_width, quad_count)],
        [up_scratch, square, square, pltpu.VMEM((res_rows, width), f32), pltpu.VMEM(w_bil_t.shape, f32)],
        (place_at, joined, pre_one, pre_two, mid, z_one, z_two, target, res_grad, *res_weights), scalars=1, flops=8 * 10**9, after=edge_blocks,
    )
    sums_shape = (2 * CLASSES * trip_width, edges // CLASSES)

    def triplet_backward(first, held, after):
        return call(
            functools.partial(triplet_backward_kernel, orders=orders), f"triplet_backward{first}", (steps,),
            [pl.BlockSpec((narrow, tile), lambda i, r: (0, first + i))] + slots_at(first) + [whole(w_bil_t.shape)] + [whole(h.shape) for h in held],
            [whole(sums_shape)],
            [out(*sums_shape)],
            [
                pltpu.VMEM((bil_rows, tile), f32),
                pltpu.VMEM((2, slots, trip_width, LANES), f32),
                pltpu.VMEM((orders, slots, tile), f32),
                pltpu.VMEM((2, *w_bil_t.shape), bf16),
            ],
            (role_arg, mid_grad, t_index, t_cos, t_live, w_bil_t, *held), scalars=1, flops=6 * 10**9, after=after,
        )

    edge_blocks, (res_send,), (back_part,), (pool_grad_send,) = phase(
        [("add", edge_parts, line[-1][1]), ("join", [res_send], 1), ("join", [back_part], 1), ("join", [pool_grad_send], 1)], "phase_two", [sum_grad]
    )
    edge_parts = send_blocks(edge_blocks, line[-1])
    res_recv = swap(res_send)
    held = triplet_backward(0, [], edge_blocks)
    (edge_piece,), res_blocks, (pool_grad,), (back_sum,) = phase(
        [
            ("add", edge_parts, 1),
            ("add", [res_keep, res_recv], plane[1]),
            ("add", [pool_grad_own, swap(pool_grad_send)], 1),
            ("add", [back_part, swap(back_part)], 1),
        ],
        "phase_three", held,
    )
    returned_sent = jnp.concatenate([by_peer(back_sum), pool_grad[atoms:].reshape(peers, -1)], axis=1)
    edge_piece, edge_codes = middle_gathers(edge_piece, line[1:], "edge_middle_gather")
    edge_pieces, edge_lists = spread(edge_piece, edge_codes, line[0])
    res_parts = middle_stages(send_blocks(res_blocks, plane), line[:-1], "res_middle")
    returned = exchange(returned_sent)
    (trip_sums,) = triplet_backward(steps, held, [edge_piece, *res_blocks, returned_sent])
    (edge_piece,), res_blocks = phase([("join", edge_pieces, 1), ("add", res_parts, line[-1][1])], "phase_four", [trip_sums])
    edge_pieces, edge_codes = spread(edge_piece, sum(edge_lists, []), plane)
    res_parts = send_blocks(res_blocks, line[-1])
    back_rows = lax.dynamic_slice_in_dim(returned[:, :cut], role * (peers // 2), peers // 2, axis=0)
    back_own = by_entry(back_rows)
    halo_back = returned[:, cut:].reshape(halo_count, half_atom)
    bil_rows = w_bil_q.shape[1]
    quad_bil, table_keep, table_send = call(
        functools.partial(quad_backward_kernel, orders=orders), "quad_backward", (1,),
        [whole(back_own.shape), whole(z_quad.shape)] + [mine_quad] * 4 + [whole(w_bil_q.shape), whole(trip_sums.shape)],
        [whole(w_bil_q.shape), whole((narrow, half)), whole((narrow, half))],
        [out(*w_bil_q.shape), out(narrow, half), out(narrow, half)],
        [pltpu.VMEM((bil_rows, half_quad), f32), pltpu.VMEM((quad_slots, quad_width, half_quad), f32), pltpu.VMEM((orders, quad_slots, half_quad), f32)],
        (role_arg, back_own, z_quad, q_index, q_cos, q_dih, q_live, w_bil_q, trip_sums), scalars=1, flops=2 * 10**9, limit=SMALL_LIMIT,
        after=[edge_piece, *res_blocks],
    )
    (res_piece,), (table_send,) = phase([("add", res_parts, 1), ("join", [table_send], 1)], "phase_quad", [table_keep])
    table_recv = swap(table_send)
    res_piece, res_codes = middle_gathers(res_piece, line[1:], "res_middle_gather")
    res_pieces, res_lists = spread(res_piece, res_codes, line[0])

    late_rows = padded_rows(2 * radial_width + narrow + w_bil_q.size // width)
    grad_own, grad_send, late_keep, late_send = call(
        functools.partial(final_kernel, codes=[0]), "final", grid,
        [rows_of(tile, width), mine_rbf] + [columns_of(narrow, tile)] * 3 + [rows_of(tile, width)]
        + [whole(x.shape) for x in (quad_bil,) + down_weights],
        [mine, rows_of(tile, half_width)] + [whole((late_rows // 2, width))] * 2,
        [kept(edges, half_width), out(half, half_width)] + [out(late_rows // 2, width)] * 2,
        down_scratch + [pltpu.VMEM((late_rows, width), f32)],
        (place_at * jnp.array([1, 0], i32), emb, rbf_mine, pre, table_keep, table_recv, sum_grad, quad_bil, *down_weights), scalars=1, flops=6 * 10**9,
        after=[res_piece],
    )
    grad_recv = swap(grad_send)
    (res_piece,), (late_send,) = phase([("join", res_pieces, 1), ("join", [late_send], 1)], "phase_five", edge_pieces[1:])
    ((late_half,),) = phase([("add", [late_keep, swap(late_send)], 1)], "phase_late")
    late_blocks = scatter_blocks(late_half)
    res_pieces, res_codes = spread(res_piece, sum(res_lists, []), plane)
    edge_full = lax.dynamic_update_slice_in_dim(new_own, new_recv, (1 - role) * half, axis=0)
    g_atom_edge, g_edge_rbf, g_edge_atom, g_out = unpack(
        edge_pieces, edge_codes, place_at, [w_atom_edge.shape, w_edge_rbf.shape, w_edge_atom.shape, w_out.shape],
        ["plain", "plain", "rows", "rows"], "edge_unpack", [late_half],
    )
    late_piece = fold(late_blocks, "late_fold", res_pieces, [g_out])
    late_all = exchange(jnp.broadcast_to(late_piece[None], late_blocks.shape)).reshape(late_half.shape)
    grad_full = lax.dynamic_update_slice_in_dim(grad_own, grad_recv, (1 - role) * half, axis=0)
    g_two, g_one, g_trip_up, g_quad_up, g_bil_t = unpack(
        res_pieces, res_codes, place_at, [w_res_two.shape, w_res_one.shape, w_trip_up.shape, w_quad_up.shape, w_bil_t.shape],
        ["plain"] * 4 + ["columns"], "res_unpack", [late_piece],
    )
    grad_atom = pool_grad[:atoms] + jnp.zeros((atoms, half_atom), f32).at[halo_send].add(halo_back)
    late_all = phase([("join", [late_all], 1)], "phase_six", [g_one], [edge_full, grad_full, grad_atom])[0][0]
    g_trip_rbf, g_quad_rbf, g_down_t, g_down_q, g_bil_q = unpack(
        [late_all], [[0]], place_at * jnp.array([1, 0], i32), [w_trip_rbf.shape, w_quad_rbf.shape, w_down_t.shape, w_down_q.shape, w_bil_q.shape],
        ["plain"] * 4 + ["columns"], "late_unpack",
    )
    return (
        edge_full, atom_out, feat_out, grad_full, grad_atom,
        g_quad_rbf, g_down_q.T, g_bil_q.T, g_quad_up, g_trip_rbf, g_down_t.T, g_bil_t.T, g_trip_up,
        g_one, g_two, g_atom_edge, g_edge_rbf, g_edge_atom, g_out,
    )


def solution(mesh):
    whole_spec, rows_spec, both_spec = P(), P("edge"), P("edge", "pair")
    in_specs = (both_spec, both_spec) + (rows_spec,) * 12 + (whole_spec,) * 14 + (both_spec,) * 3
    out_specs = (both_spec,) * 5 + (whole_spec,) * 14
    return jax.shard_map(local, mesh=mesh, in_specs=in_specs, out_specs=out_specs, check_vma=False)
```
